256 devices in a mesh: grp: 8 (over y, core), dev: 32 (over x, z).
Axes of the slice: x: 4, y: 4, z: 8, core: 2. Of those that a mesh axis runs over, the one named last changes fastest.
Arguments:
- sample_field: float32 [2, 4096, 4096], P(None, 'grp', 'dev'), may hold values from -4 to 4
- probe_modes: float32 [2, 2, 256, 256], replicated, may hold values from -4 to 4
- amplitudes: float32 [1024, 256, 256], P(('grp', 'dev')), may hold values from 0.2 to 2.5
- rows_at: int32 [1024], P(('grp', 'dev')), may hold values from 0 to 3840, as said below
- cols_at: int32 [1024], P(('grp', 'dev')), may hold values from 0 to 3840, as said below
- live_counts: int32 [256], P(('grp', 'dev')), may hold values from 1 to 4, 512 in all
Outputs:
- new_sample: float32 [2, 4096, 4096], P(None, 'grp', 'dev')
- new_probe: float32 [2, 2, 256, 256], replicated
- probe_gradient: float32 [2, 2, 256, 256], replicated
The draws below stay inside these ranges and needn't reach their ends.
Inputs may be any that keep to these rules, and one draw needn't show every extreme that they name: `rows_at`: a position held by the device at index g of grp starts at a row from g * 512 - 128 to g * 512 + 384, kept within the object. `cols_at`: a position held by the device at index d of dev starts at a column from d * 128 - 128 to d * 128, kept within the object. `live_counts`: slots at or past a device's count are unused.
All inputs are finite; a program needn't handle non-finite values.
Results may differ from the reference program's by a relative error of at most 0.006.
Values sent between devices are 32-bit elements; how exact they have to be, the bound alone decides.
A program may use at most 64 MiB of HBM per device.

```python
import math
import jax
import jax.numpy as jnp
import numpy as np
from jax import lax

PATCH = 256
MODES = 2
ITERS = 2
OR_DEV = 512
POS_CAP = 4
TILE = 128
OBJ_R = 4096
OBJ_C = 4096
POSITIONS = 1024
N_DEV = 32
DEVICES = 256


def draw_rows_at(key, part):
    key = jax.random.fold_in(key, 11)
    position_ids = jnp.arange(POSITIONS, dtype=jnp.int32)
    region = position_ids // POS_CAP // N_DEV
    offset = jax.random.randint(key, (POSITIONS,), 0, OR_DEV + 1, dtype=jnp.int32)
    return jnp.clip(region * OR_DEV - TILE + offset, 0, OBJ_R - PATCH).astype(jnp.int32)


def draw_cols_at(key, part):
    key = jax.random.fold_in(key, 23)
    position_ids = jnp.arange(POSITIONS, dtype=jnp.int32)
    column = position_ids // POS_CAP % N_DEV
    offset = jax.random.randint(key, (POSITIONS,), 0, TILE + 1, dtype=jnp.int32)
    return jnp.clip(column * TILE - TILE + offset, 0, OBJ_C - PATCH).astype(jnp.int32)


def block_scale(stream_key, extent, cuts, least, high):
    factor_of, own = 1.0, jax.random.fold_in(stream_key, 6)
    for dim, blocks in cuts:
        draws = jnp.exp(jax.random.uniform(jax.random.fold_in(own, dim), (blocks,), jnp.float32, least / len(cuts), high / len(cuts)))
        factor_of = factor_of * jnp.repeat(draws, extent[dim] // blocks).reshape([-1 if axis == dim else 1 for axis in range(len(extent))])
    return factor_of


def split_up(amount, total, bound, skew):
    weights = [(1 << 20) // math.isqrt(rank ** skew) + 1 for rank in range(2, amount + 1)]
    rest, counts = total - bound - (amount - 1), [1] * (amount - 1)
    while rest > 0:
        movable = [i for i in range(amount - 1) if counts[i] < bound]
        mass, budget = sum([weights[i] for i in movable]), rest
        for i in movable:
            more = min(bound - counts[i], max(1, budget * weights[i] // mass), rest)
            counts[i] = counts[i] + more
            rest = rest - more
    return np.array([bound] + counts)


def uneven(own_key, amount, total, bound, slope):
    if amount == 2:
        one = jax.random.randint(own_key, (), max(1, total - bound), min(bound, total - 1) + 1)
        return jnp.stack([one, total - one])
    lengths = jnp.asarray(split_up(amount, total, bound, slope), jnp.int32)
    couples = (amount - 1) // 2
    donor, sink = lengths[1:1 + 2 * couples:2], lengths[2:2 + 2 * couples:2]
    slack = jnp.minimum(donor - 1, bound - sink)
    moved = jax.random.randint(jax.random.fold_in(own_key, 1), (couples,), 0, 1 << 20) % (slack + 1)
    lengths = lengths.at[1:1 + 2 * couples:2].set(donor - moved).at[2:2 + 2 * couples:2].set(sink + moved)
    return lengths[jax.random.permutation(jax.random.fold_in(own_key, 2), amount)]


def centred(rng, extent, scale, reach, pieces=(), held_as=jnp.bfloat16):
    gain = block_scale(rng, extent, pieces, -0.22, 0.18) if pieces else 1.0
    entries = jax.random.normal(rng, extent, jnp.float32) * scale * gain
    return jnp.minimum(jnp.maximum(entries, -reach), reach).astype(held_as)


def setup_inputs(seed: int = 0) -> dict:
    arg_keys = jax.random.split(jax.random.key(seed), 7)
    sample_field = centred(arg_keys[0], (2, OBJ_R, OBJ_C), 0.7, 4.0, ((1, 8), (2, 32)), jnp.float32)
    probe_modes = centred(arg_keys[1], (MODES, 2, PATCH, PATCH), 0.7, 4.0, (), jnp.float32)
    amplitudes = jnp.clip(0.2 + 2.3 * jax.random.uniform(arg_keys[2], (POSITIONS, PATCH, PATCH), jnp.float32) ** block_scale(arg_keys[2], (POSITIONS, PATCH, PATCH), ((0, 256),), -0.2, 0.2), 0.2, 2.5)
    rows_at = draw_rows_at(jax.random.fold_in(arg_keys[6], 71), 0)
    cols_at = draw_cols_at(jax.random.fold_in(arg_keys[6], 71), 0)
    live_counts = uneven(arg_keys[5], DEVICES, DEVICES * POS_CAP // 2, POS_CAP, 2).astype(jnp.int32)
    return dict(sample_field=sample_field, probe_modes=probe_modes, amplitudes=amplitudes, rows_at=rows_at, cols_at=cols_at, live_counts=live_counts)


INTENSITY_FLOOR = 0.25
SAMPLE_DAMPING = 0.5
PROBE_DAMPING = 1.0

def dft_tables(pixels):
    indices = jnp.arange(pixels, dtype=jnp.int32)
    phases = indices[:, None] * indices[None, :] % pixels
    angles = phases.astype(jnp.float32) * (2.0 * math.pi / pixels)
    scaling = 1.0 / math.sqrt(pixels)
    return jnp.stack([jnp.cos(angles) * scaling, jnp.sin(angles) * scaling]).astype(jnp.bfloat16)

def combine(products, sign_factor):
    real_part = products[0][:, 0] + sign_factor * products[1][:, 1]
    imag_part = products[0][:, 1] - sign_factor * products[1][:, 0]
    return jnp.stack([real_part, imag_part], axis=1)

def transform(values, tables, sign_factor):
    first = jnp.einsum('tab,mcbk->tmcak', tables.astype(jnp.float32), values.astype(jnp.float32))
    rows_done = combine(first, sign_factor).astype(jnp.bfloat16)
    second = jnp.einsum('mcaj,tjk->tmcak', rows_done.astype(jnp.float32), tables.astype(jnp.float32))
    return combine(second, sign_factor)

def position_terms(patch_field, probe_modes, amplitude, tables):
    sample_re = patch_field[0]
    sample_im = patch_field[1]
    probe_re = probe_modes[:, 0]
    probe_im = probe_modes[:, 1]
    wave_re = probe_re * sample_re - probe_im * sample_im
    wave_im = probe_re * sample_im + probe_im * sample_re
    exit_wave = jnp.stack([wave_re, wave_im], axis=1).astype(jnp.bfloat16)
    spectrum = transform(exit_wave, tables, 1.0)
    intensity = lax.optimization_barrier(jnp.sum(spectrum[:, 0] ** 2 + spectrum[:, 1] ** 2, axis=0))
    factor = amplitude / jnp.sqrt(jnp.maximum(intensity, INTENSITY_FLOOR)) - 1.0
    corrected = (spectrum * factor).astype(jnp.bfloat16)
    chi_field = transform(corrected, tables, -1.0)
    back_re = chi_field[:, 0]
    back_im = chi_field[:, 1]
    grad_re = lax.optimization_barrier(jnp.sum(probe_re * back_re + probe_im * back_im, axis=0))
    grad_im = lax.optimization_barrier(jnp.sum(probe_re * back_im - probe_im * back_re, axis=0))
    lighting = lax.optimization_barrier(jnp.sum(probe_re ** 2 + probe_im ** 2, axis=0))
    sample_term = jnp.stack([grad_re, grad_im, lighting])
    probe_re_term = sample_re * back_re + sample_im * back_im
    probe_im_term = sample_re * back_im - sample_im * back_re
    probe_term = jnp.stack([probe_re_term, probe_im_term], axis=1)
    return (sample_term, probe_term, sample_re ** 2 + sample_im ** 2)

def reference(sample_field, probe_modes, amplitudes, rows_at, cols_at, live_counts):
    tables = dft_tables(PATCH)
    position_ids = jnp.arange(POSITIONS, dtype=jnp.int32)
    active = position_ids % POS_CAP < live_counts[position_ids // POS_CAP]
    probe_grad = jnp.zeros((MODES, 2, PATCH, PATCH), jnp.float32)
    for iteration in range(ITERS):
        current = sample_field
        current_probe = probe_modes

        def visit_one(carry, position):
            row_start, col_start, amplitude, active_flag = position

            def accumulate(state):
                totals, probe_sum, probe_weight = state
                anchor = (jnp.int32(0), row_start, col_start)
                patch_field = lax.dynamic_slice(current, anchor, (2, PATCH, PATCH))
                sample_term, probe_term, weight_term = position_terms(patch_field, current_probe, amplitude, tables)
                previous = lax.dynamic_slice(totals, anchor, (3, PATCH, PATCH))
                totals = lax.dynamic_update_slice(totals, previous + sample_term, anchor)
                return (totals, probe_sum + probe_term, probe_weight + weight_term)
            return (lax.cond(active_flag, accumulate, lambda state: state, carry), None)
        initial = (jnp.zeros((3, OBJ_R, OBJ_C), jnp.float32), jnp.zeros((MODES, 2, PATCH, PATCH), jnp.float32), jnp.zeros((PATCH, PATCH), jnp.float32))
        (totals, probe_grad, probe_weight), _ = lax.scan(visit_one, initial, (rows_at, cols_at, amplitudes, active))
        sample_field = current + totals[:2] / (totals[2] + SAMPLE_DAMPING)
        probe_modes = current_probe + probe_grad / (probe_weight + PROBE_DAMPING)
    return (sample_field, probe_modes, probe_grad * (1.0 / math.sqrt(POSITIONS)))
```

```python
import functools
import math

import jax
import jax.numpy as jnp
import ml_dtypes
import numpy as np
from jax import lax
from jax.experimental import pallas as pl
from jax.experimental.pallas import tpu as pltpu
from jax.sharding import PartitionSpec as P

INTENSITY_FLOOR = 0.25
SAMPLE_DAMPING = 0.5
PROBE_DAMPING = 1.0
MESH = pl.DeviceIdType.MESH
LANES = 128
N = 256
BAND = 512
EXT = BAND + 2 * LANES
FAR = 512
STEP = 16
COPIES = 112
UP, MIDDLE, DOWN = (0, 128), (128, 384), (384, 512)


def tables():
    k = np.arange(N)
    angles = (np.outer(k, k) % N).astype(np.float32) * np.float32(2.0 * math.pi / N)
    c = (np.cos(angles) / np.float32(16.0)).astype(ml_dtypes.bfloat16)
    s = (np.sin(angles) / np.float32(16.0)).astype(ml_dtypes.bfloat16)
    a = np.block([[c, s], [-s, c]])
    return a, np.ascontiguousarray(a.T)


def kernel(
    shape, sample, probe, amps, table_a, table_b, rows_at, cols_at, live,
    new_sample, new_probe, probe_gradient,
    field0, field1, probe0, probe1, amp, ta, tb, patch, wave, mid, spec, placed,
    up0, up1, dn0, dn1, own0, own1, fu0, fu1, fd0, fd1, fl0, fl1, fr0, fr1,
    part0, part1, rc0, rc1, hs0, hs1, rx0, rx1, hx0, hx1, ry0, ry1, zb0, zb1, rz0, rz1, zg0, zg1, full0, full1,
    load_sem, send_sem, recv_sem,
):
    nx, ny, nz = shape
    blocks = 2 * nx * ny
    depth = N // blocks
    zn = -(-10 // nz)
    field, prb = (field0, field1), (probe0, probe1)
    halo_up, halo_dn, own = (up0, up1), (dn0, dn1), (own0, own1)
    from_up, from_dn, from_left, from_right = (fu0, fu1), (fd0, fd1), (fl0, fl1), (fr0, fr1)
    part, rc, hs, rx, hx, ry = (part0, part1), (rc0, rc1), (hs0, hs1), (rx0, rx1), (hx0, hx1), (ry0, ry1)
    zb, rz, zg, full = (zb0, zb1), (rz0, rz1), (zg0, zg1), (full0, full1)

    g, d = lax.axis_index("grp"), lax.axis_index("dev")
    ng, nd = 2 * ny, nx * nz
    y, core = g // 2, g % 2
    x, z = d // nz, d % nz
    above = {"grp": (g + ng - 1) % ng, "dev": d}
    below = {"grp": (g + 1) % ng, "dev": d}
    left = {"grp": g, "dev": (d + nd - 1) % nd}
    right = {"grp": g, "dev": (d + 1) % nd}
    partner = {"grp": y * 2 + 1 - core, "dev": d}

    def along_x(k):
        xx = (x + k) % nx
        return xx, {"grp": g, "dev": xx * nz + z}

    def along_y(k):
        yy = (y + k) % ny
        return yy, {"grp": yy * 2 + core, "dev": d}

    def along_z(k):
        zz = (z + k) % nz
        return zz, {"grp": g, "dev": x * nz + zz}

    copies = []

    def send(src, dst, to):
        n = len(copies)
        copy = pltpu.make_async_remote_copy(
            src_ref=src, dst_ref=dst, send_sem=send_sem.at[n], recv_sem=recv_sem.at[n],
            device_id=to, device_id_type=MESH,
        )
        copy.start()
        copies.append(copy)
        return copy

    loads = [
        pltpu.make_async_copy(src, dst, load_sem.at[n])
        for n, (src, dst) in enumerate(
            (
                (sample, field0.at[1, :, LANES : LANES + BAND, :]),
                (probe, probe0),
                (table_a, ta),
                (table_b, tb),
                (amps, amp),
            )
        )
    ]
    for load in loads:
        load.start()

    barrier = pltpu.get_barrier_semaphore()
    peers = [above, below, left, right, partner]
    peers += [along_x(k)[1] for k in range(1, nx)]
    peers += [along_y(k)[1] for k in range(1, ny)]
    peers += [along_z(k)[1] for k in range(1, nz)]
    for peer in peers:
        pl.semaphore_signal(barrier, inc=1, device_id=peer, device_id_type=MESH)
    pl.semaphore_wait(barrier, len(peers))

    row_anchor = g * BAND - LANES
    col_anchor = d * LANES - LANES
    slots = 4
    starts = [jnp.clip(rows_at[p] - row_anchor, 0, FAR) for p in range(slots)]

    def send_columns(f, source, lo, hi):
        src = source(lo, hi)
        return (
            send(src, f.at[0, :, LANES + lo : LANES + hi, :], right),
            send(src, f.at[2, :, LANES + lo : LANES + hi, :], left),
        )

    def forward_up(f, t, src=None):
        src = f.at[t, :, LANES : 2 * LANES, :] if src is None else src
        return send(src, f.at[t, :, LANES + BAND : EXT, :], above)

    def forward_down(f, t, src=None):
        src = f.at[t, :, BAND : LANES + BAND, :] if src is None else src
        return send(src, f.at[t, :, 0:LANES, :], below)

    def spread(f, sent_up, sent_down, sent_middle, forwards):
        for copy in sent_up:
            copy.wait_recv()
        forwards += [forward_up(f, 0), forward_up(f, 2)]
        for copy in sent_down:
            copy.wait_recv()
        forwards += [forward_down(f, 0), forward_down(f, 2)]
        return list(sent_middle) + forwards

    def argument(lo, hi):
        return sample.at[:, lo:hi, :]

    sent_up = send_columns(field0, argument, *UP)
    sent_down = send_columns(field0, argument, *DOWN)
    forwards = [forward_up(field0, 1, argument(*UP)), forward_down(field0, 1, argument(*DOWN))]
    sent_middle = send_columns(field0, argument, *MIDDLE)

    def clear(i, _):
        zero = jnp.zeros((STEP, LANES), jnp.float32)
        rr = pl.multiple_of(i * STEP, STEP)
        for p in range(slots):
            for t in range(3):
                for ch in range(3):
                    placed[p, t, ch, pl.ds(rr, STEP), :] = zero
                    placed[p, t, ch, pl.ds(FAR + N + rr, STEP), :] = zero
        return 0

    lax.fori_loop(0, FAR // STEP, clear, 0)
    for it in range(2):
        part[it][...] = jnp.zeros(part[it].shape, jnp.float32)
        zb[it][...] = jnp.zeros(zb[it].shape, jnp.float32)

    waiting = spread(field0, sent_up, sent_down, sent_middle, forwards)
    for copy in waiting:
        copy.wait_recv()
    for load in loads:
        load.wait()

    def part_at(i8):
        if depth == 8:
            return i8, pl.ds(0, 8)
        per = depth // 8
        return i8 // per, pl.ds(pl.multiple_of(i8 % per * 8, 8), 8)

    def add_part(it, k, i, value):
        for e in range(STEP // 8):
            b, rows = part_at(i * (STEP // 8) + e)
            part[it][b, k, rows, :] += value[e * 8 : e * 8 + 8, :]

    def position(it, p):
        f, pr = field[it], prb[it]
        r0 = jnp.clip(rows_at[p] - row_anchor, 0, FAR)
        s = jnp.clip(cols_at[p] - col_anchor, 0, LANES)
        back = (LANES - s) % LANES
        ahead = s % LANES
        alive = jnp.full((STEP, LANES), p, jnp.int32) < jnp.full((STEP, LANES), live[0], jnp.int32)
        lane = lax.broadcasted_iota(jnp.int32, (STEP, LANES), 1)
        early = lane < LANES - s
        late = lane >= s

        def gather(i, _):
            rr = pl.multiple_of(i * STEP, STEP)
            rows = pl.ds(rr, STEP)
            halves = []
            for ch in range(2):
                a, b, c = (pltpu.roll(f[t, ch, pl.ds(r0 + rr, STEP), :], back, 1) for t in range(3))
                halves.append((jnp.where(early, a, b), jnp.where(early, b, c)))
            for j in range(2):
                o_re, o_im = halves[0][j], halves[1][j]
                patch[0, j, rows, :] = o_re
                patch[1, j, rows, :] = o_im
                add_part(it, 8 + j, i, jnp.where(alive, o_re * o_re + o_im * o_im, 0.0))
                for m in range(2):
                    cols = slice(m * N + j * LANES, m * N + (j + 1) * LANES)
                    p_re = pr[2 * m, rows, j * LANES : (j + 1) * LANES]
                    p_im = pr[2 * m + 1, rows, j * LANES : (j + 1) * LANES]
                    wave[rows, cols] = (p_re * o_re - p_im * o_im).astype(jnp.bfloat16)
                    wave[pl.ds(N + rr, STEP), cols] = (p_re * o_im + p_im * o_re).astype(jnp.bfloat16)
            return 0

        def columns_first(table):
            for m in range(2):
                for c in range(2):
                    mid[m * N : (m + 1) * N, c * N : (c + 1) * N] = jnp.dot(
                        table[c * N : (c + 1) * N, :],
                        wave[:, m * N : (m + 1) * N],
                        preferred_element_type=jnp.float32,
                    ).astype(jnp.bfloat16)

        def rows_next(table):
            for m in range(2):
                spec[m * N : (m + 1) * N, :] = jnp.dot(
                    mid[m * N : (m + 1) * N, :], table[...], preferred_element_type=jnp.float32
                )

        def correct(i, _):
            rr = pl.multiple_of(i * STEP, STEP)
            for j in range(2):
                values = [
                    [
                        spec[pl.ds(m * N + rr, STEP), c * N + j * LANES : c * N + (j + 1) * LANES]
                        for c in range(2)
                    ]
                    for m in range(2)
                ]
                intensity = (values[0][0] ** 2 + values[0][1] ** 2) + (
                    values[1][0] ** 2 + values[1][1] ** 2
                )
                measured = amp[p, pl.ds(rr, STEP), j * LANES : (j + 1) * LANES]
                factor = measured * lax.rsqrt(jnp.maximum(intensity, INTENSITY_FLOOR)) - 1.0
                for m in range(2):
                    for c in range(2):
                        wave[
                            pl.ds(c * N + rr, STEP), m * N + j * LANES : m * N + (j + 1) * LANES
                        ] = (values[m][c] * factor).astype(jnp.bfloat16)
            return 0

        def scatter(i, _):
            rr = pl.multiple_of(i * STEP, STEP)
            rows = pl.ds(rr, STEP)
            terms = []
            for j in range(2):
                o_re, o_im = patch[0, j, rows, :], patch[1, j, rows, :]
                g_re = g_im = light = jnp.zeros((STEP, LANES), jnp.float32)
                for m in range(2):
                    p_re = pr[2 * m, rows, j * LANES : (j + 1) * LANES]
                    p_im = pr[2 * m + 1, rows, j * LANES : (j + 1) * LANES]
                    b_re = spec[pl.ds(m * N + rr, STEP), j * LANES : (j + 1) * LANES]
                    b_im = spec[pl.ds(m * N + rr, STEP), N + j * LANES : N + (j + 1) * LANES]
                    g_re += p_re * b_re + p_im * b_im
                    g_im += p_re * b_im - p_im * b_re
                    light += p_re * p_re + p_im * p_im
                    h_re = o_re * b_re + o_im * b_im
                    h_im = o_re * b_im - o_im * b_re
                    add_part(it, 4 * m + j, i, jnp.where(alive, h_re, 0.0))
                    add_part(it, 4 * m + 2 + j, i, jnp.where(alive, h_im, 0.0))
                terms.append([jnp.where(alive, v, 0.0) for v in (g_re, g_im, light)])
            at = pl.ds(FAR + rr, STEP)
            for ch in range(3):
                a = pltpu.roll(terms[0][ch], ahead, 1)
                b = pltpu.roll(terms[1][ch], ahead, 1)
                placed[p, 0, ch, at, :] = jnp.where(late, a, 0.0)
                placed[p, 1, ch, at, :] = jnp.where(late, b, a)
                placed[p, 2, ch, at, :] = jnp.where(late, 0.0, b)
            return 0

        lax.fori_loop(0, N // STEP, gather, 0)
        columns_first(ta)
        rows_next(tb)
        lax.fori_loop(0, N // STEP, correct, 0)
        columns_first(tb)
        rows_next(ta)
        lax.fori_loop(0, N // STEP, scatter, 0)

    def total(dst, first, lo, hi):
        def body(i, _):
            rr = pl.multiple_of(lo + i * STEP, STEP)
            for t in range(3):
                for ch in range(3):
                    values = [
                        placed[p, t, ch, pl.ds(FAR + first + rr - starts[p], STEP), :] for p in range(slots)
                    ]
                    dst[t, ch, pl.ds(rr, STEP), :] = (values[0] + values[1]) + (values[2] + values[3])
            return 0

        lax.fori_loop(0, (hi - lo) // STEP, body, 0)

    def update(it, lo, hi):
        def body(i, _):
            rr = pl.multiple_of(lo + i * STEP, STEP)
            rows = pl.ds(rr, STEP)
            sums = [
                own[it][1, ch, rows, :] + (from_left[it][ch, rows, :] + from_right[it][ch, rows, :])
                for ch in range(3)
            ]
            scale = 1.0 / (sums[2] + SAMPLE_DAMPING)
            for ch in range(2):
                value = field[it][1, ch, pl.ds(LANES + rr, STEP), :] + sums[ch] * scale
                if it == 0:
                    field1[1, ch, pl.ds(LANES + rr, STEP), :] = value
                else:
                    new_sample[ch, rows, :] = value
            return 0

        lax.fori_loop(0, (hi - lo) // STEP, body, 0)

    def finish_probe(it):
        def body(i8, _):
            b, rows = part_at(i8)
            at = pl.ds(pl.multiple_of(i8 * 8, 8), 8)
            for j in range(2):
                cols = slice(j * LANES, (j + 1) * LANES)
                scale = 1.0 / (full[it][b, 8 + j, rows, :] + PROBE_DAMPING)
                for q in range(4):
                    grad = full[it][b, 2 * q + j, rows, :]
                    value = prb[it][q, at, cols] + grad * scale
                    if it == 0:
                        probe1[q, at, cols] = value
                    else:
                        new_probe[q, at, cols] = value
                        probe_gradient[q, at, cols] = grad * (1.0 / math.sqrt(slots * ng * nd))
            return 0

        lax.fori_loop(0, N // 8, body, 0)

    for it in range(2):
        lax.fori_loop(0, slots, lambda p, _: (position(it, p), 0)[1], 0)

        half = blocks // 2
        swap = send(part[it].at[pl.ds((1 - core) * half, half)], rc[it], partner)

        total(halo_up[it], 0, 0, LANES)
        rows_up = send(halo_up[it], from_dn[it], above)
        total(halo_dn[it], LANES + BAND, 0, LANES)
        rows_down = send(halo_dn[it], from_up[it], below)

        swap.wait_recv()

        def sum_core(i, _):
            hs[it][i] = part[it][core * half + i] + rc[it][i]
            return 0

        lax.fori_loop(0, half, sum_core, 0)
        to_x = []
        for k in range(1, nx):
            xx, peer = along_x(k)
            to_x.append(send(hs[it].at[pl.ds(xx * ny, ny)], rx[it].at[k - 1], peer))

        def send_sides(lo, hi):
            return (
                send(own[it].at[0, :, lo:hi, :], from_right[it].at[:, lo:hi, :], left),
                send(own[it].at[2, :, lo:hi, :], from_left[it].at[:, lo:hi, :], right),
            )

        total(own[it], LANES, *MIDDLE)
        side_middle = send_sides(*MIDDLE)
        total(own[it], LANES, *UP)
        total(own[it], LANES, *DOWN)

        def add_rows(src, lo):
            def body(i, _):
                rr = pl.multiple_of(i * STEP, STEP)
                for t in range(3):
                    for ch in range(3):
                        own[it][t, ch, pl.ds(lo + rr, STEP), :] += src[t, ch, pl.ds(rr, STEP), :]
                return 0

            lax.fori_loop(0, LANES // STEP, body, 0)

        rows_down.wait_recv()
        add_rows(from_up[it], UP[0])
        side_up = send_sides(*UP)
        rows_up.wait_recv()
        add_rows(from_dn[it], DOWN[0])
        side_down = send_sides(*DOWN)

        for copy in to_x:
            copy.wait_recv()
        for i in range(ny):
            value = hs[it][x * ny + i]
            for k in range(nx - 1):
                value += rx[it][k, i]
            hx[it][i] = value
        to_y = []
        for k in range(1, ny):
            yy, peer = along_y(k)
            to_y.append(send(hx[it].at[yy], ry[it].at[k - 1], peer))

        for copy in side_middle:
            copy.wait_recv()
        update(it, *MIDDLE)

        for copy in to_y:
            copy.wait_recv()
        value = hx[it][y]
        for k in range(ny - 1):
            value += ry[it][k]
        zb[it][0:10] = value
        to_z = []
        for k in range(1, nz):
            zz, peer = along_z(k)
            to_z.append(send(zb[it].at[pl.ds(zz * zn, zn)], rz[it].at[k - 1], peer))

        for copy in side_up:
            copy.wait_recv()
        update(it, *UP)
        if it == 0:

            def updated(lo, hi):
                return field1.at[1, :, LANES + lo : LANES + hi, :]

            sent_up = send_columns(field1, updated, *UP)
            forwards = [forward_up(field1, 1)]
        for copy in side_down:
            copy.wait_recv()
        update(it, *DOWN)
        if it == 0:
            sent_down = send_columns(field1, updated, *DOWN)
            forwards.append(forward_down(field1, 1))
            sent_middle = send_columns(field1, updated, *MIDDLE)

        for copy in to_z:
            copy.wait_recv()
        value = zb[it][pl.ds(z * zn, zn)]
        for k in range(nz - 1):
            value += rz[it][k]
        zg[it][pl.ds(z * zn, zn)] = value
        mine = zg[it].at[pl.ds(z * zn, zn)]
        back_z = [send(mine, mine, along_z(k)[1]) for k in range(1, nz)]
        for copy in back_z:
            copy.wait_recv()
        at = (core * nx + x) * ny + y
        full[it][at] = zg[it][0:10]
        mine = full[it].at[at]
        back_y = [send(mine, mine, along_y(k)[1]) for k in range(1, ny)]
        for copy in back_y:
            copy.wait_recv()
        mine = full[it].at[pl.ds((core * nx + x) * ny, ny)]
        back_x = [send(mine, mine, along_x(k)[1]) for k in range(1, nx)]
        if it == 0:
            waiting = spread(field1, sent_up, sent_down, sent_middle, forwards)
        for copy in back_x:
            copy.wait_recv()
        mine = full[it].at[pl.ds(core * half, half)]
        back_core = send(mine, mine, partner)
        back_core.wait_recv()
        finish_probe(it)
        if it == 0:
            for copy in waiting:
                copy.wait_recv()

    for copy in copies:
        copy.wait_send()


def solution(mesh):
    ng, nd = mesh.shape["grp"], mesh.shape["dev"]
    ny = ng // 2
    nx = 4 if nd == 32 else 2
    nz = nd // nx
    blocks = 2 * nx * ny
    depth = N // blocks
    zn = -(-10 // nz)
    table_a, table_b = tables()

    def two(shape, dtype=jnp.float32):
        return [pltpu.VMEM(shape, dtype)] * 2

    def local(sample, probe, amps, rows_at, cols_at, live):
        hbm = pl.BlockSpec(memory_space=pl.ANY)
        vmem = pl.BlockSpec(memory_space=pltpu.VMEM)
        smem = pl.BlockSpec(memory_space=pltpu.SMEM)
        new_sample, new_probe, probe_gradient = pl.pallas_call(
            functools.partial(kernel, (nx, ny, nz)),
            out_shape=[
                jax.ShapeDtypeStruct((2, BAND, LANES), jnp.float32),
                jax.ShapeDtypeStruct((4, N, N), jnp.float32),
                jax.ShapeDtypeStruct((4, N, N), jnp.float32),
            ],
            in_specs=[hbm] * 5 + [smem] * 3,
            out_specs=[vmem] * 3,
            scratch_shapes=[
                *two((3, 2, EXT, LANES)),
                *two((4, N, N)),
                pltpu.VMEM((4, N, N), jnp.float32),
                *two((2 * N, 2 * N), jnp.bfloat16),
                pltpu.VMEM((2, 2, N, LANES), jnp.float32),
                *two((2 * N, 2 * N), jnp.bfloat16),
                pltpu.VMEM((2 * N, 2 * N), jnp.float32),
                pltpu.VMEM((4, 3, 3, 2 * FAR + N, LANES), jnp.float32),
                *two((3, 3, LANES, LANES)),
                *two((3, 3, LANES, LANES)),
                *two((3, 3, BAND, LANES)),
                *two((3, 3, LANES, LANES)),
                *two((3, 3, LANES, LANES)),
                *two((3, BAND, LANES)),
                *two((3, BAND, LANES)),
                *two((blocks, 10, depth, LANES)),
                *two((blocks // 2, 10, depth, LANES)),
                *two((blocks // 2, 10, depth, LANES)),
                *two((nx - 1, ny, 10, depth, LANES)),
                *two((ny, 10, depth, LANES)),
                *two((ny - 1, 10, depth, LANES)),
                *two((zn * nz, depth, LANES)),
                *two((nz - 1, zn, depth, LANES)),
                *two((zn * nz, depth, LANES)),
                *two((blocks, 10, depth, LANES)),
                pltpu.SemaphoreType.DMA((5,)),
                pltpu.SemaphoreType.DMA((COPIES,)),
                pltpu.SemaphoreType.DMA((COPIES,)),
            ],
            compiler_params=pltpu.CompilerParams(
                collective_id=0, has_side_effects=True, vmem_limit_bytes=60 * 1024 * 1024
            ),
            cost_estimate=pl.CostEstimate(
                flops=2 * 4 * 4 * 2 * 512**3, bytes_accessed=6 << 20, transcendentals=8 * N * N
            ),
        )(sample, probe.reshape(4, N, N), amps, table_a, table_b, rows_at, cols_at, live)
        return new_sample, new_probe.reshape(2, 2, N, N), probe_gradient.reshape(2, 2, N, N)

    return jax.shard_map(
        local,
        mesh=mesh,
        in_specs=(
            P(None, "grp", "dev"),
            P(),
            P(("grp", "dev"), None, None),
            P(("grp", "dev")),
            P(("grp", "dev")),
            P(("grp", "dev")),
        ),
        out_specs=(P(None, "grp", "dev"), P(), P()),
        check_vma=False,
    )
```

```python
import functools
import math

import jax
import jax.numpy as jnp
import ml_dtypes
import numpy as np
from jax import lax
from jax.experimental import pallas as pl
from jax.experimental.pallas import tpu as pltpu
from jax.sharding import PartitionSpec as P

INTENSITY_FLOOR = 0.25
SAMPLE_DAMPING = 0.5
PROBE_DAMPING = 1.0
MESH = pl.DeviceIdType.MESH
LANES = 128
N = 256
HALF = 128
BAND = 512
EXT = BAND + 2 * LANES
FAR = 512
STEP = 16
SLOTS = 4
COPIES = 176
UP, MIDDLE, DOWN = (0, 128), (128, 384), (384, 512)


def tables():
    k = np.arange(N)
    angles = (np.outer(k, k) % N).astype(np.float32) * np.float32(2.0 * math.pi / N)
    c = (np.cos(angles) / np.float32(16.0)).astype(ml_dtypes.bfloat16)
    s = (np.sin(angles) / np.float32(16.0)).astype(ml_dtypes.bfloat16)
    a = np.block([[c, s], [-s, c]])
    b = np.ascontiguousarray(a.T)

    def blocked(t):
        return np.ascontiguousarray(t.reshape(2, 2, HALF, 2 * N).swapaxes(0, 1).reshape(2 * N, 2 * N))

    return a, b, blocked(a), blocked(b)


def kernel(shape, *refs):
    sample, probe, amps, *table_refs, rows_at, cols_at, live = refs[:10]
    out_sample, out_probe, out_sums, out_weight = refs[10:14]
    scratch = iter(refs[14:])

    def two():
        return next(scratch), next(scratch)

    nx, ny, nz = shape
    field, prb = two(), two()
    amp, ta, tb, la, lb, patch, wave, back, mid, corr, spec, chi, light, placed = (
        next(scratch) for _ in range(14)
    )
    halo_up, halo_dn, own, from_up, from_dn, from_left, from_right = (two() for _ in range(7))
    w_up, w_dn, w_own, w_from_up, w_from_dn, w_left, w_right = (two() for _ in range(7))
    part, rc, hs, rxa, ryb, hxa, hyb, rya, rxb, zb, rz, zg, full = (two() for _ in range(13))
    vpart, vrc, vhs, vrx, vhx, vry, vz, vfull = (two() for _ in range(8))
    load_sem, send_sem, recv_sem = scratch

    g, d = lax.axis_index("grp"), lax.axis_index("dev")
    ng, nd = 2 * ny, nx * nz
    y, core = g // 2, g % 2
    x, z = d // nz, d % nz
    above = {"grp": (g + ng - 1) % ng, "dev": d}
    below = {"grp": (g + 1) % ng, "dev": d}
    left = {"grp": g, "dev": (d + nd - 1) % nd}
    right = {"grp": g, "dev": (d + 1) % nd}
    partner = {"grp": y * 2 + 1 - core, "dev": d}
    xs = [(x + k) % nx for k in range(nx)]
    ys = [(y + k) % ny for k in range(ny)]
    zs = [(z + k) % nz for k in range(nz)]
    on_x = [{"grp": g, "dev": v * nz + z} for v in xs]
    on_y = [{"grp": v * 2 + core, "dev": d} for v in ys]
    on_z = [{"grp": g, "dev": x * nz + v} for v in zs]

    copies = []

    def remote(src, dst, to):
        n = len(copies)
        copy = pltpu.make_async_remote_copy(
            src_ref=src, dst_ref=dst, send_sem=send_sem.at[n], recv_sem=recv_sem.at[n],
            device_id=to, device_id_type=MESH,
        )
        copies.append(copy)
        return copy

    def start(group):
        for copy in group:
            copy.start()
        return group

    def send(src, dst, to):
        return start([remote(src, dst, to)])[0]

    def arrive(group):
        for copy in group:
            copy.wait_recv()

    moves = [(sample, field[0].at[1, :, LANES : LANES + BAND, :]), (probe, prb[0])]
    moves += list(zip(table_refs, (ta, tb, la, lb), strict=True)) + [(amps, amp)]
    loads = [pltpu.make_async_copy(src, dst, load_sem.at[n]) for n, (src, dst) in enumerate(moves)]
    for load in loads:
        load.start()

    barrier = pltpu.get_barrier_semaphore()
    peers = [above, below, left, right, partner] + on_x[1:] + on_y[1:] + on_z[1:]
    for peer in peers:
        pl.semaphore_signal(barrier, inc=1, device_id=peer, device_id_type=MESH)
    pl.semaphore_wait(barrier, len(peers))

    row_anchor = g * BAND - LANES
    col_anchor = d * LANES - LANES
    starts = [jnp.clip(rows_at[p] - row_anchor, 0, FAR) for p in range(SLOTS)]

    def alive(p):
        return jnp.full((STEP, LANES), p, jnp.int32) < jnp.full((STEP, LANES), live[0], jnp.int32)

    def send_columns(f, source, lo, hi):
        src = source(lo, hi)
        return [
            send(src, f.at[0, :, LANES + lo : LANES + hi, :], right),
            send(src, f.at[2, :, LANES + lo : LANES + hi, :], left),
        ]

    def forward_up(f, t, src=None):
        src = f.at[t, :, LANES : 2 * LANES, :] if src is None else src
        return send(src, f.at[t, :, LANES + BAND : EXT, :], above)

    def forward_down(f, t, src=None):
        src = f.at[t, :, BAND : LANES + BAND, :] if src is None else src
        return send(src, f.at[t, :, 0:LANES, :], below)

    def spread(f, sent_up, sent_down, sent_middle, forwards):
        arrive(sent_up)
        forwards += [forward_up(f, 0), forward_up(f, 2)]
        arrive(sent_down)
        forwards += [forward_down(f, 0), forward_down(f, 2)]
        return sent_middle + forwards

    def argument(lo, hi):
        return sample.at[:, lo:hi, :]

    sent_up = send_columns(field[0], argument, *UP)
    sent_down = send_columns(field[0], argument, *DOWN)
    forwards = [forward_up(field[0], 1, argument(*UP)), forward_down(field[0], 1, argument(*DOWN))]
    sent_middle = send_columns(field[0], argument, *MIDDLE)

    def clear(i, _):
        zero = jnp.zeros((STEP, LANES), jnp.float32)
        rr = pl.multiple_of(i * STEP, STEP)
        for p in range(SLOTS):
            for t in range(3):
                for at in (rr, FAR + N + rr):
                    for ch in range(2):
                        placed[p, t, ch, pl.ds(at, STEP), :] = zero
        return 0

    lax.fori_loop(0, FAR // STEP, clear, 0)
    for it in range(2):
        part[it][...] = jnp.zeros(part[it].shape, jnp.float32)
        vpart[it][...] = jnp.zeros(vpart[it].shape, jnp.float32)

    def placing(p):
        s = jnp.clip(cols_at[p] - col_anchor, 0, LANES)
        lane = lax.broadcasted_iota(jnp.int32, (STEP, LANES), 1)
        return s % LANES, lane >= s

    def total(sources, dst, first, lo, hi):
        def body(i, _):
            rr = pl.multiple_of(lo + i * 2 * STEP, 2 * STEP)
            for src, index in sources:
                values = [
                    placed[(p, *src, pl.ds(FAR + first + rr - starts[p], 2 * STEP), slice(None))]
                    for p in range(SLOTS)
                ]
                dst[(*index, pl.ds(rr, 2 * STEP), slice(None))] = (values[0] + values[1]) + (
                    values[2] + values[3]
                )
            return 0

        lax.fori_loop(0, (hi - lo) // (2 * STEP), body, 0)

    grads = [((t, ch), (t, ch)) for t in range(3) for ch in range(2)]
    lights = [((t, 0), (t,)) for t in range(3)]

    def illuminate(it):
        for j in range(2):
            cols = slice(j * LANES, (j + 1) * LANES)
            value = prb[it][0, :, cols] ** 2 + prb[it][1, :, cols] ** 2
            light[j] = value + (prb[it][2, :, cols] ** 2 + prb[it][3, :, cols] ** 2)

        def place(p, _):
            ahead, late = placing(p)
            used = alive(p)
            for rr in range(0, N, STEP):
                a, b = (
                    pltpu.roll(jnp.where(used, light[j, rr : rr + STEP, :], 0.0), ahead, 1) for j in range(2)
                )
                at = slice(FAR + rr, FAR + rr + STEP)
                placed[p, 0, 0, at, :] = jnp.where(late, a, 0.0)
                placed[p, 1, 0, at, :] = jnp.where(late, b, a)
                placed[p, 2, 0, at, :] = jnp.where(late, 0.0, b)
            return 0

        lax.fori_loop(0, SLOTS, place, 0)
        total(lights, w_up[it], 0, 0, LANES)
        up = send(w_up[it], w_from_dn[it], above)
        total(lights, w_dn[it], LANES + BAND, 0, LANES)
        down = send(w_dn[it], w_from_up[it], below)
        total(lights, w_own[it], LANES, 0, BAND)
        return [up, down]

    def gather(it):
        f = field[it]

        def body(p, _):
            r0 = jnp.clip(rows_at[p] - row_anchor, 0, FAR)
            s = jnp.clip(cols_at[p] - col_anchor, 0, LANES)
            behind = (LANES - s) % LANES
            early = lax.broadcasted_iota(jnp.int32, (STEP, LANES), 1) < LANES - s
            used = alive(p)
            for rr in range(0, N, STEP):
                rows = slice(rr, rr + STEP)
                halves = []
                for ch in range(2):
                    a, b, c = (pltpu.roll(f[t, ch, pl.ds(r0 + rr, STEP), :], behind, 1) for t in range(3))
                    halves.append((jnp.where(early, a, b), jnp.where(early, b, c)))
                for j in range(2):
                    o_re, o_im = halves[0][j], halves[1][j]
                    patch[p, 0, j, rows, :] = o_re
                    patch[p, 1, j, rows, :] = o_im
                    v = jnp.where(used, o_re * o_re + o_im * o_im, 0.0).reshape(2, 8, LANES)
                    vpart[it][rr // 8 : rr // 8 + 2, j] += v
            return 0

        lax.fori_loop(0, SLOTS, body, 0)

    def position(it, p):
        pr = prb[it]
        ahead, late = placing(p)
        used = alive(p)
        f32 = jnp.float32
        for rr in range(0, N, STEP):
            rows = slice(rr, rr + STEP)
            low = slice(N + rr, N + rr + STEP)
            for j in range(2):
                o_re, o_im = patch[p, 0, j, rows, :], patch[p, 1, j, rows, :]
                for m in range(2):
                    cols = slice(m * N + j * LANES, m * N + (j + 1) * LANES)
                    p_re = pr[2 * m, rows, j * LANES : (j + 1) * LANES]
                    p_im = pr[2 * m + 1, rows, j * LANES : (j + 1) * LANES]
                    wave[rows, cols] = (p_re * o_re - p_im * o_im).astype(jnp.bfloat16)
                    wave[low, cols] = (p_re * o_im + p_im * o_re).astype(jnp.bfloat16)
        for rb in range(2):
            block = slice(rb * 2 * HALF, (rb + 1) * 2 * HALF)
            first = jnp.dot(la[block, :], wave[...], preferred_element_type=f32).astype(jnp.bfloat16)
            for m in range(2):
                for c in range(2):
                    mid[rb, m * HALF : (m + 1) * HALF, c * N : (c + 1) * N] = first[
                        c * HALF : (c + 1) * HALF, m * N : (m + 1) * N
                    ]
            spec[rb] = jnp.dot(mid[rb], tb[...], preferred_element_type=f32)
            for rr in range(0, HALF, STEP):
                for j in range(2):
                    cols = [slice(c * N + j * LANES, c * N + (j + 1) * LANES) for c in range(2)]
                    rows = [slice(m * HALF + rr, m * HALF + rr + STEP) for m in range(2)]
                    values = [[spec[rb, rows[m], cols[c]] for c in range(2)] for m in range(2)]
                    intensity = (values[0][0] ** 2 + values[0][1] ** 2) + (
                        values[1][0] ** 2 + values[1][1] ** 2
                    )
                    measured = amp[p, rb * HALF + rr : rb * HALF + rr + STEP, cols[0]]
                    factor = measured * lax.rsqrt(jnp.maximum(intensity, INTENSITY_FLOOR)) - 1.0
                    factor = jnp.where(used, factor, 0.0)
                    for m in range(2):
                        for c in range(2):
                            corr[rb, rows[m], cols[c]] = (values[m][c] * factor).astype(jnp.bfloat16)
            undone = jnp.dot(corr[rb], ta[...], preferred_element_type=f32).astype(jnp.bfloat16)
            for m in range(2):
                for c in range(2):
                    back[
                        c * N + rb * HALF : c * N + (rb + 1) * HALF, m * N : (m + 1) * N
                    ] = undone[m * HALF : (m + 1) * HALF, c * N : (c + 1) * N]
        for rb in range(2):
            block = slice(rb * 2 * HALF, (rb + 1) * 2 * HALF)
            chi[rb] = jnp.dot(lb[block, :], back[...], preferred_element_type=f32)
            for rr in range(0, HALF, STEP):
                at = rb * HALF + rr
                rows = slice(at, at + STEP)
                terms = []
                for j in range(2):
                    o_re, o_im = patch[p, 0, j, rows, :], patch[p, 1, j, rows, :]
                    g_re = g_im = 0.0
                    for m in range(2):
                        p_re = pr[2 * m, rows, j * LANES : (j + 1) * LANES]
                        p_im = pr[2 * m + 1, rows, j * LANES : (j + 1) * LANES]
                        cols = slice(m * N + j * LANES, m * N + (j + 1) * LANES)
                        b_re = chi[rb, rr : rr + STEP, cols]
                        b_im = chi[rb, HALF + rr : HALF + rr + STEP, cols]
                        g_re += p_re * b_re + p_im * b_im
                        g_im += p_re * b_im - p_im * b_re
                        h_re = o_re * b_re + o_im * b_im
                        h_im = o_re * b_im - o_im * b_re
                        pair = slice(at // 8, at // 8 + 2)
                        part[it][pair, 4 * m + j] += h_re.reshape(2, 8, LANES)
                        part[it][pair, 4 * m + 2 + j] += h_im.reshape(2, 8, LANES)
                    terms.append((g_re, g_im))
                put = slice(FAR + at, FAR + at + STEP)
                for ch in range(2):
                    a = pltpu.roll(terms[0][ch], ahead, 1)
                    b = pltpu.roll(terms[1][ch], ahead, 1)
                    placed[p, 0, ch, put, :] = jnp.where(late, a, 0.0)
                    placed[p, 1, ch, put, :] = jnp.where(late, b, a)
                    placed[p, 2, ch, put, :] = jnp.where(late, 0.0, b)

    def update(it, lo, hi):
        for rr in range(lo, hi, 2 * STEP):
            rows = slice(rr, rr + 2 * STEP)
            scale = w_own[it][1, rows, :]
            for ch in range(2):
                grad = own[it][1, ch, rows, :] + (from_left[it][ch, rows, :] + from_right[it][ch, rows, :])
                value = field[it][1, ch, LANES + rr : LANES + rr + 2 * STEP, :] + grad * scale
                if it == 0:
                    field[1][1, ch, LANES + rr : LANES + rr + 2 * STEP, :] = value
                else:
                    own[1][1, ch, rows, :] = value
        if it == 1:
            return [write(own[1].at[1, :, lo:hi, :], out_sample.at[:, lo:hi, :])]
        return []

    def finish_probe():
        for i in range(N // 8):
            at = slice(i * 8, i * 8 + 8)
            c, xy = i // (nx * ny), i % (nx * ny)
            for j in range(2):
                cols = slice(j * LANES, (j + 1) * LANES)
                scale = 1.0 / (vfull[0][i, j] + PROBE_DAMPING)
                for q in range(4):
                    grad = full[0][c, xy // ny, xy % ny, 2 * q + j]
                    prb[1][q, at, cols] = prb[0][q, at, cols] + grad * scale

    written = []

    def write(src, dst):
        copy = pltpu.make_async_copy(src, dst, load_sem.at[len(moves) + len(written)])
        copy.start()
        written.append(copy)
        return copy

    flushed = [0]

    def flush():
        for copy in copies[flushed[0] :]:
            copy.wait_send()
        flushed[0] = len(copies)

    for load in loads:
        load.wait()
    rows_w = illuminate(0)
    waiting = spread(field[0], sent_up, sent_down, sent_middle, forwards)
    arrive(waiting)

    half = nx * ny
    for it in range(2):
        if it == 0:
            gather(0)
        else:
            write(prb[1], out_probe)
            rows_w = illuminate(1)

        mine = vfull[it].at[(core * nx + x) * ny + y]
        v_core = remote(vpart[it].at[pl.ds((1 - core) * half, half)], vrc[it], partner)
        v_x = [remote(vhs[it].at[pl.ds(xs[k] * ny, ny)], vrx[it].at[k - 1], on_x[k]) for k in range(1, nx)]
        v_y = [remote(vhx[it].at[ys[k]], vry[it].at[k - 1], on_y[k]) for k in range(1, ny)]
        v_z = [remote(vz[it].at[z], vz[it].at[z], on_z[k]) for k in range(1, nz)]
        v_back_y = [remote(mine, mine, on_y[k]) for k in range(1, ny)]
        row = vfull[it].at[pl.ds((core * nx + x) * ny, ny)]
        v_back_x = [remote(row, row, on_x[k]) for k in range(1, nx)]
        whole = vfull[it].at[pl.ds(core * half, half)]
        v_back_core = remote(whole, whole, partner)
        w_sides = [
            remote(w_own[it].at[0], w_right[it], left),
            remote(w_own[it].at[2], w_left[it], right),
        ]
        v_core.start()

        def weight_core(it=it, v_core=v_core, v_x=v_x):
            v_core.wait_recv()
            vhs[it][...] = vpart[it][pl.ds(core * half, half)] + vrc[it][...]
            start(v_x)

        def weight_x(it=it, v_x=v_x, v_y=v_y):
            arrive(v_x)
            value = vhs[it][pl.ds(x * ny, ny)]
            for k in range(nx - 1):
                value += vrx[it][k]
            vhx[it][...] = value
            start(v_y)

        def light_sides(it=it, rows_w=rows_w, w_sides=w_sides):
            arrive(rows_w)
            for t in range(3):
                w_own[it][t, 0:LANES, :] += w_from_up[it][t]
                w_own[it][t, BAND - LANES : BAND, :] += w_from_dn[it][t]
            start(w_sides)

        def weight_y(it=it, v_y=v_y, v_z=v_z):
            arrive(v_y)
            value = vhx[it][y]
            for k in range(ny - 1):
                value += vry[it][k]
            vz[it][z] = value
            start(v_z)

        def visit(p, _, it=it, hooks=(weight_core, weight_x, light_sides, weight_y)):
            for n, hook in zip((1, 2, 2, 3), hooks, strict=True):
                pl.when(p == n)(hook)
            position(it, p)
            return 0

        lax.fori_loop(0, SLOTS, visit, 0)

        swap = send(part[it].at[pl.ds((1 - core) * half, half)], rc[it], partner)

        total(grads, halo_up[it], 0, 0, LANES)
        rows_up = send(halo_up[it], from_dn[it], above)
        total(grads, halo_dn[it], LANES + BAND, 0, LANES)
        rows_down = send(halo_dn[it], from_up[it], below)

        swap.wait_recv()
        for i in range(nx):
            for j in range(ny):
                hs[it][i, j] = part[it][core * half + i * ny + j] + rc[it][i * ny + j]
        ax = [send(hs[it].at[xs[k], :, 0:4], rxa[it].at[k - 1], on_x[k]) for k in range(1, nx)]
        by = [send(hs[it].at[:, ys[k], 4:8], ryb[it].at[k - 1], on_y[k]) for k in range(1, ny)]

        def send_sides(lo, hi, it=it):
            return [
                send(own[it].at[0, :, lo:hi, :], from_right[it].at[:, lo:hi, :], left),
                send(own[it].at[2, :, lo:hi, :], from_left[it].at[:, lo:hi, :], right),
            ]

        total(grads, own[it], LANES, *MIDDLE)
        side_middle = send_sides(*MIDDLE)

        arrive(v_z)
        value = vz[it][0]
        for k in range(1, nz):
            value += vz[it][k]
        vfull[it][(core * nx + x) * ny + y] = value
        start(v_back_y)

        total(grads, own[it], LANES, *UP)
        total(grads, own[it], LANES, *DOWN)

        def add_rows(src, lo, it=it):
            for t in range(3):
                for ch in range(2):
                    own[it][t, ch, lo : lo + LANES, :] += src[t, ch]

        rows_down.wait_recv()
        add_rows(from_up[it], UP[0])
        side_up = send_sides(*UP)
        rows_up.wait_recv()
        add_rows(from_dn[it], DOWN[0])
        side_down = send_sides(*DOWN)

        arrive(ax)
        value = hs[it][x, :, 0:4]
        for k in range(nx - 1):
            value += rxa[it][k]
        hxa[it][...] = value
        ay = [send(hxa[it].at[ys[k]], rya[it].at[k - 1], on_y[k]) for k in range(1, ny)]
        arrive(by)
        for i in range(nx):
            value = hs[it][i, y, 4:8]
            for k in range(ny - 1):
                value += ryb[it][k, i]
            hyb[it][i] = value
        bx = [send(hyb[it].at[xs[k]], rxb[it].at[k - 1], on_x[k]) for k in range(1, nx)]

        arrive(v_back_y)
        start(v_back_x)

        arrive(w_sides)
        lit = w_own[it][1] + (w_left[it][...] + w_right[it][...])
        w_own[it][1] = 1.0 / (lit + SAMPLE_DAMPING)

        arrive(ay)
        value = hxa[it][y]
        for k in range(ny - 1):
            value += rya[it][k]
        zb[it][0:4] = value
        arrive(bx)
        value = hyb[it][x]
        for k in range(nx - 1):
            value += rxb[it][k]
        zb[it][4:8] = value
        to_z = [send(zb[it].at[zs[k]], rz[it].at[k - 1], on_z[k]) for k in range(1, nz)]

        arrive(v_back_x)
        v_back_core.start()
        if it == 1:
            flush()

        arrive(side_middle)
        update(it, *MIDDLE)

        arrive(to_z)
        value = zb[it][z]
        for k in range(nz - 1):
            value += rz[it][k]
        zg[it][z] = value
        back_z = [send(zg[it].at[z], zg[it].at[z], on_z[k]) for k in range(1, nz)]

        arrive(side_up)
        update(it, *UP)
        if it == 0:

            def updated(lo, hi):
                return field[1].at[1, :, LANES + lo : LANES + hi, :]

            sent_up = send_columns(field[1], updated, *UP)
            forwards = [forward_up(field[1], 1)]

        arrive(back_z)
        full[it][core, x, y] = zg[it][...]
        mine = full[it].at[core, x, y, 0:4]
        ay = [send(mine, mine, on_y[k]) for k in range(1, ny)]
        mine = full[it].at[core, x, y, 4:8]
        bx = [send(mine, mine, on_x[k]) for k in range(1, nx)]

        arrive(side_down)
        update(it, *DOWN)
        if it == 0:
            sent_down = send_columns(field[1], updated, *DOWN)
            forwards.append(forward_down(field[1], 1))
            sent_middle = send_columns(field[1], updated, *MIDDLE)

        arrive(ay)
        mine = full[it].at[core, x, :, 0:4]
        ax = [send(mine, mine, on_x[k]) for k in range(1, nx)]
        arrive(bx)
        mine = full[it].at[core, :, y, 4:8]
        by = [send(mine, mine, on_y[k]) for k in range(1, ny)]
        if it == 0:
            waiting = spread(field[1], sent_up, sent_down, sent_middle, forwards)
        arrive(ax)
        arrive(by)
        mine = full[it].at[core]
        back_core = send(mine, mine, partner)
        v_back_core.wait_recv()
        if it == 0:
            arrive(waiting)
            gather(1)
            back_core.wait_recv()
            finish_probe()
        else:
            write(vfull[1], out_weight)
            flush()
            back_core.wait_recv()
            write(full[1], out_sums)

    for copy in written:
        copy.wait()


def finish(scale, sample, probe, sums, weight, new_sample, new_probe, probe_gradient):
    new_sample[...] = sample[...]
    for b in range(sums.shape[0]):
        rows = slice(8 * b, 8 * b + 8)
        for j in range(2):
            cols = slice(j * LANES, (j + 1) * LANES)
            damped = 1.0 / (weight[b, j] + PROBE_DAMPING)
            for q in range(4):
                grad = sums[b, 2 * q + j]
                new_probe[q // 2, q % 2, rows, cols] = probe[q, rows, cols] + grad * damped
                probe_gradient[q // 2, q % 2, rows, cols] = grad * scale


def solution(mesh):
    ng, nd = mesh.shape["grp"], mesh.shape["dev"]
    ny = ng // 2
    nz = nd // 4
    nx = nd // nz
    blocks = 2 * nx * ny
    args = tables()

    def vmem(*shape, dtype=jnp.float32):
        return pltpu.VMEM(shape, dtype)

    def two(*shape):
        return [vmem(*shape)] * 2

    def local(sample, probe, amps, rows_at, cols_at, live):
        hbm = pl.BlockSpec(memory_space=pl.ANY)
        smem = pl.BlockSpec(memory_space=pltpu.SMEM)
        square = (2 * N, 2 * N)
        f32 = jnp.float32
        raw_sample, raw_probe, sums, weight = pl.pallas_call(
            functools.partial(kernel, (nx, ny, nz)),
            out_shape=[
                jax.ShapeDtypeStruct((2, BAND, LANES), f32),
                jax.ShapeDtypeStruct((4, N, N), f32),
                jax.ShapeDtypeStruct((2, nx, ny, 8, 8, LANES), f32),
                jax.ShapeDtypeStruct((blocks, 2, 8, LANES), f32),
            ],
            in_specs=[hbm] * 7 + [smem] * 3,
            out_specs=[hbm] * 4,
            scratch_shapes=[
                *two(3, 2, EXT, LANES),
                *two(4, N, N),
                vmem(SLOTS, N, N),
                *[vmem(*square, dtype=jnp.bfloat16)] * 4,
                vmem(SLOTS, 2, 2, N, LANES),
                *[vmem(*square, dtype=jnp.bfloat16)] * 2,
                *[vmem(2, 2 * HALF, 2 * N, dtype=jnp.bfloat16)] * 2,
                *[vmem(2, 2 * HALF, 2 * N)] * 2,
                vmem(2, N, LANES),
                vmem(SLOTS, 3, 2, 2 * FAR + N, LANES),
                *two(3, 2, LANES, LANES),
                *two(3, 2, LANES, LANES),
                *two(3, 2, BAND, LANES),
                *two(3, 2, LANES, LANES),
                *two(3, 2, LANES, LANES),
                *two(2, BAND, LANES),
                *two(2, BAND, LANES),
                *two(3, LANES, LANES),
                *two(3, LANES, LANES),
                *two(3, BAND, LANES),
                *two(3, LANES, LANES),
                *two(3, LANES, LANES),
                *two(BAND, LANES),
                *two(BAND, LANES),
                *two(blocks, 8, 8, LANES),
                *two(blocks // 2, 8, 8, LANES),
                *two(nx, ny, 8, 8, LANES),
                *two(nx - 1, ny, 4, 8, LANES),
                *two(ny - 1, nx, 4, 8, LANES),
                *two(ny, 4, 8, LANES),
                *two(nx, 4, 8, LANES),
                *two(ny - 1, 4, 8, LANES),
                *two(nx - 1, 4, 8, LANES),
                *two(8, 8, LANES),
                *two(nz - 1, 8, LANES),
                *two(8, 8, LANES),
                *two(2, nx, ny, 8, 8, LANES),
                *two(blocks, 2, 8, LANES),
                *two(blocks // 2, 2, 8, LANES),
                *two(blocks // 2, 2, 8, LANES),
                *two(nx - 1, ny, 2, 8, LANES),
                *two(ny, 2, 8, LANES),
                *two(ny - 1, 2, 8, LANES),
                *two(nz, 2, 8, LANES),
                *two(blocks, 2, 8, LANES),
                pltpu.SemaphoreType.DMA((13,)),
                pltpu.SemaphoreType.DMA((COPIES,)),
                pltpu.SemaphoreType.DMA((COPIES,)),
            ],
            compiler_params=pltpu.CompilerParams(
                collective_id=0, has_side_effects=True, vmem_limit_bytes=60 * 1024 * 1024
            ),
            cost_estimate=pl.CostEstimate(
                flops=2 * 4 * 4 * 2 * 512**3, bytes_accessed=6 << 20, transcendentals=8 * N * N
            ),
        )(sample, probe.reshape(4, N, N), amps, *args, rows_at, cols_at, live)
        steps = 4
        some, rows = blocks // steps, N // steps
        tile = pl.BlockSpec((2, BAND // steps, LANES), lambda i: (0, i, 0))
        modes = pl.BlockSpec((2, 2, rows, N), lambda i: (0, 0, i, 0))
        return pl.pallas_call(
            functools.partial(finish, 1.0 / math.sqrt(SLOTS * ng * nd)),
            grid=(steps,),
            out_shape=[
                jax.ShapeDtypeStruct((2, BAND, LANES), f32),
                jax.ShapeDtypeStruct((2, 2, N, N), f32),
                jax.ShapeDtypeStruct((2, 2, N, N), f32),
            ],
            in_specs=[
                tile,
                pl.BlockSpec((4, rows, N), lambda i: (0, i, 0)),
                pl.BlockSpec((some, 8, 8, LANES), lambda i: (i, 0, 0, 0)),
                pl.BlockSpec((some, 2, 8, LANES), lambda i: (i, 0, 0, 0)),
            ],
            out_specs=[tile, modes, modes],
            compiler_params=pltpu.CompilerParams(vmem_limit_bytes=60 * 1024 * 1024),
            cost_estimate=pl.CostEstimate(flops=16 * N * N, bytes_accessed=6 << 20, transcendentals=0),
        )(raw_sample, raw_probe, sums.reshape(blocks, 8, 8, LANES), weight)

    return jax.shard_map(
        local,
        mesh=mesh,
        in_specs=(
            P(None, "grp", "dev"),
            P(),
            P(("grp", "dev"), None, None),
            P(("grp", "dev")),
            P(("grp", "dev")),
            P(("grp", "dev")),
        ),
        out_specs=(P(None, "grp", "dev"), P(), P()),
        check_vma=False,
    )
```

```python
import functools
import math

import jax
import jax.numpy as jnp
import ml_dtypes
import numpy as np
from jax import lax
from jax.experimental import pallas as pl
from jax.experimental.pallas import tpu as pltpu
from jax.sharding import PartitionSpec as P

INTENSITY_FLOOR = 0.25
SAMPLE_DAMPING = 0.5
PROBE_DAMPING = 1.0
MESH = pl.DeviceIdType.MESH
LANES = 128
N = 256
HALF = 128
BAND = 512
EXT = BAND + 2 * LANES
FAR = 512
STEP = 16
SLOTS = 4
COPIES = 192
UP, MIDDLE, DOWN = (0, 128), (128, 384), (384, 512)


def tables():
    k = np.arange(N)
    angles = (np.outer(k, k) % N).astype(np.float32) * np.float32(2.0 * math.pi / N)
    c = (np.cos(angles) / np.float32(16.0)).astype(ml_dtypes.bfloat16)
    s = (np.sin(angles) / np.float32(16.0)).astype(ml_dtypes.bfloat16)
    a = np.block([[c, s], [-s, c]])
    b = np.ascontiguousarray(a.T)

    def blocked(t):
        return np.ascontiguousarray(t.reshape(2, 2, HALF, 2 * N).swapaxes(0, 1).reshape(2 * N, 2 * N))

    return a, b, blocked(a), blocked(b)


def kernel(shape, *refs):
    sample, probe, amps, *table_refs, rows_at, cols_at, live = refs[:10]
    out_sample, out_probe, out_sums, out_weight = refs[10:14]
    scratch = iter(refs[14:])

    def two():
        return next(scratch), next(scratch)

    nx, ny, nz = shape
    field, prb = two(), two()
    amp, ta, tb, la, lb, patch, wave, back, mid, corr, spec, chi, light, placed = (
        next(scratch) for _ in range(14)
    )
    halo_up, halo_dn, own, from_up, from_dn, from_left, from_right = (two() for _ in range(7))
    w_up, w_dn, w_own, w_from_up, w_from_dn, w_left, w_right = (two() for _ in range(7))
    part, rc, hs, r1, r2, hy, rx, zb, rz, zg, full = (two() for _ in range(11))
    vpart, vrc, vhs, vrx, vhx, vry, vz, vfull = (two() for _ in range(8))
    load_sem, send_sem, recv_sem = scratch

    g, d = lax.axis_index("grp"), lax.axis_index("dev")
    ng, nd = 2 * ny, nx * nz
    y, core = g // 2, g % 2
    x, z = d // nz, d % nz
    above = {"grp": (g + ng - 1) % ng, "dev": d}
    below = {"grp": (g + 1) % ng, "dev": d}
    left = {"grp": g, "dev": (d + nd - 1) % nd}
    right = {"grp": g, "dev": (d + 1) % nd}
    partner = {"grp": y * 2 + 1 - core, "dev": d}
    xs = [(x + k) % nx for k in range(nx)]
    ys = [(y + k) % ny for k in range(ny)]
    zs = [(z + k) % nz for k in range(nz)]
    on_x = [{"grp": g, "dev": v * nz + z} for v in xs]
    on_y = [{"grp": v * 2 + core, "dev": d} for v in ys]
    on_z = [{"grp": g, "dev": x * nz + v} for v in zs]

    copies = []

    def remote(src, dst, to):
        n = len(copies)
        copy = pltpu.make_async_remote_copy(
            src_ref=src, dst_ref=dst, send_sem=send_sem.at[n], recv_sem=recv_sem.at[n],
            device_id=to, device_id_type=MESH,
        )
        copies.append(copy)
        return copy

    def start(group):
        for copy in group:
            copy.start()
        return group

    def send(src, dst, to):
        return start([remote(src, dst, to)])[0]

    def arrive(group):
        for copy in group:
            copy.wait_recv()

    moves = [(sample, field[0].at[1, :, LANES : LANES + BAND, :]), (probe, prb[0])]
    moves += list(zip(table_refs, (ta, tb, la, lb), strict=True)) + [(amps, amp)]
    loads = [pltpu.make_async_copy(src, dst, load_sem.at[n]) for n, (src, dst) in enumerate(moves)]
    for load in loads:
        load.start()

    barrier = pltpu.get_barrier_semaphore()
    peers = [above, below, left, right, partner] + on_x[1:] + on_y[1:] + on_z[1:]
    for peer in peers:
        pl.semaphore_signal(barrier, inc=1, device_id=peer, device_id_type=MESH)
    pl.semaphore_wait(barrier, len(peers))

    row_anchor = g * BAND - LANES
    col_anchor = d * LANES - LANES
    starts = [jnp.clip(rows_at[p] - row_anchor, 0, FAR) for p in range(SLOTS)]

    def alive(p):
        return jnp.full((STEP, LANES), p, jnp.int32) < jnp.full((STEP, LANES), live[0], jnp.int32)

    def send_columns(f, source, lo, hi):
        src = source(lo, hi)
        return [
            send(src, f.at[0, :, LANES + lo : LANES + hi, :], right),
            send(src, f.at[2, :, LANES + lo : LANES + hi, :], left),
        ]

    def forward_up(f, t, src=None):
        src = f.at[t, :, LANES : 2 * LANES, :] if src is None else src
        return send(src, f.at[t, :, LANES + BAND : EXT, :], above)

    def forward_down(f, t, src=None):
        src = f.at[t, :, BAND : LANES + BAND, :] if src is None else src
        return send(src, f.at[t, :, 0:LANES, :], below)

    def spread(f, sent_up, sent_down, sent_middle, forwards):
        arrive(sent_up)
        forwards += [forward_up(f, 0), forward_up(f, 2)]
        arrive(sent_down)
        forwards += [forward_down(f, 0), forward_down(f, 2)]
        return sent_middle + forwards

    def argument(lo, hi):
        return sample.at[:, lo:hi, :]

    sent_up = send_columns(field[0], argument, *UP)
    sent_down = send_columns(field[0], argument, *DOWN)
    forwards = [forward_up(field[0], 1, argument(*UP)), forward_down(field[0], 1, argument(*DOWN))]
    sent_middle = send_columns(field[0], argument, *MIDDLE)

    def clear(i, _):
        zero = jnp.zeros((STEP, LANES), jnp.float32)
        rr = pl.multiple_of(i * STEP, STEP)
        for p in range(SLOTS):
            for t in range(3):
                for at in (rr, FAR + N + rr):
                    for ch in range(2):
                        placed[p, t, ch, pl.ds(at, STEP), :] = zero
        return 0

    lax.fori_loop(0, FAR // STEP, clear, 0)
    for it in range(2):
        part[it][...] = jnp.zeros(part[it].shape, jnp.float32)
        vpart[it][...] = jnp.zeros(vpart[it].shape, jnp.float32)

    def placing(p):
        s = jnp.clip(cols_at[p] - col_anchor, 0, LANES)
        lane = lax.broadcasted_iota(jnp.int32, (STEP, LANES), 1)
        return s % LANES, lane >= s

    def total(sources, dst, first, lo, hi):
        def body(i, _):
            rr = pl.multiple_of(lo + i * 2 * STEP, 2 * STEP)
            for src, index in sources:
                values = [
                    placed[(p, *src, pl.ds(FAR + first + rr - starts[p], 2 * STEP), slice(None))]
                    for p in range(SLOTS)
                ]
                dst[(*index, pl.ds(rr, 2 * STEP), slice(None))] = (values[0] + values[1]) + (
                    values[2] + values[3]
                )
            return 0

        lax.fori_loop(0, (hi - lo) // (2 * STEP), body, 0)

    grads = [((t, ch), (t, ch)) for t in range(3) for ch in range(2)]
    lights = [((t, 0), (t,)) for t in range(3)]

    def illuminate(it):
        for j in range(2):
            cols = slice(j * LANES, (j + 1) * LANES)
            value = prb[it][0, :, cols] ** 2 + prb[it][1, :, cols] ** 2
            light[j] = value + (prb[it][2, :, cols] ** 2 + prb[it][3, :, cols] ** 2)

        def place(p, _):
            ahead, late = placing(p)
            used = alive(p)
            for rr in range(0, N, STEP):
                a, b = (
                    pltpu.roll(jnp.where(used, light[j, rr : rr + STEP, :], 0.0), ahead, 1) for j in range(2)
                )
                at = slice(FAR + rr, FAR + rr + STEP)
                placed[p, 0, 0, at, :] = jnp.where(late, a, 0.0)
                placed[p, 1, 0, at, :] = jnp.where(late, b, a)
                placed[p, 2, 0, at, :] = jnp.where(late, 0.0, b)
            return 0

        lax.fori_loop(0, SLOTS, place, 0)
        total(lights, w_up[it], 0, 0, LANES)
        up = send(w_up[it], w_from_dn[it], above)
        total(lights, w_dn[it], LANES + BAND, 0, LANES)
        down = send(w_dn[it], w_from_up[it], below)
        total(lights, w_own[it], LANES, 0, BAND)
        return [up, down]

    def gather(it):
        f = field[it]

        def body(p, _):
            r0 = jnp.clip(rows_at[p] - row_anchor, 0, FAR)
            s = jnp.clip(cols_at[p] - col_anchor, 0, LANES)
            behind = (LANES - s) % LANES
            early = lax.broadcasted_iota(jnp.int32, (STEP, LANES), 1) < LANES - s
            used = alive(p)
            for rr in range(0, N, STEP):
                rows = slice(rr, rr + STEP)
                halves = []
                for ch in range(2):
                    a, b, c = (pltpu.roll(f[t, ch, pl.ds(r0 + rr, STEP), :], behind, 1) for t in range(3))
                    halves.append((jnp.where(early, a, b), jnp.where(early, b, c)))
                for j in range(2):
                    o_re, o_im = halves[0][j], halves[1][j]
                    patch[p, 0, j, rows, :] = o_re
                    patch[p, 1, j, rows, :] = o_im
                    v = jnp.where(used, o_re * o_re + o_im * o_im, 0.0).reshape(2, 8, LANES)
                    vpart[it][rr // 8 : rr // 8 + 2, j] += v
            return 0

        lax.fori_loop(0, SLOTS, body, 0)

    def position(it, p):
        pr = prb[it]
        ahead, late = placing(p)
        used = alive(p)
        f32 = jnp.float32
        for rr in range(0, N, STEP):
            rows = slice(rr, rr + STEP)
            low = slice(N + rr, N + rr + STEP)
            for j in range(2):
                o_re, o_im = patch[p, 0, j, rows, :], patch[p, 1, j, rows, :]
                for m in range(2):
                    cols = slice(m * N + j * LANES, m * N + (j + 1) * LANES)
                    p_re = pr[2 * m, rows, j * LANES : (j + 1) * LANES]
                    p_im = pr[2 * m + 1, rows, j * LANES : (j + 1) * LANES]
                    wave[rows, cols] = (p_re * o_re - p_im * o_im).astype(jnp.bfloat16)
                    wave[low, cols] = (p_re * o_im + p_im * o_re).astype(jnp.bfloat16)
        for rb in range(2):
            block = slice(rb * 2 * HALF, (rb + 1) * 2 * HALF)
            first = jnp.dot(la[block, :], wave[...], preferred_element_type=f32).astype(jnp.bfloat16)
            for m in range(2):
                for c in range(2):
                    mid[rb, m * HALF : (m + 1) * HALF, c * N : (c + 1) * N] = first[
                        c * HALF : (c + 1) * HALF, m * N : (m + 1) * N
                    ]
            spec[rb] = jnp.dot(mid[rb], tb[...], preferred_element_type=f32)
            for rr in range(0, HALF, STEP):
                for j in range(2):
                    cols = [slice(c * N + j * LANES, c * N + (j + 1) * LANES) for c in range(2)]
                    rows = [slice(m * HALF + rr, m * HALF + rr + STEP) for m in range(2)]
                    values = [[spec[rb, rows[m], cols[c]] for c in range(2)] for m in range(2)]
                    intensity = (values[0][0] ** 2 + values[0][1] ** 2) + (
                        values[1][0] ** 2 + values[1][1] ** 2
                    )
                    measured = amp[p, rb * HALF + rr : rb * HALF + rr + STEP, cols[0]]
                    factor = measured * lax.rsqrt(jnp.maximum(intensity, INTENSITY_FLOOR)) - 1.0
                    factor = jnp.where(used, factor, 0.0)
                    for m in range(2):
                        for c in range(2):
                            corr[rb, rows[m], cols[c]] = (values[m][c] * factor).astype(jnp.bfloat16)
            undone = jnp.dot(corr[rb], ta[...], preferred_element_type=f32).astype(jnp.bfloat16)
            for m in range(2):
                for c in range(2):
                    back[
                        c * N + rb * HALF : c * N + (rb + 1) * HALF, m * N : (m + 1) * N
                    ] = undone[m * HALF : (m + 1) * HALF, c * N : (c + 1) * N]
        for rb in range(2):
            block = slice(rb * 2 * HALF, (rb + 1) * 2 * HALF)
            chi[rb] = jnp.dot(lb[block, :], back[...], preferred_element_type=f32)
            for rr in range(0, HALF, STEP):
                at = rb * HALF + rr
                rows = slice(at, at + STEP)
                terms = []
                for j in range(2):
                    o_re, o_im = patch[p, 0, j, rows, :], patch[p, 1, j, rows, :]
                    g_re = g_im = 0.0
                    for m in range(2):
                        p_re = pr[2 * m, rows, j * LANES : (j + 1) * LANES]
                        p_im = pr[2 * m + 1, rows, j * LANES : (j + 1) * LANES]
                        cols = slice(m * N + j * LANES, m * N + (j + 1) * LANES)
                        b_re = chi[rb, rr : rr + STEP, cols]
                        b_im = chi[rb, HALF + rr : HALF + rr + STEP, cols]
                        g_re += p_re * b_re + p_im * b_im
                        g_im += p_re * b_im - p_im * b_re
                        h_re = o_re * b_re + o_im * b_im
                        h_im = o_re * b_im - o_im * b_re
                        b = at // 8
                        pair = (b // (nx * ny), b // ny % nx, slice(b % ny, b % ny + 2))
                        part[it][(*pair, 4 * m + j)] += h_re.reshape(2, 8, LANES)
                        part[it][(*pair, 4 * m + 2 + j)] += h_im.reshape(2, 8, LANES)
                    terms.append((g_re, g_im))
                put = slice(FAR + at, FAR + at + STEP)
                for ch in range(2):
                    a = pltpu.roll(terms[0][ch], ahead, 1)
                    b = pltpu.roll(terms[1][ch], ahead, 1)
                    placed[p, 0, ch, put, :] = jnp.where(late, a, 0.0)
                    placed[p, 1, ch, put, :] = jnp.where(late, b, a)
                    placed[p, 2, ch, put, :] = jnp.where(late, 0.0, b)

    def update(it, lo, hi):
        for rr in range(lo, hi, 2 * STEP):
            rows = slice(rr, rr + 2 * STEP)
            scale = w_own[it][1, rows, :]
            for ch in range(2):
                grad = own[it][1, ch, rows, :] + (from_left[it][ch, rows, :] + from_right[it][ch, rows, :])
                value = field[it][1, ch, LANES + rr : LANES + rr + 2 * STEP, :] + grad * scale
                if it == 0:
                    field[1][1, ch, LANES + rr : LANES + rr + 2 * STEP, :] = value
                else:
                    own[1][1, ch, rows, :] = value
        if it == 1:
            return [write(own[1].at[1, :, lo:hi, :], out_sample.at[:, lo:hi, :])]
        return []

    def finish_probe():
        for i in range(N // 8):
            at = slice(i * 8, i * 8 + 8)
            c, xy = i // (nx * ny), i % (nx * ny)
            for j in range(2):
                cols = slice(j * LANES, (j + 1) * LANES)
                scale = 1.0 / (vfull[0][i, j] + PROBE_DAMPING)
                for q in range(4):
                    grad = full[0][c, xy // ny, xy % ny, 2 * q + j]
                    prb[1][q, at, cols] = prb[0][q, at, cols] + grad * scale

    written = []

    def write(src, dst):
        copy = pltpu.make_async_copy(src, dst, load_sem.at[len(moves) + len(written)])
        copy.start()
        written.append(copy)
        return copy

    flushed = [0]

    def flush():
        for copy in copies[flushed[0] :]:
            copy.wait_send()
        flushed[0] = len(copies)

    for load in loads:
        load.wait()
    rows_w = illuminate(0)
    waiting = spread(field[0], sent_up, sent_down, sent_middle, forwards)
    arrive(waiting)

    half = nx * ny
    for it in range(2):
        if it == 0:
            gather(0)
        else:
            write(prb[1], out_probe)
            rows_w = illuminate(1)

        mine = vfull[it].at[(core * nx + x) * ny + y]
        v_core = remote(vpart[it].at[pl.ds((1 - core) * half, half)], vrc[it], partner)
        v_x = [remote(vhs[it].at[pl.ds(xs[k] * ny, ny)], vrx[it].at[k - 1], on_x[k]) for k in range(1, nx)]
        v_y = [remote(vhx[it].at[ys[k]], vry[it].at[k - 1], on_y[k]) for k in range(1, ny)]
        v_z = [remote(vz[it].at[z], vz[it].at[z], on_z[k]) for k in range(1, nz)]
        v_back_y = [remote(mine, mine, on_y[k]) for k in range(1, ny)]
        row = vfull[it].at[pl.ds((core * nx + x) * ny, ny)]
        v_back_x = [remote(row, row, on_x[k]) for k in range(1, nx)]
        whole = vfull[it].at[pl.ds(core * half, half)]
        v_back_core = remote(whole, whole, partner)
        w_sides = [
            remote(w_own[it].at[0], w_right[it], left),
            remote(w_own[it].at[2], w_left[it], right),
        ]
        v_core.start()

        def weight_core(it=it, v_core=v_core, v_x=v_x):
            v_core.wait_recv()
            vhs[it][...] = vpart[it][pl.ds(core * half, half)] + vrc[it][...]
            start(v_x)

        def weight_x(it=it, v_x=v_x, v_y=v_y):
            arrive(v_x)
            value = vhs[it][pl.ds(x * ny, ny)]
            for k in range(nx - 1):
                value += vrx[it][k]
            vhx[it][...] = value
            start(v_y)

        def light_sides(it=it, rows_w=rows_w, w_sides=w_sides):
            arrive(rows_w)
            for t in range(3):
                w_own[it][t, 0:LANES, :] += w_from_up[it][t]
                w_own[it][t, BAND - LANES : BAND, :] += w_from_dn[it][t]
            start(w_sides)

        def weight_y(it=it, v_y=v_y, v_z=v_z):
            arrive(v_y)
            value = vhx[it][y]
            for k in range(ny - 1):
                value += vry[it][k]
            vz[it][z] = value
            start(v_z)

        def visit(p, _, it=it, hooks=(weight_core, weight_x, light_sides, weight_y)):
            for n, hook in zip((1, 2, 2, 3), hooks, strict=True):
                pl.when(p == n)(hook)
            position(it, p)
            return 0

        lax.fori_loop(0, SLOTS, visit, 0)

        sums, mates = part[it], rc[it]
        order = (2, 1, 3, 0)
        swap = [send(sums.at[1 - core, :, ys[k]], mates.at[:, ys[k]], partner) for k in order]
        planes = [slice(4 * h, 4 * h + 4) for h in range(2)]

        total(grads, halo_up[it], 0, 0, LANES)
        rows_up = send(halo_up[it], from_dn[it], above)
        total(grads, halo_dn[it], LANES + BAND, 0, LANES)
        rows_down = send(halo_dn[it], from_up[it], below)

        def sum_core(n, it=it, swap=swap):
            swap[n].wait_recv()
            at = ys[order[n]]
            hs[it][:, at] = part[it][core, :, at] + rc[it][:, at]

        sum_core(0)
        far = [
            [
                send(hs[it].at[0:2, ys[2], p], r1[it].at[0, h], on_y[1]),
                send(hs[it].at[2:4, ys[2], p], r1[it].at[1, h], on_y[3]),
            ]
            for h, p in enumerate(planes)
        ]

        def send_sides(lo, hi, it=it):
            return [
                send(own[it].at[0, :, lo:hi, :], from_right[it].at[:, lo:hi, :], left),
                send(own[it].at[2, :, lo:hi, :], from_left[it].at[:, lo:hi, :], right),
            ]

        total(grads, own[it], LANES, *MIDDLE)
        side_middle = send_sides(*MIDDLE)

        sum_core(1)
        sum_core(2)
        near = []
        for h, p in enumerate(planes):
            arrive(far[h])
            hs[it][0:2, ys[1], p] += r1[it][0, h]
            hs[it][2:4, ys[3], p] += r1[it][1, h]
            near.append(
                [
                    send(hs[it].at[:, ys[1], p], r2[it].at[0, h], on_y[1]),
                    send(hs[it].at[:, ys[3], p], r2[it].at[1, h], on_y[3]),
                ]
            )
        sum_core(3)

        total(grads, own[it], LANES, *UP)
        total(grads, own[it], LANES, *DOWN)

        def add_rows(src, lo, it=it):
            for t in range(3):
                for ch in range(2):
                    own[it][t, ch, lo : lo + LANES, :] += src[t, ch]

        rows_down.wait_recv()
        add_rows(from_up[it], UP[0])
        side_up = send_sides(*UP)
        rows_up.wait_recv()
        add_rows(from_dn[it], DOWN[0])
        side_down = send_sides(*DOWN)

        to_x = []
        for h, p in enumerate(planes):
            arrive(near[h])
            hy[it][h] = hs[it][:, y, p] + (r2[it][0, h] + r2[it][1, h])
            to_x.append([send(hy[it].at[h, xs[k]], rx[it].at[h, k - 1], on_x[k]) for k in range(1, nx)])

        arrive(v_z)
        value = vz[it][0]
        for k in range(1, nz):
            value += vz[it][k]
        vfull[it][(core * nx + x) * ny + y] = value
        start(v_back_y)

        arrive(w_sides)
        lit = w_own[it][1] + (w_left[it][...] + w_right[it][...])
        w_own[it][1] = 1.0 / (lit + SAMPLE_DAMPING)

        for h, p in enumerate(planes):
            arrive(to_x[h])
            value = hy[it][h, x]
            for k in range(nx - 1):
                value += rx[it][h, k]
            zb[it][p] = value
        to_z = [send(zb[it].at[zs[k]], rz[it].at[k - 1], on_z[k]) for k in range(1, nz)]

        arrive(v_back_y)
        start(v_back_x)

        arrive(side_middle)
        update(it, *MIDDLE)

        arrive(to_z)
        value = zb[it][z]
        for k in range(nz - 1):
            value += rz[it][k]
        zg[it][z] = value
        back_z = [send(zg[it].at[z], zg[it].at[z], on_z[k]) for k in range(1, nz)]

        arrive(side_up)
        update(it, *UP)
        if it == 0:

            def updated(lo, hi):
                return field[1].at[1, :, LANES + lo : LANES + hi, :]

            sent_up = send_columns(field[1], updated, *UP)
            forwards = [forward_up(field[1], 1)]

        arrive(back_z)
        result = full[it]
        result[core, x, y] = zg[it][...]
        mine = [result.at[core, x, y, p] for p in planes]
        back_x = [[send(m, m, on_x[k]) for k in range(1, nx)] for m in mine]
        arrive(v_back_x)
        v_back_core.start()
        if it == 1:
            flush()

        arrive(side_down)
        update(it, *DOWN)
        if it == 0:
            sent_down = send_columns(field[1], updated, *DOWN)
            forwards.append(forward_down(field[1], 1))
            sent_middle = send_columns(field[1], updated, *MIDDLE)

        def to_core(k, result=result):
            piece = result.at[core, :, ys[k]]
            return send(piece, piece, partner)

        back_near = []
        for h, p in enumerate(planes):
            arrive(back_x[h])
            mine = result.at[core, :, y, p]
            back_near.append([send(mine, mine, on_y[k]) for k in (1, 3)])
        back_core = [to_core(0)]
        back_far = []
        for h, p in enumerate(planes):
            arrive(back_near[h])
            low, high = result.at[core, 0:2, ys[3], p], result.at[core, 2:4, ys[1], p]
            back_far.append([send(low, low, on_y[1]), send(high, high, on_y[3])])
        back_core += [to_core(1), to_core(3)]
        if it == 0:
            waiting = spread(field[1], sent_up, sent_down, sent_middle, forwards)
        for h in range(2):
            arrive(back_far[h])
        back_core.append(to_core(2))
        v_back_core.wait_recv()
        if it == 0:
            arrive(waiting)
            gather(1)
            arrive(back_core)
            finish_probe()
        else:
            write(vfull[1], out_weight)
            flush()
            arrive(back_core)
            write(full[1], out_sums)

    for copy in written:
        copy.wait()


def finish(scale, sample, probe, sums, weight, new_sample, new_probe, probe_gradient):
    new_sample[...] = sample[...]
    for b in range(sums.shape[0]):
        rows = slice(8 * b, 8 * b + 8)
        for j in range(2):
            cols = slice(j * LANES, (j + 1) * LANES)
            damped = 1.0 / (weight[b, j] + PROBE_DAMPING)
            for q in range(4):
                grad = sums[b, 2 * q + j]
                new_probe[q // 2, q % 2, rows, cols] = probe[q, rows, cols] + grad * damped
                probe_gradient[q // 2, q % 2, rows, cols] = grad * scale


def solution(mesh):
    ng, nd = mesh.shape["grp"], mesh.shape["dev"]
    ny = ng // 2
    nz = nd // 4
    nx = nd // nz
    blocks = 2 * nx * ny
    args = tables()

    def vmem(*shape, dtype=jnp.float32):
        return pltpu.VMEM(shape, dtype)

    def two(*shape):
        return [vmem(*shape)] * 2

    def local(sample, probe, amps, rows_at, cols_at, live):
        hbm = pl.BlockSpec(memory_space=pl.ANY)
        smem = pl.BlockSpec(memory_space=pltpu.SMEM)
        square = (2 * N, 2 * N)
        f32 = jnp.float32
        raw_sample, raw_probe, sums, weight = pl.pallas_call(
            functools.partial(kernel, (nx, ny, nz)),
            out_shape=[
                jax.ShapeDtypeStruct((2, BAND, LANES), f32),
                jax.ShapeDtypeStruct((4, N, N), f32),
                jax.ShapeDtypeStruct((2, nx, ny, 8, 8, LANES), f32),
                jax.ShapeDtypeStruct((blocks, 2, 8, LANES), f32),
            ],
            in_specs=[hbm] * 7 + [smem] * 3,
            out_specs=[hbm] * 4,
            scratch_shapes=[
                *two(3, 2, EXT, LANES),
                *two(4, N, N),
                vmem(SLOTS, N, N),
                *[vmem(*square, dtype=jnp.bfloat16)] * 4,
                vmem(SLOTS, 2, 2, N, LANES),
                *[vmem(*square, dtype=jnp.bfloat16)] * 2,
                *[vmem(2, 2 * HALF, 2 * N, dtype=jnp.bfloat16)] * 2,
                *[vmem(2, 2 * HALF, 2 * N)] * 2,
                vmem(2, N, LANES),
                vmem(SLOTS, 3, 2, 2 * FAR + N, LANES),
                *two(3, 2, LANES, LANES),
                *two(3, 2, LANES, LANES),
                *two(3, 2, BAND, LANES),
                *two(3, 2, LANES, LANES),
                *two(3, 2, LANES, LANES),
                *two(2, BAND, LANES),
                *two(2, BAND, LANES),
                *two(3, LANES, LANES),
                *two(3, LANES, LANES),
                *two(3, BAND, LANES),
                *two(3, LANES, LANES),
                *two(3, LANES, LANES),
                *two(BAND, LANES),
                *two(BAND, LANES),
                *two(2, nx, ny, 8, 8, LANES),
                *two(nx, ny, 8, 8, LANES),
                *two(nx, ny, 8, 8, LANES),
                *two(2, 2, nx // 2, 4, 8, LANES),
                *two(2, 2, nx, 4, 8, LANES),
                *two(2, nx, 4, 8, LANES),
                *two(2, nx - 1, 4, 8, LANES),
                *two(8, 8, LANES),
                *two(nz - 1, 8, LANES),
                *two(8, 8, LANES),
                *two(2, nx, ny, 8, 8, LANES),
                *two(blocks, 2, 8, LANES),
                *two(blocks // 2, 2, 8, LANES),
                *two(blocks // 2, 2, 8, LANES),
                *two(nx - 1, ny, 2, 8, LANES),
                *two(ny, 2, 8, LANES),
                *two(ny - 1, 2, 8, LANES),
                *two(nz, 2, 8, LANES),
                *two(blocks, 2, 8, LANES),
                pltpu.SemaphoreType.DMA((13,)),
                pltpu.SemaphoreType.DMA((COPIES,)),
                pltpu.SemaphoreType.DMA((COPIES,)),
            ],
            compiler_params=pltpu.CompilerParams(
                collective_id=0, has_side_effects=True, vmem_limit_bytes=60 * 1024 * 1024
            ),
            cost_estimate=pl.CostEstimate(
                flops=2 * 4 * 4 * 2 * 512**3, bytes_accessed=6 << 20, transcendentals=8 * N * N
            ),
        )(sample, probe.reshape(4, N, N), amps, *args, rows_at, cols_at, live)
        steps = 4
        some, rows = blocks // steps, N // steps
        tile = pl.BlockSpec((2, BAND // steps, LANES), lambda i: (0, i, 0))
        modes = pl.BlockSpec((2, 2, rows, N), lambda i: (0, 0, i, 0))
        return pl.pallas_call(
            functools.partial(finish, 1.0 / math.sqrt(SLOTS * ng * nd)),
            grid=(steps,),
            out_shape=[
                jax.ShapeDtypeStruct((2, BAND, LANES), f32),
                jax.ShapeDtypeStruct((2, 2, N, N), f32),
                jax.ShapeDtypeStruct((2, 2, N, N), f32),
            ],
            in_specs=[
                tile,
                pl.BlockSpec((4, rows, N), lambda i: (0, i, 0)),
                pl.BlockSpec((some, 8, 8, LANES), lambda i: (i, 0, 0, 0)),
                pl.BlockSpec((some, 2, 8, LANES), lambda i: (i, 0, 0, 0)),
            ],
            out_specs=[tile, modes, modes],
            compiler_params=pltpu.CompilerParams(vmem_limit_bytes=60 * 1024 * 1024),
            cost_estimate=pl.CostEstimate(flops=16 * N * N, bytes_accessed=6 << 20, transcendentals=0),
        )(raw_sample, raw_probe, sums.reshape(blocks, 8, 8, LANES), weight)

    return jax.shard_map(
        local,
        mesh=mesh,
        in_specs=(
            P(None, "grp", "dev"),
            P(),
            P(("grp", "dev"), None, None),
            P(("grp", "dev")),
            P(("grp", "dev")),
            P(("grp", "dev")),
        ),
        out_specs=(P(None, "grp", "dev"), P(), P()),
        check_vma=False,
    )
```

```python
import functools
import math

import jax
import jax.numpy as jnp
import ml_dtypes
import numpy as np
from jax import lax
from jax.experimental import pallas as pl
from jax.experimental.pallas import tpu as pltpu
from jax.sharding import PartitionSpec as P

INTENSITY_FLOOR = 0.25
SAMPLE_DAMPING = 0.5
PROBE_DAMPING = 1.0
MESH = pl.DeviceIdType.MESH
LANES = 128
N = 256
HALF = 128
BAND = 512
EXT = BAND + 2 * LANES
FAR = 512
STEP = 16
SLOTS = 4
COPIES = 192
UP, MIDDLE, DOWN = (0, 128), (128, 384), (384, 512)


def tables():
    k = np.arange(N)
    angles = (np.outer(k, k) % N).astype(np.float32) * np.float32(2.0 * math.pi / N)
    c = (np.cos(angles) / np.float32(16.0)).astype(ml_dtypes.bfloat16)
    s = (np.sin(angles) / np.float32(16.0)).astype(ml_dtypes.bfloat16)
    split = [np.block([[c[e::2, :HALF], s[e::2, :HALF]], [-s[e::2, :HALF], c[e::2, :HALF]]]) for e in range(2)]
    order = np.eye(N)[np.concatenate([k[0::2], k[1::2]])].astype(ml_dtypes.bfloat16)
    return np.stack([*split, split[0].T, split[1].T, order, order.T])


def kernel(shape, *refs):
    sample, probe, amps, table, rows_at, cols_at, live = refs[:7]
    out_sample, out_probe, out_sums, out_weight = refs[7:11]
    scratch = iter(refs[11:])

    def two():
        return next(scratch), next(scratch)

    nx, ny, nz = shape
    field, prb = two(), two()
    amp, tab, patch, wave, back, mid, corr, done, spec, undone, chi, light, placed = (
        next(scratch) for _ in range(13)
    )
    halo_up, halo_dn, own, from_up, from_dn, from_left, from_right = (two() for _ in range(7))
    w_up, w_dn, w_own, w_from_up, w_from_dn, w_left, w_right = (two() for _ in range(7))
    part, rc, hs, r1, r2, hy, rx, zb, rz, zg, full = (two() for _ in range(11))
    vpart, vrc, vhs, vrx, vhx, vry, vz, vfull = (two() for _ in range(8))
    load_sem, send_sem, recv_sem = scratch

    g, d = lax.axis_index("grp"), lax.axis_index("dev")
    ng, nd = 2 * ny, nx * nz
    y, core = g // 2, g % 2
    x, z = d // nz, d % nz
    above = {"grp": (g + ng - 1) % ng, "dev": d}
    below = {"grp": (g + 1) % ng, "dev": d}
    left = {"grp": g, "dev": (d + nd - 1) % nd}
    right = {"grp": g, "dev": (d + 1) % nd}
    partner = {"grp": y * 2 + 1 - core, "dev": d}
    xs = [(x + k) % nx for k in range(nx)]
    ys = [(y + k) % ny for k in range(ny)]
    zs = [(z + k) % nz for k in range(nz)]
    on_x = [{"grp": g, "dev": v * nz + z} for v in xs]
    on_y = [{"grp": v * 2 + core, "dev": d} for v in ys]
    on_z = [{"grp": g, "dev": x * nz + v} for v in zs]

    copies = []

    def remote(src, dst, to):
        n = len(copies)
        copy = pltpu.make_async_remote_copy(
            src_ref=src, dst_ref=dst, send_sem=send_sem.at[n], recv_sem=recv_sem.at[n],
            device_id=to, device_id_type=MESH,
        )
        copies.append(copy)
        return copy

    def start(group):
        for copy in group:
            copy.start()
        return group

    def send(src, dst, to):
        return start([remote(src, dst, to)])[0]

    def arrive(group):
        for copy in group:
            copy.wait_recv()

    moves = [(sample, field[0].at[1, :, LANES : LANES + BAND, :]), (probe, prb[0]), (table, tab), (amps, amp)]
    loads = [pltpu.make_async_copy(src, dst, load_sem.at[n]) for n, (src, dst) in enumerate(moves)]
    for load in loads:
        load.start()

    barrier = pltpu.get_barrier_semaphore()
    peers = [above, below, left, right, partner] + on_x[1:] + on_y[1:] + on_z[1:]
    for peer in peers:
        pl.semaphore_signal(barrier, inc=1, device_id=peer, device_id_type=MESH)
    pl.semaphore_wait(barrier, len(peers))

    row_anchor = g * BAND - LANES
    col_anchor = d * LANES - LANES
    starts = [jnp.clip(rows_at[p] - row_anchor, 0, FAR) for p in range(SLOTS)]

    def alive(p):
        return jnp.full((STEP, LANES), p, jnp.int32) < jnp.full((STEP, LANES), live[0], jnp.int32)

    def send_columns(f, source, lo, hi):
        src = source(lo, hi)
        return [
            send(src, f.at[0, :, LANES + lo : LANES + hi, :], right),
            send(src, f.at[2, :, LANES + lo : LANES + hi, :], left),
        ]

    def forward_up(f, t, src=None):
        src = f.at[t, :, LANES : 2 * LANES, :] if src is None else src
        return send(src, f.at[t, :, LANES + BAND : EXT, :], above)

    def forward_down(f, t, src=None):
        src = f.at[t, :, BAND : LANES + BAND, :] if src is None else src
        return send(src, f.at[t, :, 0:LANES, :], below)

    def spread(f, sent_up, sent_down, sent_middle, forwards):
        arrive(sent_up)
        forwards += [forward_up(f, 0), forward_up(f, 2)]
        arrive(sent_down)
        forwards += [forward_down(f, 0), forward_down(f, 2)]
        return sent_middle + forwards

    def argument(lo, hi):
        return sample.at[:, lo:hi, :]

    sent_up = send_columns(field[0], argument, *UP)
    sent_down = send_columns(field[0], argument, *DOWN)
    forwards = [forward_up(field[0], 1, argument(*UP)), forward_down(field[0], 1, argument(*DOWN))]
    sent_middle = send_columns(field[0], argument, *MIDDLE)

    def clear(i, _):
        zero = jnp.zeros((STEP, LANES), jnp.float32)
        rr = pl.multiple_of(i * STEP, STEP)
        for p in range(SLOTS):
            for t in range(3):
                for at in (rr, FAR + N + rr):
                    for ch in range(2):
                        placed[p, t, ch, pl.ds(at, STEP), :] = zero
        return 0

    lax.fori_loop(0, FAR // STEP, clear, 0)
    for it in range(2):
        part[it][...] = jnp.zeros(part[it].shape, jnp.float32)
        vpart[it][...] = jnp.zeros(vpart[it].shape, jnp.float32)

    def placing(p):
        s = jnp.clip(cols_at[p] - col_anchor, 0, LANES)
        lane = lax.broadcasted_iota(jnp.int32, (STEP, LANES), 1)
        return s % LANES, lane >= s

    def total(sources, dst, first, lo, hi):
        def body(i, _):
            rr = pl.multiple_of(lo + i * 2 * STEP, 2 * STEP)
            for src, index in sources:
                values = [
                    placed[(p, *src, pl.ds(FAR + first + rr - starts[p], 2 * STEP), slice(None))]
                    for p in range(SLOTS)
                ]
                dst[(*index, pl.ds(rr, 2 * STEP), slice(None))] = (values[0] + values[1]) + (
                    values[2] + values[3]
                )
            return 0

        lax.fori_loop(0, (hi - lo) // (2 * STEP), body, 0)

    grads = [((t, ch), (t, ch)) for t in range(3) for ch in range(2)]
    lights = [((t, 0), (t,)) for t in range(3)]

    def illuminate(it):
        for j in range(2):
            cols = slice(j * LANES, (j + 1) * LANES)
            value = prb[it][0, :, cols] ** 2 + prb[it][1, :, cols] ** 2
            light[j] = value + (prb[it][2, :, cols] ** 2 + prb[it][3, :, cols] ** 2)

        def place(p, _):
            ahead, late = placing(p)
            used = alive(p)
            for rr in range(0, N, STEP):
                a, b = (
                    pltpu.roll(jnp.where(used, light[j, rr : rr + STEP, :], 0.0), ahead, 1) for j in range(2)
                )
                at = slice(FAR + rr, FAR + rr + STEP)
                placed[p, 0, 0, at, :] = jnp.where(late, a, 0.0)
                placed[p, 1, 0, at, :] = jnp.where(late, b, a)
                placed[p, 2, 0, at, :] = jnp.where(late, 0.0, b)
            return 0

        lax.fori_loop(0, SLOTS, place, 0)
        total(lights, w_up[it], 0, 0, LANES)
        up = send(w_up[it], w_from_dn[it], above)
        total(lights, w_dn[it], LANES + BAND, 0, LANES)
        down = send(w_dn[it], w_from_up[it], below)
        total(lights, w_own[it], LANES, 0, BAND)
        return [up, down]

    def gather(it):
        f = field[it]

        def body(p, _):
            r0 = jnp.clip(rows_at[p] - row_anchor, 0, FAR)
            s = jnp.clip(cols_at[p] - col_anchor, 0, LANES)
            behind = (LANES - s) % LANES
            early = lax.broadcasted_iota(jnp.int32, (STEP, LANES), 1) < LANES - s
            used = alive(p)
            for rr in range(0, N, STEP):
                rows = slice(rr, rr + STEP)
                halves = []
                for ch in range(2):
                    a, b, c = (pltpu.roll(f[t, ch, pl.ds(r0 + rr, STEP), :], behind, 1) for t in range(3))
                    halves.append((jnp.where(early, a, b), jnp.where(early, b, c)))
                for j in range(2):
                    o_re, o_im = halves[0][j], halves[1][j]
                    patch[p, 0, j, rows, :] = o_re
                    patch[p, 1, j, rows, :] = o_im
                    v = jnp.where(used, o_re * o_re + o_im * o_im, 0.0).reshape(2, 8, LANES)
                    vpart[it][rr // 8 : rr // 8 + 2, j] += v
            return 0

        lax.fori_loop(0, SLOTS, body, 0)

    def order_amplitudes(p, _):
        rest = amp[p]
        total_of = None
        for _ in range(3):
            bits = rest.astype(jnp.bfloat16)
            rest = rest - bits.astype(jnp.float32)
            rows = jnp.dot(tab[4], bits, preferred_element_type=jnp.float32).astype(jnp.bfloat16)
            moved = jnp.dot(rows, tab[5], preferred_element_type=jnp.float32)
            total_of = moved if total_of is None else total_of + moved
        amp[p] = total_of
        return 0

    def position(it, p):
        pr = prb[it]
        ahead, late = placing(p)
        used = alive(p)
        f32, bf16 = jnp.float32, jnp.bfloat16
        halves = range(2)

        def lanes(first, j):
            return slice(first + j * LANES, first + (j + 1) * LANES)

        for rr in range(0, HALF, STEP):
            for j in halves:
                for m in halves:
                    both = []
                    for e in halves:
                        rows = slice(e * HALF + rr, e * HALF + rr + STEP)
                        o_re, o_im = patch[p, 0, j, rows, :], patch[p, 1, j, rows, :]
                        p_re, p_im = pr[2 * m, rows, lanes(0, j)], pr[2 * m + 1, rows, lanes(0, j)]
                        both.append((p_re * o_re - p_im * o_im, p_re * o_im + p_im * o_re))
                    for c in halves:
                        rows = slice(c * HALF + rr, c * HALF + rr + STEP)
                        wave[0, rows, lanes(m * N, j)] = (both[0][c] + both[1][c]).astype(bf16)
                        wave[1, rows, lanes(m * N, j)] = (both[0][c] - both[1][c]).astype(bf16)
        for e in halves:
            done[e] = jnp.dot(tab[e], wave[e], preferred_element_type=f32)
        for e in halves:
            for rr in range(0, HALF, STEP):
                for m in halves:
                    for c in halves:
                        rows = slice(c * HALF + rr, c * HALF + rr + STEP)
                        a, b = done[e, rows, lanes(m * N, 0)], done[e, rows, lanes(m * N, 1)]
                        rows = slice(m * HALF + rr, m * HALF + rr + STEP)
                        mid[e, 0, rows, lanes(0, c)] = (a + b).astype(bf16)
                        mid[e, 1, rows, lanes(0, c)] = (a - b).astype(bf16)
            for o in halves:
                spec[e, o] = jnp.dot(mid[e, o], tab[2 + o], preferred_element_type=f32)
            for o in halves:
                for rr in range(0, HALF, STEP):
                    rows = [slice(m * HALF + rr, m * HALF + rr + STEP) for m in halves]
                    values = [[spec[e, o, rows[m], lanes(0, c)] for c in halves] for m in halves]
                    intensity = (values[0][0] ** 2 + values[0][1] ** 2) + (
                        values[1][0] ** 2 + values[1][1] ** 2
                    )
                    measured = amp[p, e * HALF + rr : e * HALF + rr + STEP, lanes(0, o)]
                    factor = measured * lax.rsqrt(jnp.maximum(intensity, INTENSITY_FLOOR)) - 1.0
                    factor = jnp.where(used, factor, 0.0)
                    for m in halves:
                        for c in halves:
                            corr[e, o, rows[m], lanes(0, c)] = (values[m][c] * factor).astype(bf16)
            for o in halves:
                undone[e, o] = jnp.dot(corr[e, o], tab[o], preferred_element_type=f32)
            for rr in range(0, HALF, STEP):
                for m in halves:
                    for c in halves:
                        rows = slice(m * HALF + rr, m * HALF + rr + STEP)
                        a, b = undone[e, 0, rows, lanes(0, c)], undone[e, 1, rows, lanes(0, c)]
                        rows = slice(c * HALF + rr, c * HALF + rr + STEP)
                        back[e, rows, lanes(m * N, 0)] = (a + b).astype(bf16)
                        back[e, rows, lanes(m * N, 1)] = (a - b).astype(bf16)
        for e in halves:
            chi[e] = jnp.dot(tab[2 + e], back[e], preferred_element_type=f32)
        for rr in range(0, HALF, STEP):
            terms = [[None, None], [None, None]]
            for j in halves:
                waves = []
                for m in halves:
                    parts = [
                        [chi[e, c * HALF + rr : c * HALF + rr + STEP, lanes(m * N, j)] for e in halves]
                        for c in halves
                    ]
                    waves.append([(a + b, a - b) for a, b in parts])
                for e in halves:
                    at = e * HALF + rr
                    rows = slice(at, at + STEP)
                    o_re, o_im = patch[p, 0, j, rows, :], patch[p, 1, j, rows, :]
                    g_re = g_im = 0.0
                    for m in halves:
                        p_re, p_im = pr[2 * m, rows, lanes(0, j)], pr[2 * m + 1, rows, lanes(0, j)]
                        b_re, b_im = waves[m][0][e], waves[m][1][e]
                        g_re += p_re * b_re + p_im * b_im
                        g_im += p_re * b_im - p_im * b_re
                        h_re = o_re * b_re + o_im * b_im
                        h_im = o_re * b_im - o_im * b_re
                        b = at // 8
                        pair = (b // (nx * ny), b // ny % nx, slice(b % ny, b % ny + 2))
                        part[it][(*pair, 4 * m + j)] += h_re.reshape(2, 8, LANES)
                        part[it][(*pair, 4 * m + 2 + j)] += h_im.reshape(2, 8, LANES)
                    terms[e][j] = g_re, g_im
            for e in halves:
                put = slice(FAR + e * HALF + rr, FAR + e * HALF + rr + STEP)
                for ch in range(2):
                    a = pltpu.roll(terms[e][0][ch], ahead, 1)
                    b = pltpu.roll(terms[e][1][ch], ahead, 1)
                    placed[p, 0, ch, put, :] = jnp.where(late, a, 0.0)
                    placed[p, 1, ch, put, :] = jnp.where(late, b, a)
                    placed[p, 2, ch, put, :] = jnp.where(late, 0.0, b)

    def update(it, lo, hi):
        for rr in range(lo, hi, 2 * STEP):
            rows = slice(rr, rr + 2 * STEP)
            scale = w_own[it][1, rows, :]
            for ch in range(2):
                grad = own[it][1, ch, rows, :] + (from_left[it][ch, rows, :] + from_right[it][ch, rows, :])
                value = field[it][1, ch, LANES + rr : LANES + rr + 2 * STEP, :] + grad * scale
                if it == 0:
                    field[1][1, ch, LANES + rr : LANES + rr + 2 * STEP, :] = value
                else:
                    own[1][1, ch, rows, :] = value
        if it == 1:
            return [write(own[1].at[1, :, lo:hi, :], out_sample.at[:, lo:hi, :])]
        return []

    def finish_probe():
        for i in range(N // 8):
            at = slice(i * 8, i * 8 + 8)
            c, xy = i // (nx * ny), i % (nx * ny)
            for j in range(2):
                cols = slice(j * LANES, (j + 1) * LANES)
                scale = 1.0 / (vfull[0][i, j] + PROBE_DAMPING)
                for q in range(4):
                    grad = full[0][c, xy // ny, xy % ny, 2 * q + j]
                    prb[1][q, at, cols] = prb[0][q, at, cols] + grad * scale

    written = []

    def write(src, dst):
        copy = pltpu.make_async_copy(src, dst, load_sem.at[len(moves) + len(written)])
        copy.start()
        written.append(copy)
        return copy

    flushed = [0]

    def flush():
        for copy in copies[flushed[0] :]:
            copy.wait_send()
        flushed[0] = len(copies)

    for load in loads:
        load.wait()
    lax.fori_loop(0, SLOTS, order_amplitudes, 0)
    rows_w = illuminate(0)
    waiting = spread(field[0], sent_up, sent_down, sent_middle, forwards)
    arrive(waiting)

    half = nx * ny
    for it in range(2):
        if it == 0:
            gather(0)
        else:
            write(prb[1], out_probe)
            rows_w = illuminate(1)

        mine = vfull[it].at[(core * nx + x) * ny + y]
        v_core = remote(vpart[it].at[pl.ds((1 - core) * half, half)], vrc[it], partner)
        v_x = [remote(vhs[it].at[pl.ds(xs[k] * ny, ny)], vrx[it].at[k - 1], on_x[k]) for k in range(1, nx)]
        v_y = [remote(vhx[it].at[ys[k]], vry[it].at[k - 1], on_y[k]) for k in range(1, ny)]
        v_z = [remote(vz[it].at[z], vz[it].at[z], on_z[k]) for k in range(1, nz)]
        v_back_y = [remote(mine, mine, on_y[k]) for k in range(1, ny)]
        row = vfull[it].at[pl.ds((core * nx + x) * ny, ny)]
        v_back_x = [remote(row, row, on_x[k]) for k in range(1, nx)]
        whole = vfull[it].at[pl.ds(core * half, half)]
        v_back_core = remote(whole, whole, partner)
        w_sides = [
            remote(w_own[it].at[0], w_right[it], left),
            remote(w_own[it].at[2], w_left[it], right),
        ]
        v_core.start()

        def weight_core(it=it, v_core=v_core, v_x=v_x):
            v_core.wait_recv()
            vhs[it][...] = vpart[it][pl.ds(core * half, half)] + vrc[it][...]
            start(v_x)

        def weight_x(it=it, v_x=v_x, v_y=v_y):
            arrive(v_x)
            value = vhs[it][pl.ds(x * ny, ny)]
            for k in range(nx - 1):
                value += vrx[it][k]
            vhx[it][...] = value
            start(v_y)

        def light_sides(it=it, rows_w=rows_w, w_sides=w_sides):
            arrive(rows_w)
            for t in range(3):
                w_own[it][t, 0:LANES, :] += w_from_up[it][t]
                w_own[it][t, BAND - LANES : BAND, :] += w_from_dn[it][t]
            start(w_sides)

        def weight_y(it=it, v_y=v_y, v_z=v_z):
            arrive(v_y)
            value = vhx[it][y]
            for k in range(ny - 1):
                value += vry[it][k]
            vz[it][z] = value
            start(v_z)

        def visit(p, _, it=it, hooks=(weight_core, weight_x, light_sides, weight_y)):
            for n, hook in zip((1, 2, 2, 3), hooks, strict=True):
                pl.when(p == n)(hook)
            position(it, p)
            return 0

        lax.fori_loop(0, SLOTS, visit, 0)

        sums, mates = part[it], rc[it]
        order = (2, 1, 3, 0)
        swap = [send(sums.at[1 - core, :, ys[k]], mates.at[:, ys[k]], partner) for k in order]
        planes = [slice(4 * h, 4 * h + 4) for h in range(2)]

        total(grads, halo_up[it], 0, 0, LANES)
        rows_up = send(halo_up[it], from_dn[it], above)
        total(grads, halo_dn[it], LANES + BAND, 0, LANES)
        rows_down = send(halo_dn[it], from_up[it], below)

        def sum_core(n, it=it, swap=swap):
            swap[n].wait_recv()
            at = ys[order[n]]
            hs[it][:, at] = part[it][core, :, at] + rc[it][:, at]

        def send_sides(lo, hi, it=it):
            return [
                send(own[it].at[0, :, lo:hi, :], from_right[it].at[:, lo:hi, :], left),
                send(own[it].at[2, :, lo:hi, :], from_left[it].at[:, lo:hi, :], right),
            ]

        total(grads, own[it], LANES, *MIDDLE)
        side_middle = send_sides(*MIDDLE)

        sum_core(0)
        far = [
            [
                send(hs[it].at[0:2, ys[2], p], r1[it].at[0, h], on_y[1]),
                send(hs[it].at[2:4, ys[2], p], r1[it].at[1, h], on_y[3]),
            ]
            for h, p in enumerate(planes)
        ]

        sum_core(1)
        sum_core(2)
        near = []
        for h, p in enumerate(planes):
            arrive(far[h])
            hs[it][0:2, ys[1], p] += r1[it][0, h]
            hs[it][2:4, ys[3], p] += r1[it][1, h]
            near.append(
                [
                    send(hs[it].at[:, ys[1], p], r2[it].at[0, h], on_y[1]),
                    send(hs[it].at[:, ys[3], p], r2[it].at[1, h], on_y[3]),
                ]
            )
        sum_core(3)

        total(grads, own[it], LANES, *UP)
        total(grads, own[it], LANES, *DOWN)

        def add_rows(src, lo, it=it):
            for t in range(3):
                for ch in range(2):
                    own[it][t, ch, lo : lo + LANES, :] += src[t, ch]

        rows_down.wait_recv()
        add_rows(from_up[it], UP[0])
        side_up = send_sides(*UP)
        rows_up.wait_recv()
        add_rows(from_dn[it], DOWN[0])
        side_down = send_sides(*DOWN)

        to_x = []
        for h, p in enumerate(planes):
            arrive(near[h])
            hy[it][h] = hs[it][:, y, p] + (r2[it][0, h] + r2[it][1, h])
            to_x.append([send(hy[it].at[h, xs[k]], rx[it].at[h, k - 1], on_x[k]) for k in range(1, nx)])

        arrive(v_z)
        value = vz[it][0]
        for k in range(1, nz):
            value += vz[it][k]
        vfull[it][(core * nx + x) * ny + y] = value
        start(v_back_y)

        arrive(w_sides)
        lit = w_own[it][1] + (w_left[it][...] + w_right[it][...])
        w_own[it][1] = 1.0 / (lit + SAMPLE_DAMPING)

        for h, p in enumerate(planes):
            arrive(to_x[h])
            value = hy[it][h, x]
            for k in range(nx - 1):
                value += rx[it][h, k]
            zb[it][p] = value
        to_z = [send(zb[it].at[zs[k]], rz[it].at[k - 1], on_z[k]) for k in range(1, nz)]

        arrive(v_back_y)
        start(v_back_x)

        arrive(side_middle)
        update(it, *MIDDLE)

        arrive(to_z)
        value = zb[it][z]
        for k in range(nz - 1):
            value += rz[it][k]
        zg[it][z] = value
        back_z = [send(zg[it].at[z], zg[it].at[z], on_z[k]) for k in range(1, nz)]

        arrive(side_up)
        update(it, *UP)
        if it == 0:

            def updated(lo, hi):
                return field[1].at[1, :, LANES + lo : LANES + hi, :]

            sent_up = send_columns(field[1], updated, *UP)
            forwards = [forward_up(field[1], 1)]

        arrive(back_z)
        result = full[it]
        result[core, x, y] = zg[it][...]
        mine = [result.at[core, x, y, p] for p in planes]
        back_x = [[send(m, m, on_x[k]) for k in range(1, nx)] for m in mine]
        arrive(v_back_x)
        v_back_core.start()
        if it == 1:
            flush()

        arrive(side_down)
        update(it, *DOWN)
        if it == 0:
            sent_down = send_columns(field[1], updated, *DOWN)
            forwards.append(forward_down(field[1], 1))
            sent_middle = send_columns(field[1], updated, *MIDDLE)

        def to_core(k, result=result):
            piece = result.at[core, :, ys[k]]
            return send(piece, piece, partner)

        back_near = []
        for h, p in enumerate(planes):
            arrive(back_x[h])
            mine = result.at[core, :, y, p]
            back_near.append([send(mine, mine, on_y[k]) for k in (1, 3)])
        back_core = [to_core(0)]
        back_far = []
        for h, p in enumerate(planes):
            arrive(back_near[h])
            low, high = result.at[core, 0:2, ys[3], p], result.at[core, 2:4, ys[1], p]
            back_far.append([send(low, low, on_y[1]), send(high, high, on_y[3])])
        back_core += [to_core(1), to_core(3)]
        if it == 0:
            waiting = spread(field[1], sent_up, sent_down, sent_middle, forwards)
        for h in range(2):
            arrive(back_far[h])
        back_core.append(to_core(2))
        v_back_core.wait_recv()
        if it == 0:
            arrive(waiting)
            gather(1)
            arrive(back_core)
            finish_probe()
        else:
            write(vfull[1], out_weight)
            flush()
            arrive(back_core)
            write(full[1], out_sums)

    for copy in written:
        copy.wait()


def finish(scale, sample, probe, sums, weight, new_sample, new_probe, probe_gradient):
    new_sample[...] = sample[...]
    for b in range(sums.shape[0]):
        rows = slice(8 * b, 8 * b + 8)
        for j in range(2):
            cols = slice(j * LANES, (j + 1) * LANES)
            damped = 1.0 / (weight[b, j] + PROBE_DAMPING)
            for q in range(4):
                grad = sums[b, 2 * q + j]
                new_probe[q // 2, q % 2, rows, cols] = probe[q, rows, cols] + grad * damped
                probe_gradient[q // 2, q % 2, rows, cols] = grad * scale


def solution(mesh):
    ng, nd = mesh.shape["grp"], mesh.shape["dev"]
    ny = ng // 2
    nz = nd // 4
    nx = nd // nz
    blocks = 2 * nx * ny
    table = tables()

    def vmem(*shape, dtype=jnp.float32):
        return pltpu.VMEM(shape, dtype)

    def two(*shape):
        return [vmem(*shape)] * 2

    def local(sample, probe, amps, rows_at, cols_at, live):
        hbm = pl.BlockSpec(memory_space=pl.ANY)
        smem = pl.BlockSpec(memory_space=pltpu.SMEM)
        f32 = jnp.float32
        raw_sample, raw_probe, sums, weight = pl.pallas_call(
            functools.partial(kernel, (nx, ny, nz)),
            out_shape=[
                jax.ShapeDtypeStruct((2, BAND, LANES), f32),
                jax.ShapeDtypeStruct((4, N, N), f32),
                jax.ShapeDtypeStruct((2, nx, ny, 8, 8, LANES), f32),
                jax.ShapeDtypeStruct((blocks, 2, 8, LANES), f32),
            ],
            in_specs=[hbm] * 4 + [smem] * 3,
            out_specs=[hbm] * 4,
            scratch_shapes=[
                *two(3, 2, EXT, LANES),
                *two(4, N, N),
                vmem(SLOTS, N, N),
                vmem(6, N, N, dtype=jnp.bfloat16),
                vmem(SLOTS, 2, 2, N, LANES),
                *[vmem(2, N, 2 * N, dtype=jnp.bfloat16)] * 2,
                *[vmem(2, 2, N, N, dtype=jnp.bfloat16)] * 2,
                vmem(2, N, 2 * N),
                *[vmem(2, 2, N, N)] * 2,
                vmem(2, N, 2 * N),
                vmem(2, N, LANES),
                vmem(SLOTS, 3, 2, 2 * FAR + N, LANES),
                *two(3, 2, LANES, LANES),
                *two(3, 2, LANES, LANES),
                *two(3, 2, BAND, LANES),
                *two(3, 2, LANES, LANES),
                *two(3, 2, LANES, LANES),
                *two(2, BAND, LANES),
                *two(2, BAND, LANES),
                *two(3, LANES, LANES),
                *two(3, LANES, LANES),
                *two(3, BAND, LANES),
                *two(3, LANES, LANES),
                *two(3, LANES, LANES),
                *two(BAND, LANES),
                *two(BAND, LANES),
                *two(2, nx, ny, 8, 8, LANES),
                *two(nx, ny, 8, 8, LANES),
                *two(nx, ny, 8, 8, LANES),
                *two(2, 2, nx // 2, 4, 8, LANES),
                *two(2, 2, nx, 4, 8, LANES),
                *two(2, nx, 4, 8, LANES),
                *two(2, nx - 1, 4, 8, LANES),
                *two(8, 8, LANES),
                *two(nz - 1, 8, LANES),
                *two(8, 8, LANES),
                *two(2, nx, ny, 8, 8, LANES),
                *two(blocks, 2, 8, LANES),
                *two(blocks // 2, 2, 8, LANES),
                *two(blocks // 2, 2, 8, LANES),
                *two(nx - 1, ny, 2, 8, LANES),
                *two(ny, 2, 8, LANES),
                *two(ny - 1, 2, 8, LANES),
                *two(nz, 2, 8, LANES),
                *two(blocks, 2, 8, LANES),
                pltpu.SemaphoreType.DMA((10,)),
                pltpu.SemaphoreType.DMA((COPIES,)),
                pltpu.SemaphoreType.DMA((COPIES,)),
            ],
            compiler_params=pltpu.CompilerParams(
                collective_id=0, has_side_effects=True, vmem_limit_bytes=60 * 1024 * 1024
            ),
            cost_estimate=pl.CostEstimate(
                flops=2 * 4 * 4 * 2 * 512**3, bytes_accessed=6 << 20, transcendentals=8 * N * N
            ),
        )(sample, probe.reshape(4, N, N), amps, table, rows_at, cols_at, live)
        steps = 4
        some, rows = blocks // steps, N // steps
        tile = pl.BlockSpec((2, BAND // steps, LANES), lambda i: (0, i, 0))
        modes = pl.BlockSpec((2, 2, rows, N), lambda i: (0, 0, i, 0))
        return pl.pallas_call(
            functools.partial(finish, 1.0 / math.sqrt(SLOTS * ng * nd)),
            grid=(steps,),
            out_shape=[
                jax.ShapeDtypeStruct((2, BAND, LANES), f32),
                jax.ShapeDtypeStruct((2, 2, N, N), f32),
                jax.ShapeDtypeStruct((2, 2, N, N), f32),
            ],
            in_specs=[
                tile,
                pl.BlockSpec((4, rows, N), lambda i: (0, i, 0)),
                pl.BlockSpec((some, 8, 8, LANES), lambda i: (i, 0, 0, 0)),
                pl.BlockSpec((some, 2, 8, LANES), lambda i: (i, 0, 0, 0)),
            ],
            out_specs=[tile, modes, modes],
            compiler_params=pltpu.CompilerParams(vmem_limit_bytes=60 * 1024 * 1024),
            cost_estimate=pl.CostEstimate(flops=16 * N * N, bytes_accessed=6 << 20, transcendentals=0),
        )(raw_sample, raw_probe, sums.reshape(blocks, 8, 8, LANES), weight)

    return jax.shard_map(
        local,
        mesh=mesh,
        in_specs=(
            P(None, "grp", "dev"),
            P(),
            P(("grp", "dev"), None, None),
            P(("grp", "dev")),
            P(("grp", "dev")),
            P(("grp", "dev")),
        ),
        out_specs=(P(None, "grp", "dev"), P(), P()),
        check_vma=False,
    )
```

```python
import functools
import math

import jax
import jax.numpy as jnp
import ml_dtypes
import numpy as np
from jax import lax
from jax.experimental import pallas as pl
from jax.experimental.pallas import tpu as pltpu
from jax.sharding import PartitionSpec as P

INTENSITY_FLOOR = 0.25
SAMPLE_DAMPING = 0.5
PROBE_DAMPING = 1.0
MESH = pl.DeviceIdType.MESH
LANES = 128
N = 256
HALF = 128
BAND = 512
EXT = BAND + 2 * LANES
FAR = 512
STEP = 16
SLOTS = 4
COPIES = 192
UP, MIDDLE, DOWN = (0, 128), (128, 384), (384, 512)


def tables():
    k = np.arange(N)
    angles = (np.outer(k, k) % N).astype(np.float32) * np.float32(2.0 * math.pi / N)
    c = (np.cos(angles) / np.float32(16.0)).astype(ml_dtypes.bfloat16)
    s = (np.sin(angles) / np.float32(16.0)).astype(ml_dtypes.bfloat16)
    split = [np.block([[c[e::2, :HALF], s[e::2, :HALF]], [-s[e::2, :HALF], c[e::2, :HALF]]]) for e in range(2)]
    order = np.eye(N)[np.concatenate([k[0::2], k[1::2]])].astype(ml_dtypes.bfloat16)
    return np.stack([*split, split[0].T, split[1].T, order, order.T])


def kernel(shape, *refs):
    sample, probe, amps, table, rows_at, cols_at, live = refs[:7]
    out_sample, out_probe, out_sums = refs[7:10]
    scratch = iter(refs[10:])

    def two():
        return next(scratch), next(scratch)

    nx, ny, nz = shape
    field, prb = two(), two()
    amp, tab, patch, wave, back, mid, corr, done, spec, undone, chi, light, placed = (
        next(scratch) for _ in range(13)
    )
    halo_up, halo_dn, own, from_up, from_dn, from_left, from_right = (two() for _ in range(7))
    w_all, w_left, w_right, w_from_up, w_from_dn = (two() for _ in range(5))
    part, rc, hs, rxy, zb, rz, rv, zg, full = (two() for _ in range(9))
    load_sem, send_sem, recv_sem = scratch

    g, d = lax.axis_index("grp"), lax.axis_index("dev")
    ng, nd = 2 * ny, nx * nz
    y, core = g // 2, g % 2
    x, z = d // nz, d % nz
    above = {"grp": (g + ng - 1) % ng, "dev": d}
    below = {"grp": (g + 1) % ng, "dev": d}
    left = {"grp": g, "dev": (d + nd - 1) % nd}
    right = {"grp": g, "dev": (d + 1) % nd}
    partner = {"grp": y * 2 + 1 - core, "dev": d}
    xs = [(x + k) % nx for k in range(nx)]
    ys = [(y + k) % ny for k in range(ny)]
    zs = [(z + k) % nz for k in range(nz)]
    on_xy = [[{"grp": v * 2 + core, "dev": u * nz + z} for v in ys] for u in xs]
    on_z = [{"grp": g, "dev": x * nz + v} for v in zs]

    copies = []

    def remote(src, dst, to):
        n = len(copies)
        copy = pltpu.make_async_remote_copy(
            src_ref=src, dst_ref=dst, send_sem=send_sem.at[n], recv_sem=recv_sem.at[n],
            device_id=to, device_id_type=MESH,
        )
        copies.append(copy)
        return copy

    def start(group):
        for copy in group:
            copy.start()
        return group

    def send(src, dst, to):
        return start([remote(src, dst, to)])[0]

    def arrive(group):
        for copy in group:
            copy.wait_recv()

    moves = [(sample, field[0].at[1, :, LANES : LANES + BAND, :]), (probe, prb[0]), (table, tab), (amps, amp)]
    loads = [pltpu.make_async_copy(src, dst, load_sem.at[n]) for n, (src, dst) in enumerate(moves)]
    for load in loads:
        load.start()

    barrier = pltpu.get_barrier_semaphore()
    peers = [above, below, left, right, partner] + on_z[1:]
    peers += [on_xy[i][j] for i in range(nx) for j in range(ny) if i or j]
    for peer in peers:
        pl.semaphore_signal(barrier, inc=1, device_id=peer, device_id_type=MESH)
    pl.semaphore_wait(barrier, len(peers))

    row_anchor = g * BAND - LANES
    col_anchor = d * LANES - LANES
    starts = [jnp.clip(rows_at[p] - row_anchor, 0, FAR) for p in range(SLOTS)]

    def alive(p):
        return jnp.full((STEP, LANES), p, jnp.int32) < jnp.full((STEP, LANES), live[0], jnp.int32)

    def send_columns(f, source, lo, hi):
        src = source(lo, hi)
        return [
            send(src, f.at[0, :, LANES + lo : LANES + hi, :], right),
            send(src, f.at[2, :, LANES + lo : LANES + hi, :], left),
        ]

    def forward_up(f, t, src=None):
        src = f.at[t, :, LANES : 2 * LANES, :] if src is None else src
        return send(src, f.at[t, :, LANES + BAND : EXT, :], above)

    def forward_down(f, t, src=None):
        src = f.at[t, :, BAND : LANES + BAND, :] if src is None else src
        return send(src, f.at[t, :, 0:LANES, :], below)

    def spread(f, sent_up, sent_down, sent_middle, forwards):
        arrive(sent_up)
        forwards += [forward_up(f, 0), forward_up(f, 2)]
        arrive(sent_down)
        forwards += [forward_down(f, 0), forward_down(f, 2)]
        return sent_middle + forwards

    def argument(lo, hi):
        return sample.at[:, lo:hi, :]

    sent_up = send_columns(field[0], argument, *UP)
    sent_down = send_columns(field[0], argument, *DOWN)
    forwards = [forward_up(field[0], 1, argument(*UP)), forward_down(field[0], 1, argument(*DOWN))]
    sent_middle = send_columns(field[0], argument, *MIDDLE)

    def clear(i, _):
        zero = jnp.zeros((STEP, LANES), jnp.float32)
        rr = pl.multiple_of(i * STEP, STEP)
        for p in range(SLOTS):
            for t in range(3):
                for at in (rr, FAR + N + rr):
                    for ch in range(2):
                        placed[p, t, ch, pl.ds(at, STEP), :] = zero
        return 0

    lax.fori_loop(0, FAR // STEP, clear, 0)
    for it in range(2):
        part[it][...] = jnp.zeros(part[it].shape, jnp.float32)

    def placing(p):
        s = jnp.clip(cols_at[p] - col_anchor, 0, LANES)
        lane = lax.broadcasted_iota(jnp.int32, (STEP, LANES), 1)
        return s % LANES, lane >= s

    def total(sources, dst, first, lo, hi):
        def body(i, _):
            rr = pl.multiple_of(lo + i * 2 * STEP, 2 * STEP)
            for src, index in sources:
                values = [
                    placed[(p, *src, pl.ds(FAR + first + rr - starts[p], 2 * STEP), slice(None))]
                    for p in range(SLOTS)
                ]
                dst[(*index, pl.ds(rr, 2 * STEP), slice(None))] = (values[0] + values[1]) + (
                    values[2] + values[3]
                )
            return 0

        lax.fori_loop(0, (hi - lo) // (2 * STEP), body, 0)

    grads = [((t, ch), (t, ch)) for t in range(3) for ch in range(2)]
    lights = [((t, 0), (t,)) for t in range(3)]

    def illuminate(it):
        for j in range(2):
            cols = slice(j * LANES, (j + 1) * LANES)
            value = prb[it][0, :, cols] ** 2 + prb[it][1, :, cols] ** 2
            light[j] = value + (prb[it][2, :, cols] ** 2 + prb[it][3, :, cols] ** 2)

        def place(p, _):
            ahead, late = placing(p)
            used = alive(p)
            for rr in range(0, N, STEP):
                a, b = (
                    pltpu.roll(jnp.where(used, light[j, rr : rr + STEP, :], 0.0), ahead, 1) for j in range(2)
                )
                at = slice(FAR + rr, FAR + rr + STEP)
                placed[p, 0, 0, at, :] = jnp.where(late, a, 0.0)
                placed[p, 1, 0, at, :] = jnp.where(late, b, a)
                placed[p, 2, 0, at, :] = jnp.where(late, 0.0, b)
            return 0

        lax.fori_loop(0, SLOTS, place, 0)
        total(lights, w_all[it], 0, 0, EXT)

    def pair_at(row):
        b = row // 8
        return b // (nx * ny), b // ny % nx, slice(b % ny, b % ny + 2)

    def gather(it):
        f = field[it]

        def body(p, _):
            r0 = jnp.clip(rows_at[p] - row_anchor, 0, FAR)
            s = jnp.clip(cols_at[p] - col_anchor, 0, LANES)
            behind = (LANES - s) % LANES
            early = lax.broadcasted_iota(jnp.int32, (STEP, LANES), 1) < LANES - s
            used = alive(p)
            for rr in range(0, N, STEP):
                rows = slice(rr, rr + STEP)
                halves = []
                for ch in range(2):
                    a, b, c = (pltpu.roll(f[t, ch, pl.ds(r0 + rr, STEP), :], behind, 1) for t in range(3))
                    halves.append((jnp.where(early, a, b), jnp.where(early, b, c)))
                for j in range(2):
                    o_re, o_im = halves[0][j], halves[1][j]
                    patch[p, 0, j, rows, :] = o_re
                    patch[p, 1, j, rows, :] = o_im
                    v = jnp.where(used, o_re * o_re + o_im * o_im, 0.0).reshape(2, 8, LANES)
                    part[it][(*pair_at(rr), 8 + j)] += v
            return 0

        lax.fori_loop(0, SLOTS, body, 0)

    def order_amplitudes(p, _):
        rest = amp[p]
        total_of = None
        for _ in range(3):
            bits = rest.astype(jnp.bfloat16)
            rest = rest - bits.astype(jnp.float32)
            rows = jnp.dot(tab[4], bits, preferred_element_type=jnp.float32).astype(jnp.bfloat16)
            moved = jnp.dot(rows, tab[5], preferred_element_type=jnp.float32)
            total_of = moved if total_of is None else total_of + moved
        amp[p] = total_of
        return 0

    def position(it, p):
        pr = prb[it]
        ahead, late = placing(p)
        used = alive(p)
        f32, bf16 = jnp.float32, jnp.bfloat16
        halves = range(2)

        def lanes(first, j):
            return slice(first + j * LANES, first + (j + 1) * LANES)

        for rr in range(0, HALF, STEP):
            for j in halves:
                for m in halves:
                    both = []
                    for e in halves:
                        rows = slice(e * HALF + rr, e * HALF + rr + STEP)
                        o_re, o_im = patch[p, 0, j, rows, :], patch[p, 1, j, rows, :]
                        p_re, p_im = pr[2 * m, rows, lanes(0, j)], pr[2 * m + 1, rows, lanes(0, j)]
                        both.append((p_re * o_re - p_im * o_im, p_re * o_im + p_im * o_re))
                    for c in halves:
                        rows = slice(c * HALF + rr, c * HALF + rr + STEP)
                        wave[0, rows, lanes(m * N, j)] = (both[0][c] + both[1][c]).astype(bf16)
                        wave[1, rows, lanes(m * N, j)] = (both[0][c] - both[1][c]).astype(bf16)
        for e in halves:
            done[e] = jnp.dot(tab[e], wave[e], preferred_element_type=f32)
        for e in halves:
            for rr in range(0, HALF, STEP):
                for m in halves:
                    for c in halves:
                        rows = slice(c * HALF + rr, c * HALF + rr + STEP)
                        a, b = done[e, rows, lanes(m * N, 0)], done[e, rows, lanes(m * N, 1)]
                        rows = slice(m * HALF + rr, m * HALF + rr + STEP)
                        mid[e, 0, rows, lanes(0, c)] = (a + b).astype(bf16)
                        mid[e, 1, rows, lanes(0, c)] = (a - b).astype(bf16)
            for o in halves:
                spec[e, o] = jnp.dot(mid[e, o], tab[2 + o], preferred_element_type=f32)
            for o in halves:
                for rr in range(0, HALF, STEP):
                    rows = [slice(m * HALF + rr, m * HALF + rr + STEP) for m in halves]
                    values = [[spec[e, o, rows[m], lanes(0, c)] for c in halves] for m in halves]
                    intensity = (values[0][0] ** 2 + values[0][1] ** 2) + (
                        values[1][0] ** 2 + values[1][1] ** 2
                    )
                    measured = amp[p, e * HALF + rr : e * HALF + rr + STEP, lanes(0, o)]
                    factor = measured * lax.rsqrt(jnp.maximum(intensity, INTENSITY_FLOOR)) - 1.0
                    factor = jnp.where(used, factor, 0.0)
                    for m in halves:
                        for c in halves:
                            corr[e, o, rows[m], lanes(0, c)] = (values[m][c] * factor).astype(bf16)
            for o in halves:
                undone[e, o] = jnp.dot(corr[e, o], tab[o], preferred_element_type=f32)
            for rr in range(0, HALF, STEP):
                for m in halves:
                    for c in halves:
                        rows = slice(m * HALF + rr, m * HALF + rr + STEP)
                        a, b = undone[e, 0, rows, lanes(0, c)], undone[e, 1, rows, lanes(0, c)]
                        rows = slice(c * HALF + rr, c * HALF + rr + STEP)
                        back[e, rows, lanes(m * N, 0)] = (a + b).astype(bf16)
                        back[e, rows, lanes(m * N, 1)] = (a - b).astype(bf16)
        for e in halves:
            chi[e] = jnp.dot(tab[2 + e], back[e], preferred_element_type=f32)
        for rr in range(0, HALF, STEP):
            terms = [[None, None], [None, None]]
            for j in halves:
                waves = []
                for m in halves:
                    parts = [
                        [chi[e, c * HALF + rr : c * HALF + rr + STEP, lanes(m * N, j)] for e in halves]
                        for c in halves
                    ]
                    waves.append([(a + b, a - b) for a, b in parts])
                for e in halves:
                    at = e * HALF + rr
                    rows = slice(at, at + STEP)
                    o_re, o_im = patch[p, 0, j, rows, :], patch[p, 1, j, rows, :]
                    g_re = g_im = 0.0
                    for m in halves:
                        p_re, p_im = pr[2 * m, rows, lanes(0, j)], pr[2 * m + 1, rows, lanes(0, j)]
                        b_re, b_im = waves[m][0][e], waves[m][1][e]
                        g_re += p_re * b_re + p_im * b_im
                        g_im += p_re * b_im - p_im * b_re
                        h_re = o_re * b_re + o_im * b_im
                        h_im = o_re * b_im - o_im * b_re
                        pair = pair_at(at)
                        part[it][(*pair, 4 * m + j)] += h_re.reshape(2, 8, LANES)
                        part[it][(*pair, 4 * m + 2 + j)] += h_im.reshape(2, 8, LANES)
                    terms[e][j] = g_re, g_im
            for e in halves:
                put = slice(FAR + e * HALF + rr, FAR + e * HALF + rr + STEP)
                for ch in range(2):
                    a = pltpu.roll(terms[e][0][ch], ahead, 1)
                    b = pltpu.roll(terms[e][1][ch], ahead, 1)
                    placed[p, 0, ch, put, :] = jnp.where(late, a, 0.0)
                    placed[p, 1, ch, put, :] = jnp.where(late, b, a)
                    placed[p, 2, ch, put, :] = jnp.where(late, 0.0, b)

    def update(it, lo, hi):
        for rr in range(lo, hi, 2 * STEP):
            rows = slice(rr, rr + 2 * STEP)
            scale = w_all[it][1, LANES + rr : LANES + rr + 2 * STEP, :]
            for ch in range(2):
                grad = own[it][1, ch, rows, :] + (from_left[it][ch, rows, :] + from_right[it][ch, rows, :])
                value = field[it][1, ch, LANES + rr : LANES + rr + 2 * STEP, :] + grad * scale
                if it == 0:
                    field[1][1, ch, LANES + rr : LANES + rr + 2 * STEP, :] = value
                else:
                    own[1][1, ch, rows, :] = value
        if it == 1:
            return [write(own[1].at[1, :, lo:hi, :], out_sample.at[:, lo:hi, :])]
        return []

    def finish_probe():
        for i in range(N // 8):
            at = slice(i * 8, i * 8 + 8)
            c, xy = i // (nx * ny), i % (nx * ny)
            for j in range(2):
                cols = slice(j * LANES, (j + 1) * LANES)
                scale = 1.0 / (full[0][c, xy // ny, xy % ny, 8 + j] + PROBE_DAMPING)
                for q in range(4):
                    grad = full[0][c, xy // ny, xy % ny, 2 * q + j]
                    prb[1][q, at, cols] = prb[0][q, at, cols] + grad * scale

    written = []

    def write(src, dst):
        copy = pltpu.make_async_copy(src, dst, load_sem.at[len(moves) + len(written)])
        copy.start()
        written.append(copy)
        return copy

    flushed = [0]

    def flush():
        for copy in copies[flushed[0] :]:
            copy.wait_send()
        flushed[0] = len(copies)

    for load in loads:
        load.wait()
    lax.fori_loop(0, SLOTS, order_amplitudes, 0)
    illuminate(0)
    waiting = spread(field[0], sent_up, sent_down, sent_middle, forwards)
    arrive(waiting)

    half = nx * ny
    for it in range(2):
        if it == 0:
            gather(0)
        else:
            write(prb[1], out_probe)
            illuminate(1)

        sides_w = [
            send(w_all[it].at[0], w_right[it], left),
            send(w_all[it].at[2], w_left[it], right),
        ]
        lax.fori_loop(0, SLOTS, lambda p, _, it=it: (position(it, p), 0)[1], 0)

        order = (2, 1, 3, 0)
        swap = [send(part[it].at[1 - core, xs[i]], rc[it].at[xs[i]], partner) for i in order]

        total(grads, halo_up[it], 0, 0, LANES)
        rows_up = send(halo_up[it], from_dn[it], above)
        total(grads, halo_dn[it], LANES + BAND, 0, LANES)
        rows_down = send(halo_dn[it], from_up[it], below)

        def send_sides(lo, hi, it=it):
            return [
                send(own[it].at[0, :, lo:hi, :], from_right[it].at[:, lo:hi, :], left),
                send(own[it].at[2, :, lo:hi, :], from_left[it].at[:, lo:hi, :], right),
            ]

        total(grads, own[it], LANES, *MIDDLE)
        side_middle = send_sides(*MIDDLE)

        to_plane = []
        for n, i in enumerate(order):
            swap[n].wait_recv()
            at = xs[i]
            hs[it][at] = part[it][core, at] + rc[it][at]
            for j in (2, 1, 3, 0):
                if i or j:
                    to_plane.append(send(hs[it].at[at, ys[j]], rxy[it].at[i * ny + j - 1], on_xy[i][j]))

        total(grads, own[it], LANES, *UP)
        total(grads, own[it], LANES, *DOWN)

        arrive(sides_w)
        w_all[it][1] += w_left[it][...] + w_right[it][...]
        rows_w = [
            send(w_all[it].at[1, 0:LANES, :], w_from_dn[it], above),
            send(w_all[it].at[1, LANES + BAND : EXT, :], w_from_up[it], below),
        ]

        def add_rows(src, lo, it=it):
            for t in range(3):
                for ch in range(2):
                    own[it][t, ch, lo : lo + LANES, :] += src[t, ch]

        rows_down.wait_recv()
        add_rows(from_up[it], UP[0])
        side_up = send_sides(*UP)
        rows_up.wait_recv()
        add_rows(from_dn[it], DOWN[0])
        side_down = send_sides(*DOWN)

        arrive(to_plane)
        value = hs[it][x, y]
        for k in range(nx * ny - 1):
            value += rxy[it][k]
        zb[it][0:8] = value[0:8]
        rv[it][z] = value[8:10]
        to_z = [send(zb[it].at[zs[k]], rz[it].at[k - 1], on_z[k]) for k in range(1, nz)]
        to_z += [send(rv[it].at[z], rv[it].at[z], on_z[k]) for k in range(1, nz)]

        arrive(rows_w)
        w_all[it][1, LANES : 2 * LANES, :] += w_from_up[it][...]
        w_all[it][1, BAND : LANES + BAND, :] += w_from_dn[it][...]
        w_all[it][1, LANES : LANES + BAND, :] = 1.0 / (w_all[it][1, LANES : LANES + BAND, :] + SAMPLE_DAMPING)

        arrive(side_middle)
        update(it, *MIDDLE)

        arrive(to_z)
        value = zb[it][z]
        for k in range(nz - 1):
            value += rz[it][k]
        zg[it][z] = value
        back_z = [send(zg[it].at[z], zg[it].at[z], on_z[k]) for k in range(1, nz)]
        result = full[it]
        value = rv[it][0]
        for k in range(1, nz):
            value += rv[it][k]
        result[core, x, y, 8:10] = value

        arrive(side_up)
        update(it, *UP)
        if it == 0:

            def updated(lo, hi):
                return field[1].at[1, :, LANES + lo : LANES + hi, :]

            sent_up = send_columns(field[1], updated, *UP)
            forwards = [forward_up(field[1], 1)]

        arrive(back_z)
        result[core, x, y, 0:8] = zg[it][...]
        mine = result.at[core, x, y]
        returned = {(i, j): send(mine, mine, on_xy[i][j]) for i in order for j in order if i or j}

        arrive(side_down)
        update(it, *DOWN)
        if it == 0:
            sent_down = send_columns(field[1], updated, *DOWN)
            forwards.append(forward_down(field[1], 1))
            sent_middle = send_columns(field[1], updated, *MIDDLE)
        else:
            flush()

        back_core = []
        for i in (0, 1, 3, 2):
            arrive([returned[i, j] for j in range(ny) if i or j])
            piece = result.at[core, xs[(nx - i) % nx]]
            back_core.append(send(piece, piece, partner))
        if it == 0:
            arrive(spread(field[1], sent_up, sent_down, sent_middle, forwards))
            gather(1)
            arrive(back_core)
            finish_probe()
        else:
            flush()
            arrive(back_core)
            write(full[1], out_sums)

    for copy in written:
        copy.wait()


def finish(scale, sample, probe, sums, new_sample, new_probe, probe_gradient):
    new_sample[...] = sample[...]
    for b in range(sums.shape[0]):
        rows = slice(8 * b, 8 * b + 8)
        for j in range(2):
            cols = slice(j * LANES, (j + 1) * LANES)
            damped = 1.0 / (sums[b, 8 + j] + PROBE_DAMPING)
            for q in range(4):
                grad = sums[b, 2 * q + j]
                new_probe[q // 2, q % 2, rows, cols] = probe[q, rows, cols] + grad * damped
                probe_gradient[q // 2, q % 2, rows, cols] = grad * scale


def solution(mesh):
    ng, nd = mesh.shape["grp"], mesh.shape["dev"]
    ny = ng // 2
    nz = nd // 4
    nx = nd // nz
    blocks = 2 * nx * ny
    table = tables()

    def vmem(*shape, dtype=jnp.float32):
        return pltpu.VMEM(shape, dtype)

    def two(*shape):
        return [vmem(*shape)] * 2

    def local(sample, probe, amps, rows_at, cols_at, live):
        hbm = pl.BlockSpec(memory_space=pl.ANY)
        smem = pl.BlockSpec(memory_space=pltpu.SMEM)
        f32 = jnp.float32
        raw_sample, raw_probe, sums = pl.pallas_call(
            functools.partial(kernel, (nx, ny, nz)),
            out_shape=[
                jax.ShapeDtypeStruct((2, BAND, LANES), f32),
                jax.ShapeDtypeStruct((4, N, N), f32),
                jax.ShapeDtypeStruct((2, nx, ny, 10, 8, LANES), f32),
            ],
            in_specs=[hbm] * 4 + [smem] * 3,
            out_specs=[hbm] * 3,
            scratch_shapes=[
                *two(3, 2, EXT, LANES),
                *two(4, N, N),
                vmem(SLOTS, N, N),
                vmem(6, N, N, dtype=jnp.bfloat16),
                vmem(SLOTS, 2, 2, N, LANES),
                *[vmem(2, N, 2 * N, dtype=jnp.bfloat16)] * 2,
                *[vmem(2, 2, N, N, dtype=jnp.bfloat16)] * 2,
                vmem(2, N, 2 * N),
                *[vmem(2, 2, N, N)] * 2,
                vmem(2, N, 2 * N),
                vmem(2, N, LANES),
                vmem(SLOTS, 3, 2, 2 * FAR + N, LANES),
                *two(3, 2, LANES, LANES),
                *two(3, 2, LANES, LANES),
                *two(3, 2, BAND, LANES),
                *two(3, 2, LANES, LANES),
                *two(3, 2, LANES, LANES),
                *two(2, BAND, LANES),
                *two(2, BAND, LANES),
                *two(3, EXT, LANES),
                *two(EXT, LANES),
                *two(EXT, LANES),
                *two(LANES, LANES),
                *two(LANES, LANES),
                *two(2, nx, ny, 10, 8, LANES),
                *two(nx, ny, 10, 8, LANES),
                *two(nx, ny, 10, 8, LANES),
                *two(nx * ny - 1, 10, 8, LANES),
                *two(8, 8, LANES),
                *two(nz - 1, 8, LANES),
                *two(nz, 2, 8, LANES),
                *two(8, 8, LANES),
                *two(2, nx, ny, 10, 8, LANES),
                pltpu.SemaphoreType.DMA((9,)),
                pltpu.SemaphoreType.DMA((COPIES,)),
                pltpu.SemaphoreType.DMA((COPIES,)),
            ],
            compiler_params=pltpu.CompilerParams(
                collective_id=0, has_side_effects=True, vmem_limit_bytes=60 * 1024 * 1024
            ),
            cost_estimate=pl.CostEstimate(
                flops=2 * 4 * 4 * 2 * 512**3, bytes_accessed=6 << 20, transcendentals=8 * N * N
            ),
        )(sample, probe.reshape(4, N, N), amps, table, rows_at, cols_at, live)
        steps = 4
        some, rows = blocks // steps, N // steps
        tile = pl.BlockSpec((2, BAND // steps, LANES), lambda i: (0, i, 0))
        modes = pl.BlockSpec((2, 2, rows, N), lambda i: (0, 0, i, 0))
        return pl.pallas_call(
            functools.partial(finish, 1.0 / math.sqrt(SLOTS * ng * nd)),
            grid=(steps,),
            out_shape=[
                jax.ShapeDtypeStruct((2, BAND, LANES), f32),
                jax.ShapeDtypeStruct((2, 2, N, N), f32),
                jax.ShapeDtypeStruct((2, 2, N, N), f32),
            ],
            in_specs=[
                tile,
                pl.BlockSpec((4, rows, N), lambda i: (0, i, 0)),
                pl.BlockSpec((some, 10, 8, LANES), lambda i: (i, 0, 0, 0)),
            ],
            out_specs=[tile, modes, modes],
            compiler_params=pltpu.CompilerParams(vmem_limit_bytes=60 * 1024 * 1024),
            cost_estimate=pl.CostEstimate(flops=16 * N * N, bytes_accessed=6 << 20, transcendentals=0),
        )(raw_sample, raw_probe, sums.reshape(blocks, 10, 8, LANES))

    return jax.shard_map(
        local,
        mesh=mesh,
        in_specs=(
            P(None, "grp", "dev"),
            P(),
            P(("grp", "dev"), None, None),
            P(("grp", "dev")),
            P(("grp", "dev")),
            P(("grp", "dev")),
        ),
        out_specs=(P(None, "grp", "dev"), P(), P()),
        check_vma=False,
    )
```

```python
import functools
import math

import jax
import jax.numpy as jnp
import ml_dtypes
import numpy as np
from jax import lax
from jax.experimental import pallas as pl
from jax.experimental.pallas import tpu as pltpu
from jax.sharding import PartitionSpec as P

INTENSITY_FLOOR = 0.25
SAMPLE_DAMPING = 0.5
PROBE_DAMPING = 1.0
MESH = pl.DeviceIdType.MESH
LANES = 128
N = 256
HALF = 128
BAND = 512
EXT = BAND + 2 * LANES
FAR = 512
STEP = 16
SLOTS = 4
COPIES = 192
UP, MIDDLE, DOWN = (0, 128), (128, 384), (384, 512)


def tables():
    k = np.arange(N)
    angles = (np.outer(k, k) % N).astype(np.float32) * np.float32(2.0 * math.pi / N)
    c = (np.cos(angles) / np.float32(16.0)).astype(ml_dtypes.bfloat16)
    s = (np.sin(angles) / np.float32(16.0)).astype(ml_dtypes.bfloat16)
    split = [np.block([[c[e::2, :HALF], s[e::2, :HALF]], [-s[e::2, :HALF], c[e::2, :HALF]]]) for e in range(2)]
    order = np.eye(N)[np.concatenate([k[0::2], k[1::2]])].astype(ml_dtypes.bfloat16)
    return np.stack([*split, split[0].T, split[1].T, order, order.T])


def kernel(shape, *refs):
    sample, probe, amps, table, rows_at, cols_at, live = refs[:7]
    out_sample, out_probe, out_sums, out_weight = refs[7:11]
    scratch = iter(refs[11:])

    def two():
        return next(scratch), next(scratch)

    nx, ny, nz = shape
    field, prb = two(), two()
    amp, tab, patch, wave, back, mid, corr, done, spec, undone, chi, light, placed = (
        next(scratch) for _ in range(13)
    )
    halo_up, halo_dn, own, from_up, from_dn, from_left, from_right = (two() for _ in range(7))
    told, heard, known = (next(scratch) for _ in range(3))
    w_own, w_from_up, w_from_dn = (two() for _ in range(3))
    part, rc, hs, r1, r2, hy, rx, zb, rz, zg, full = (two() for _ in range(11))
    vpart, vrc, vhs, vrx, vhx, vry, vz, vfull = (two() for _ in range(8))
    load_sem, send_sem, recv_sem = scratch

    g, d = lax.axis_index("grp"), lax.axis_index("dev")
    ng, nd = 2 * ny, nx * nz
    y, core = g // 2, g % 2
    x, z = d // nz, d % nz
    above = {"grp": (g + ng - 1) % ng, "dev": d}
    below = {"grp": (g + 1) % ng, "dev": d}
    left = {"grp": g, "dev": (d + nd - 1) % nd}
    right = {"grp": g, "dev": (d + 1) % nd}
    partner = {"grp": y * 2 + 1 - core, "dev": d}
    xs = [(x + k) % nx for k in range(nx)]
    ys = [(y + k) % ny for k in range(ny)]
    zs = [(z + k) % nz for k in range(nz)]
    on_x = [{"grp": g, "dev": v * nz + z} for v in xs]
    on_y = [{"grp": v * 2 + core, "dev": d} for v in ys]
    on_z = [{"grp": g, "dev": x * nz + v} for v in zs]

    copies = []

    def remote(src, dst, to):
        n = len(copies)
        copy = pltpu.make_async_remote_copy(
            src_ref=src, dst_ref=dst, send_sem=send_sem.at[n], recv_sem=recv_sem.at[n],
            device_id=to, device_id_type=MESH,
        )
        copies.append(copy)
        return copy

    def start(group):
        for copy in group:
            copy.start()
        return group

    def send(src, dst, to):
        return start([remote(src, dst, to)])[0]

    def arrive(group):
        for copy in group:
            copy.wait_recv()

    moves = [(sample, field[0].at[1, :, LANES : LANES + BAND, :]), (probe, prb[0]), (table, tab), (amps, amp)]
    loads = [pltpu.make_async_copy(src, dst, load_sem.at[n]) for n, (src, dst) in enumerate(moves)]
    for load in loads:
        load.start()

    barrier = pltpu.get_barrier_semaphore()
    peers = [above, below, left, right, partner] + on_x[1:] + on_y[1:] + on_z[1:]
    for peer in peers:
        pl.semaphore_signal(barrier, inc=1, device_id=peer, device_id_type=MESH)
    pl.semaphore_wait(barrier, len(peers))

    row_anchor = g * BAND - LANES
    col_anchor = d * LANES - LANES
    starts = [jnp.clip(rows_at[p] - row_anchor, 0, FAR) for p in range(SLOTS)]

    shifts = [jnp.clip(cols_at[p] - col_anchor, 0, LANES) for p in range(SLOTS)]

    def alive(p, count):
        return jnp.full((STEP, LANES), p, jnp.int32) < jnp.full((STEP, LANES), count, jnp.int32)

    place_in_row = lax.broadcasted_iota(jnp.int32, (8, LANES), 1)
    facts = jnp.zeros((8, LANES), jnp.int32)
    for n, fact in enumerate([*starts, *shifts, live[0]]):
        facts = jnp.where(place_in_row == n, fact, facts)
    told[...] = facts
    tell = [send(told, heard.at[0], right), send(told, heard.at[1], left)]

    def send_columns(f, source, lo, hi):
        src = source(lo, hi)
        return [
            send(src, f.at[0, :, LANES + lo : LANES + hi, :], right),
            send(src, f.at[2, :, LANES + lo : LANES + hi, :], left),
        ]

    def forward_up(f, t, src=None):
        src = f.at[t, :, LANES : 2 * LANES, :] if src is None else src
        return send(src, f.at[t, :, LANES + BAND : EXT, :], above)

    def forward_down(f, t, src=None):
        src = f.at[t, :, BAND : LANES + BAND, :] if src is None else src
        return send(src, f.at[t, :, 0:LANES, :], below)

    def spread(f, sent_up, sent_down, sent_middle, forwards):
        arrive(sent_up)
        forwards += [forward_up(f, 0), forward_up(f, 2)]
        arrive(sent_down)
        forwards += [forward_down(f, 0), forward_down(f, 2)]
        return sent_middle + forwards

    def argument(lo, hi):
        return sample.at[:, lo:hi, :]

    sent_up = send_columns(field[0], argument, *UP)
    sent_down = send_columns(field[0], argument, *DOWN)
    forwards = [forward_up(field[0], 1, argument(*UP)), forward_down(field[0], 1, argument(*DOWN))]
    sent_middle = send_columns(field[0], argument, *MIDDLE)

    def clear(i, _):
        zero = jnp.zeros((STEP, LANES), jnp.float32)
        rr = pl.multiple_of(i * STEP, STEP)
        for p in range(SLOTS):
            for t in range(3):
                for at in (rr, FAR + N + rr):
                    for ch in range(2):
                        placed[p, t, ch, pl.ds(at, STEP), :] = zero
        return 0

    lax.fori_loop(0, FAR // STEP, clear, 0)
    for it in range(2):
        part[it][...] = jnp.zeros(part[it].shape, jnp.float32)
        vpart[it][...] = jnp.zeros(vpart[it].shape, jnp.float32)

    def placing(p):
        s = jnp.clip(cols_at[p] - col_anchor, 0, LANES)
        lane = lax.broadcasted_iota(jnp.int32, (STEP, LANES), 1)
        return s % LANES, lane >= s

    def total(sources, dst, first, lo, hi):
        def body(i, _):
            rr = pl.multiple_of(lo + i * 2 * STEP, 2 * STEP)
            for src, index in sources:
                values = [
                    placed[(p, *src, pl.ds(FAR + first + rr - starts[p], 2 * STEP), slice(None))]
                    for p in range(SLOTS)
                ]
                dst[(*index, pl.ds(rr, 2 * STEP), slice(None))] = (values[0] + values[1]) + (
                    values[2] + values[3]
                )
            return 0

        lax.fori_loop(0, (hi - lo) // (2 * STEP), body, 0)

    grads = [((t, ch), (t, ch)) for t in range(3) for ch in range(2)]

    def illuminate(it):
        for j in range(2):
            cols = slice(j * LANES, (j + 1) * LANES)
            value = prb[it][0, :, cols] ** 2 + prb[it][1, :, cols] ** 2
            light[j] = value + (prb[it][2, :, cols] ** 2 + prb[it][3, :, cols] ** 2)

        zero = jnp.zeros((STEP, LANES), jnp.float32)
        lane = lax.broadcasted_iota(jnp.int32, (STEP, LANES), 1)

        def place(p, _):
            for t in range(3):
                shift = known[t, 0, SLOTS + p]
                late = lane >= shift
                used = alive(p, known[t, 0, 2 * SLOTS])
                for rr in range(0, N, STEP):
                    a, b = (
                        pltpu.roll(jnp.where(used, light[j, rr : rr + STEP, :], 0.0), shift % LANES, 1)
                        for j in range(2)
                    )
                    value = (jnp.where(late, zero, b), jnp.where(late, b, a), jnp.where(late, a, zero))[t]
                    placed[p, t, 0, FAR + rr : FAR + rr + STEP, :] = value
            return 0

        lax.fori_loop(0, SLOTS, place, 0)

        def body(i, _):
            rr = pl.multiple_of(i * 2 * STEP, 2 * STEP)
            values = [
                placed[p, t, 0, pl.ds(FAR + rr - known[t, 0, p], 2 * STEP), :]
                for t in range(3)
                for p in range(SLOTS)
            ]
            w_own[it][pl.ds(rr, 2 * STEP), :] = sum(values[1:], values[0])
            return 0

        lax.fori_loop(0, EXT // (2 * STEP), body, 0)
        return [
            send(w_own[it].at[0:LANES, :], w_from_dn[it], above),
            send(w_own[it].at[LANES + BAND : EXT, :], w_from_up[it], below),
        ]

    def gather(it):
        f = field[it]

        def body(p, _):
            r0 = jnp.clip(rows_at[p] - row_anchor, 0, FAR)
            s = jnp.clip(cols_at[p] - col_anchor, 0, LANES)
            behind = (LANES - s) % LANES
            early = lax.broadcasted_iota(jnp.int32, (STEP, LANES), 1) < LANES - s
            used = alive(p, live[0])
            for rr in range(0, N, STEP):
                rows = slice(rr, rr + STEP)
                halves = []
                for ch in range(2):
                    a, b, c = (pltpu.roll(f[t, ch, pl.ds(r0 + rr, STEP), :], behind, 1) for t in range(3))
                    halves.append((jnp.where(early, a, b), jnp.where(early, b, c)))
                for j in range(2):
                    o_re, o_im = halves[0][j], halves[1][j]
                    patch[p, 0, j, rows, :] = o_re
                    patch[p, 1, j, rows, :] = o_im
                    v = jnp.where(used, o_re * o_re + o_im * o_im, 0.0).reshape(2, 8, LANES)
                    vpart[it][rr // 8 : rr // 8 + 2, j] += v
            return 0

        lax.fori_loop(0, SLOTS, body, 0)

    def order_amplitudes(p, _):
        rest = amp[p]
        total_of = None
        for _ in range(3):
            bits = rest.astype(jnp.bfloat16)
            rest = rest - bits.astype(jnp.float32)
            rows = jnp.dot(tab[4], bits, preferred_element_type=jnp.float32).astype(jnp.bfloat16)
            moved = jnp.dot(rows, tab[5], preferred_element_type=jnp.float32)
            total_of = moved if total_of is None else total_of + moved
        amp[p] = total_of
        return 0

    def position(it, p):
        pr = prb[it]
        ahead, late = placing(p)
        used = alive(p, live[0])
        f32, bf16 = jnp.float32, jnp.bfloat16
        halves = range(2)

        def lanes(first, j):
            return slice(first + j * LANES, first + (j + 1) * LANES)

        for rr in range(0, HALF, STEP):
            for j in halves:
                for m in halves:
                    both = []
                    for e in halves:
                        rows = slice(e * HALF + rr, e * HALF + rr + STEP)
                        o_re, o_im = patch[p, 0, j, rows, :], patch[p, 1, j, rows, :]
                        p_re, p_im = pr[2 * m, rows, lanes(0, j)], pr[2 * m + 1, rows, lanes(0, j)]
                        both.append((p_re * o_re - p_im * o_im, p_re * o_im + p_im * o_re))
                    for c in halves:
                        rows = slice(c * HALF + rr, c * HALF + rr + STEP)
                        wave[0, rows, lanes(m * N, j)] = (both[0][c] + both[1][c]).astype(bf16)
                        wave[1, rows, lanes(m * N, j)] = (both[0][c] - both[1][c]).astype(bf16)
        for e in halves:
            done[e] = jnp.dot(tab[e], wave[e], preferred_element_type=f32)
        for e in halves:
            for rr in range(0, HALF, STEP):
                for m in halves:
                    for c in halves:
                        rows = slice(c * HALF + rr, c * HALF + rr + STEP)
                        a, b = done[e, rows, lanes(m * N, 0)], done[e, rows, lanes(m * N, 1)]
                        rows = slice(m * HALF + rr, m * HALF + rr + STEP)
                        mid[e, 0, rows, lanes(0, c)] = (a + b).astype(bf16)
                        mid[e, 1, rows, lanes(0, c)] = (a - b).astype(bf16)
            for o in halves:
                spec[e, o] = jnp.dot(mid[e, o], tab[2 + o], preferred_element_type=f32)
            for o in halves:
                for rr in range(0, HALF, STEP):
                    rows = [slice(m * HALF + rr, m * HALF + rr + STEP) for m in halves]
                    values = [[spec[e, o, rows[m], lanes(0, c)] for c in halves] for m in halves]
                    intensity = (values[0][0] ** 2 + values[0][1] ** 2) + (
                        values[1][0] ** 2 + values[1][1] ** 2
                    )
                    measured = amp[p, e * HALF + rr : e * HALF + rr + STEP, lanes(0, o)]
                    factor = measured * lax.rsqrt(jnp.maximum(intensity, INTENSITY_FLOOR)) - 1.0
                    factor = jnp.where(used, factor, 0.0)
                    for m in halves:
                        for c in halves:
                            corr[e, o, rows[m], lanes(0, c)] = (values[m][c] * factor).astype(bf16)
            for o in halves:
                undone[e, o] = jnp.dot(corr[e, o], tab[o], preferred_element_type=f32)
            for rr in range(0, HALF, STEP):
                for m in halves:
                    for c in halves:
                        rows = slice(m * HALF + rr, m * HALF + rr + STEP)
                        a, b = undone[e, 0, rows, lanes(0, c)], undone[e, 1, rows, lanes(0, c)]
                        rows = slice(c * HALF + rr, c * HALF + rr + STEP)
                        back[e, rows, lanes(m * N, 0)] = (a + b).astype(bf16)
                        back[e, rows, lanes(m * N, 1)] = (a - b).astype(bf16)
        for e in halves:
            chi[e] = jnp.dot(tab[2 + e], back[e], preferred_element_type=f32)
        for rr in range(0, HALF, STEP):
            terms = [[None, None], [None, None]]
            for j in halves:
                waves = []
                for m in halves:
                    parts = [
                        [chi[e, c * HALF + rr : c * HALF + rr + STEP, lanes(m * N, j)] for e in halves]
                        for c in halves
                    ]
                    waves.append([(a + b, a - b) for a, b in parts])
                for e in halves:
                    at = e * HALF + rr
                    rows = slice(at, at + STEP)
                    o_re, o_im = patch[p, 0, j, rows, :], patch[p, 1, j, rows, :]
                    g_re = g_im = 0.0
                    for m in halves:
                        p_re, p_im = pr[2 * m, rows, lanes(0, j)], pr[2 * m + 1, rows, lanes(0, j)]
                        b_re, b_im = waves[m][0][e], waves[m][1][e]
                        g_re += p_re * b_re + p_im * b_im
                        g_im += p_re * b_im - p_im * b_re
                        h_re = o_re * b_re + o_im * b_im
                        h_im = o_re * b_im - o_im * b_re
                        b = at // 8
                        pair = (b // (nx * ny), b // ny % nx, slice(b % ny, b % ny + 2))
                        part[it][(*pair, 4 * m + j)] += h_re.reshape(2, 8, LANES)
                        part[it][(*pair, 4 * m + 2 + j)] += h_im.reshape(2, 8, LANES)
                    terms[e][j] = g_re, g_im
            for e in halves:
                put = slice(FAR + e * HALF + rr, FAR + e * HALF + rr + STEP)
                for ch in range(2):
                    a = pltpu.roll(terms[e][0][ch], ahead, 1)
                    b = pltpu.roll(terms[e][1][ch], ahead, 1)
                    placed[p, 0, ch, put, :] = jnp.where(late, a, 0.0)
                    placed[p, 1, ch, put, :] = jnp.where(late, b, a)
                    placed[p, 2, ch, put, :] = jnp.where(late, 0.0, b)

    def update(it, lo, hi):
        for rr in range(lo, hi, 2 * STEP):
            rows = slice(rr, rr + 2 * STEP)
            scale = w_own[it][LANES + rr : LANES + rr + 2 * STEP, :]
            for ch in range(2):
                grad = own[it][1, ch, rows, :] + (from_left[it][ch, rows, :] + from_right[it][ch, rows, :])
                value = field[it][1, ch, LANES + rr : LANES + rr + 2 * STEP, :] + grad * scale
                if it == 0:
                    field[1][1, ch, LANES + rr : LANES + rr + 2 * STEP, :] = value
                else:
                    own[1][1, ch, rows, :] = value
        if it == 1:
            return [write(own[1].at[1, :, lo:hi, :], out_sample.at[:, lo:hi, :])]
        return []

    def finish_probe():
        for i in range(N // 8):
            c, xy = i // (nx * ny), i % (nx * ny)
            for j in range(2):
                for q in range(4):
                    value = full[0][c, xy // ny, xy % ny, 2 * q + j]
                    prb[1][q, i * 8 : i * 8 + 8, j * LANES : (j + 1) * LANES] = value

    written = []

    def write(src, dst):
        copy = pltpu.make_async_copy(src, dst, load_sem.at[len(moves) + len(written)])
        copy.start()
        written.append(copy)
        return copy

    flushed = [0]

    def flush():
        for copy in copies[flushed[0] :]:
            copy.wait_send()
        flushed[0] = len(copies)

    for load in loads:
        load.wait()
    lax.fori_loop(0, SLOTS, order_amplitudes, 0)
    arrive(tell)
    facts_in = [
        pltpu.make_async_copy(src, known.at[t], load_sem.at[len(moves) + 6 + t])
        for t, src in enumerate((heard.at[0], told, heard.at[1]))
    ]
    for copy in facts_in:
        copy.start()
    for copy in facts_in:
        copy.wait()
    rows_w = illuminate(0)
    waiting = spread(field[0], sent_up, sent_down, sent_middle, forwards)
    arrive(waiting)

    half = nx * ny
    for it in range(2):
        if it == 0:
            gather(0)
        else:
            write(prb[1], out_probe)
            rows_w = illuminate(1)

        mine = vfull[it].at[(core * nx + x) * ny + y]
        v_core = remote(vpart[it].at[pl.ds((1 - core) * half, half)], vrc[it], partner)
        v_x = [remote(vhs[it].at[pl.ds(xs[k] * ny, ny)], vrx[it].at[k - 1], on_x[k]) for k in range(1, nx)]
        v_y = [remote(vhx[it].at[ys[k]], vry[it].at[k - 1], on_y[k]) for k in range(1, ny)]
        v_z = [remote(vz[it].at[z], vz[it].at[z], on_z[k]) for k in range(1, nz)]
        if it == 1:
            v_back_y = [remote(mine, mine, on_y[k]) for k in range(1, ny)]
            row = vfull[it].at[pl.ds((core * nx + x) * ny, ny)]
            v_back_x = [remote(row, row, on_x[k]) for k in range(1, nx)]
            whole = vfull[it].at[pl.ds(core * half, half)]
            v_back_core = remote(whole, whole, partner)
        v_core.start()

        def weight_core(it=it, v_core=v_core, v_x=v_x):
            v_core.wait_recv()
            vhs[it][...] = vpart[it][pl.ds(core * half, half)] + vrc[it][...]
            start(v_x)

        def weight_x(it=it, v_x=v_x, v_y=v_y):
            arrive(v_x)
            value = vhs[it][pl.ds(x * ny, ny)]
            for k in range(nx - 1):
                value += vrx[it][k]
            vhx[it][...] = value
            start(v_y)

        def weight_y(it=it, v_y=v_y, v_z=v_z):
            arrive(v_y)
            value = vhx[it][y]
            for k in range(ny - 1):
                value += vry[it][k]
            vz[it][z] = value
            start(v_z)

        def visit(p, _, it=it, hooks=(weight_core, weight_x, weight_y)):
            for n, hook in zip((1, 2, 3), hooks, strict=True):
                pl.when(p == n)(hook)
            position(it, p)
            return 0

        lax.fori_loop(0, SLOTS, visit, 0)

        sums, mates = part[it], rc[it]
        order = (2, 1, 3, 0)
        swap = [send(sums.at[1 - core, :, ys[k]], mates.at[:, ys[k]], partner) for k in order]
        planes = [slice(4 * h, 4 * h + 4) for h in range(2)]

        total(grads, halo_up[it], 0, 0, LANES)
        rows_up = send(halo_up[it], from_dn[it], above)
        total(grads, halo_dn[it], LANES + BAND, 0, LANES)
        rows_down = send(halo_dn[it], from_up[it], below)

        def sum_core(n, it=it, swap=swap):
            swap[n].wait_recv()
            at = ys[order[n]]
            hs[it][:, at] = part[it][core, :, at] + rc[it][:, at]

        def send_sides(lo, hi, it=it):
            return [
                send(own[it].at[0, :, lo:hi, :], from_right[it].at[:, lo:hi, :], left),
                send(own[it].at[2, :, lo:hi, :], from_left[it].at[:, lo:hi, :], right),
            ]

        total(grads, own[it], LANES, *MIDDLE)
        side_middle = send_sides(*MIDDLE)

        sum_core(0)
        far = [
            [
                send(hs[it].at[0:2, ys[2], p], r1[it].at[0, h], on_y[1]),
                send(hs[it].at[2:4, ys[2], p], r1[it].at[1, h], on_y[3]),
            ]
            for h, p in enumerate(planes)
        ]

        sum_core(1)
        sum_core(2)
        near = []
        for h, p in enumerate(planes):
            arrive(far[h])
            hs[it][0:2, ys[1], p] += r1[it][0, h]
            hs[it][2:4, ys[3], p] += r1[it][1, h]
            near.append(
                [
                    send(hs[it].at[:, ys[1], p], r2[it].at[0, h], on_y[1]),
                    send(hs[it].at[:, ys[3], p], r2[it].at[1, h], on_y[3]),
                ]
            )
        sum_core(3)

        total(grads, own[it], LANES, *UP)
        total(grads, own[it], LANES, *DOWN)

        def add_rows(src, lo, it=it):
            for t in range(3):
                for ch in range(2):
                    own[it][t, ch, lo : lo + LANES, :] += src[t, ch]

        rows_down.wait_recv()
        add_rows(from_up[it], UP[0])
        side_up = send_sides(*UP)
        rows_up.wait_recv()
        add_rows(from_dn[it], DOWN[0])
        side_down = send_sides(*DOWN)

        to_x = []
        for h, p in enumerate(planes):
            arrive(near[h])
            hy[it][h] = hs[it][:, y, p] + (r2[it][0, h] + r2[it][1, h])
            to_x.append([send(hy[it].at[h, xs[k]], rx[it].at[h, k - 1], on_x[k]) for k in range(1, nx)])

        arrive(v_z)
        value = vz[it][0]
        for k in range(1, nz):
            value += vz[it][k]
        vfull[it][(core * nx + x) * ny + y] = value
        if it == 1:
            start(v_back_y)

        arrive(rows_w)
        w_own[it][LANES : 2 * LANES, :] += w_from_up[it][...]
        w_own[it][BAND : LANES + BAND, :] += w_from_dn[it][...]
        w_own[it][LANES : LANES + BAND, :] = 1.0 / (w_own[it][LANES : LANES + BAND, :] + SAMPLE_DAMPING)

        for h, p in enumerate(planes):
            arrive(to_x[h])
            value = hy[it][h, x]
            for k in range(nx - 1):
                value += rx[it][h, k]
            zb[it][p] = value
        to_z = [send(zb[it].at[zs[k]], rz[it].at[k - 1], on_z[k]) for k in range(1, nz)]

        if it == 1:
            arrive(v_back_y)
            start(v_back_x)

        arrive(side_middle)
        update(it, *MIDDLE)

        arrive(to_z)
        value = zb[it][z]
        for k in range(nz - 1):
            value += rz[it][k]
        if it == 0:
            at = (core * nx + x) * ny + y
            rows = pl.ds(pl.multiple_of(at * 8, 8), 8)
            even = lax.broadcasted_iota(jnp.int32, (8, LANES), 0) * 0 + z % 2 == 0
            base = jnp.where(even, prb[0][z // 2, rows, 0:LANES], prb[0][z // 2, rows, LANES:N])
            value = base + value / (vfull[0][at, z % 2] + PROBE_DAMPING)
        zg[it][z] = value
        back_z = [send(zg[it].at[z], zg[it].at[z], on_z[k]) for k in range(1, nz)]

        arrive(side_up)
        update(it, *UP)
        if it == 0:

            def updated(lo, hi):
                return field[1].at[1, :, LANES + lo : LANES + hi, :]

            sent_up = send_columns(field[1], updated, *UP)
            forwards = [forward_up(field[1], 1)]

        arrive(back_z)
        result = full[it]
        result[core, x, y] = zg[it][...]
        mine = [result.at[core, x, y, p] for p in planes]
        back_x = [[send(m, m, on_x[k]) for k in range(1, nx)] for m in mine]
        if it == 1:
            arrive(v_back_x)
            v_back_core.start()
            flush()

        arrive(side_down)
        update(it, *DOWN)
        if it == 0:
            sent_down = send_columns(field[1], updated, *DOWN)
            forwards.append(forward_down(field[1], 1))
            sent_middle = send_columns(field[1], updated, *MIDDLE)

        def to_core(k, result=result):
            piece = result.at[core, :, ys[k]]
            return send(piece, piece, partner)

        back_near = []
        for h, p in enumerate(planes):
            arrive(back_x[h])
            mine = result.at[core, :, y, p]
            back_near.append([send(mine, mine, on_y[k]) for k in (1, 3)])
        back_core = [to_core(0)]
        back_far = []
        for h, p in enumerate(planes):
            arrive(back_near[h])
            low, high = result.at[core, 0:2, ys[3], p], result.at[core, 2:4, ys[1], p]
            back_far.append([send(low, low, on_y[1]), send(high, high, on_y[3])])
        back_core += [to_core(1), to_core(3)]
        if it == 0:
            waiting = spread(field[1], sent_up, sent_down, sent_middle, forwards)
        for h in range(2):
            arrive(back_far[h])
        back_core.append(to_core(2))
        if it == 0:
            arrive(waiting)
            gather(1)
            arrive(back_core)
            finish_probe()
        else:
            v_back_core.wait_recv()
            write(vfull[1], out_weight)
            flush()
            arrive(back_core)
            write(full[1], out_sums)

    for copy in written:
        copy.wait()


def finish(scale, sample, probe, sums, weight, new_sample, new_probe, probe_gradient):
    new_sample[...] = sample[...]
    for b in range(sums.shape[0]):
        rows = slice(8 * b, 8 * b + 8)
        for j in range(2):
            cols = slice(j * LANES, (j + 1) * LANES)
            damped = 1.0 / (weight[b, j] + PROBE_DAMPING)
            for q in range(4):
                grad = sums[b, 2 * q + j]
                new_probe[q // 2, q % 2, rows, cols] = probe[q, rows, cols] + grad * damped
                probe_gradient[q // 2, q % 2, rows, cols] = grad * scale


def solution(mesh):
    ng, nd = mesh.shape["grp"], mesh.shape["dev"]
    ny = ng // 2
    nz = nd // 4
    nx = nd // nz
    blocks = 2 * nx * ny
    table = tables()

    def vmem(*shape, dtype=jnp.float32):
        return pltpu.VMEM(shape, dtype)

    def two(*shape):
        return [vmem(*shape)] * 2

    def local(sample, probe, amps, rows_at, cols_at, live):
        hbm = pl.BlockSpec(memory_space=pl.ANY)
        smem = pl.BlockSpec(memory_space=pltpu.SMEM)
        f32 = jnp.float32
        raw_sample, raw_probe, sums, weight = pl.pallas_call(
            functools.partial(kernel, (nx, ny, nz)),
            out_shape=[
                jax.ShapeDtypeStruct((2, BAND, LANES), f32),
                jax.ShapeDtypeStruct((4, N, N), f32),
                jax.ShapeDtypeStruct((2, nx, ny, 8, 8, LANES), f32),
                jax.ShapeDtypeStruct((blocks, 2, 8, LANES), f32),
            ],
            in_specs=[hbm] * 4 + [smem] * 3,
            out_specs=[hbm] * 4,
            scratch_shapes=[
                *two(3, 2, EXT, LANES),
                *two(4, N, N),
                vmem(SLOTS, N, N),
                vmem(6, N, N, dtype=jnp.bfloat16),
                vmem(SLOTS, 2, 2, N, LANES),
                *[vmem(2, N, 2 * N, dtype=jnp.bfloat16)] * 2,
                *[vmem(2, 2, N, N, dtype=jnp.bfloat16)] * 2,
                vmem(2, N, 2 * N),
                *[vmem(2, 2, N, N)] * 2,
                vmem(2, N, 2 * N),
                vmem(2, N, LANES),
                vmem(SLOTS, 3, 2, 2 * FAR + N, LANES),
                *two(3, 2, LANES, LANES),
                *two(3, 2, LANES, LANES),
                *two(3, 2, BAND, LANES),
                *two(3, 2, LANES, LANES),
                *two(3, 2, LANES, LANES),
                *two(2, BAND, LANES),
                *two(2, BAND, LANES),
                vmem(8, LANES, dtype=jnp.int32),
                vmem(2, 8, LANES, dtype=jnp.int32),
                pltpu.SMEM((3, 8, LANES), jnp.int32),
                *two(EXT, LANES),
                *two(LANES, LANES),
                *two(LANES, LANES),
                *two(2, nx, ny, 8, 8, LANES),
                *two(nx, ny, 8, 8, LANES),
                *two(nx, ny, 8, 8, LANES),
                *two(2, 2, nx // 2, 4, 8, LANES),
                *two(2, 2, nx, 4, 8, LANES),
                *two(2, nx, 4, 8, LANES),
                *two(2, nx - 1, 4, 8, LANES),
                *two(8, 8, LANES),
                *two(nz - 1, 8, LANES),
                *two(8, 8, LANES),
                *two(2, nx, ny, 8, 8, LANES),
                *two(blocks, 2, 8, LANES),
                *two(blocks // 2, 2, 8, LANES),
                *two(blocks // 2, 2, 8, LANES),
                *two(nx - 1, ny, 2, 8, LANES),
                *two(ny, 2, 8, LANES),
                *two(ny - 1, 2, 8, LANES),
                *two(nz, 2, 8, LANES),
                *two(blocks, 2, 8, LANES),
                pltpu.SemaphoreType.DMA((13,)),
                pltpu.SemaphoreType.DMA((COPIES,)),
                pltpu.SemaphoreType.DMA((COPIES,)),
            ],
            compiler_params=pltpu.CompilerParams(
                collective_id=0, has_side_effects=True, vmem_limit_bytes=60 * 1024 * 1024
            ),
            cost_estimate=pl.CostEstimate(
                flops=2 * 4 * 4 * 2 * 512**3, bytes_accessed=6 << 20, transcendentals=8 * N * N
            ),
        )(sample, probe.reshape(4, N, N), amps, table, rows_at, cols_at, live)
        steps = 4
        some, rows = blocks // steps, N // steps
        tile = pl.BlockSpec((2, BAND // steps, LANES), lambda i: (0, i, 0))
        modes = pl.BlockSpec((2, 2, rows, N), lambda i: (0, 0, i, 0))
        return pl.pallas_call(
            functools.partial(finish, 1.0 / math.sqrt(SLOTS * ng * nd)),
            grid=(steps,),
            out_shape=[
                jax.ShapeDtypeStruct((2, BAND, LANES), f32),
                jax.ShapeDtypeStruct((2, 2, N, N), f32),
                jax.ShapeDtypeStruct((2, 2, N, N), f32),
            ],
            in_specs=[
                tile,
                pl.BlockSpec((4, rows, N), lambda i: (0, i, 0)),
                pl.BlockSpec((some, 8, 8, LANES), lambda i: (i, 0, 0, 0)),
                pl.BlockSpec((some, 2, 8, LANES), lambda i: (i, 0, 0, 0)),
            ],
            out_specs=[tile, modes, modes],
            compiler_params=pltpu.CompilerParams(vmem_limit_bytes=60 * 1024 * 1024),
            cost_estimate=pl.CostEstimate(flops=16 * N * N, bytes_accessed=6 << 20, transcendentals=0),
        )(raw_sample, raw_probe, sums.reshape(blocks, 8, 8, LANES), weight)

    return jax.shard_map(
        local,
        mesh=mesh,
        in_specs=(
            P(None, "grp", "dev"),
            P(),
            P(("grp", "dev"), None, None),
            P(("grp", "dev")),
            P(("grp", "dev")),
            P(("grp", "dev")),
        ),
        out_specs=(P(None, "grp", "dev"), P(), P()),
        check_vma=False,
    )
```

```python
import functools
import math

import jax
import jax.numpy as jnp
import ml_dtypes
import numpy as np
from jax import lax
from jax.experimental import pallas as pl
from jax.experimental.pallas import tpu as pltpu
from jax.sharding import PartitionSpec as P

INTENSITY_FLOOR = 0.25
SAMPLE_DAMPING = 0.5
PROBE_DAMPING = 1.0
MESH = pl.DeviceIdType.MESH
LANES = 128
N = 256
HALF = 128
BAND = 512
EXT = BAND + 2 * LANES
FAR = 512
STEP = 16
SLOTS = 4
COPIES = 192
UP, MIDDLE, DOWN = (0, 128), (128, 384), (384, 512)


def tables():
    k = np.arange(N)
    angles = (np.outer(k, k) % N).astype(np.float32) * np.float32(2.0 * math.pi / N)
    c = (np.cos(angles) / np.float32(16.0)).astype(ml_dtypes.bfloat16)
    s = (np.sin(angles) / np.float32(16.0)).astype(ml_dtypes.bfloat16)
    split = [np.block([[c[e::2, :HALF], s[e::2, :HALF]], [-s[e::2, :HALF], c[e::2, :HALF]]]) for e in range(2)]
    order = np.eye(N)[np.concatenate([k[0::2], k[1::2]])].astype(ml_dtypes.bfloat16)
    return np.stack([*split, split[0].T, split[1].T, order, order.T])


def kernel(shape, *refs):
    sample, probe, amps, table, rows_at, cols_at, live = refs[:7]
    out_sample, out_probe, out_sums, out_weight = refs[7:11]
    scratch = iter(refs[11:])

    def two():
        return next(scratch), next(scratch)

    nx, ny, nz = shape
    field, prb = two(), two()
    amp, tab, patch, wave, back, mid, corr, done, spec, undone, chi, light, placed = (
        next(scratch) for _ in range(13)
    )
    halo_up, halo_dn, own, from_up, from_dn, from_left, from_right = (two() for _ in range(7))
    told, heard, known = (next(scratch) for _ in range(3))
    w_own, w_from_up, w_from_dn = (two() for _ in range(3))
    part, rc, hs, r1, r2, hy, rx, zb, rz, zg, full = (two() for _ in range(11))
    vpart, vrc, vhs, vrx, vhx, vry, vz, vfull = (two() for _ in range(8))
    load_sem, send_sem, recv_sem = scratch

    g, d = lax.axis_index("grp"), lax.axis_index("dev")
    ng, nd = 2 * ny, nx * nz
    y, core = g // 2, g % 2
    x, z = d // nz, d % nz
    above = {"grp": (g + ng - 1) % ng, "dev": d}
    below = {"grp": (g + 1) % ng, "dev": d}
    left = {"grp": g, "dev": (d + nd - 1) % nd}
    right = {"grp": g, "dev": (d + 1) % nd}
    partner = {"grp": y * 2 + 1 - core, "dev": d}
    xs = [(x + k) % nx for k in range(nx)]
    ys = [(y + k) % ny for k in range(ny)]
    zs = [(z + k) % nz for k in range(nz)]
    on_x = [{"grp": g, "dev": v * nz + z} for v in xs]
    on_y = [{"grp": v * 2 + core, "dev": d} for v in ys]
    on_z = [{"grp": g, "dev": x * nz + v} for v in zs]

    copies = []

    def remote(src, dst, to):
        n = len(copies)
        copy = pltpu.make_async_remote_copy(
            src_ref=src, dst_ref=dst, send_sem=send_sem.at[n], recv_sem=recv_sem.at[n],
            device_id=to, device_id_type=MESH,
        )
        copies.append(copy)
        return copy

    def start(group):
        for copy in group:
            copy.start()
        return group

    def send(src, dst, to):
        return start([remote(src, dst, to)])[0]

    def arrive(group):
        for copy in group:
            copy.wait_recv()

    moves = [(sample, field[0].at[1, :, LANES : LANES + BAND, :]), (probe, prb[0]), (table, tab), (amps, amp)]
    loads = [pltpu.make_async_copy(src, dst, load_sem.at[n]) for n, (src, dst) in enumerate(moves)]
    for load in loads:
        load.start()

    barrier = pltpu.get_barrier_semaphore()
    peers = [above, below, left, right, partner] + on_x[1:] + on_y[1:] + on_z[1:]
    for peer in peers:
        pl.semaphore_signal(barrier, inc=1, device_id=peer, device_id_type=MESH)
    pl.semaphore_wait(barrier, len(peers))

    row_anchor = g * BAND - LANES
    col_anchor = d * LANES - LANES
    starts = [jnp.clip(rows_at[p] - row_anchor, 0, FAR) for p in range(SLOTS)]

    shifts = [jnp.clip(cols_at[p] - col_anchor, 0, LANES) for p in range(SLOTS)]

    def alive(p, count):
        return jnp.full((STEP, LANES), p, jnp.int32) < jnp.full((STEP, LANES), count, jnp.int32)

    place_in_row = lax.broadcasted_iota(jnp.int32, (8, LANES), 1)
    facts = jnp.zeros((8, LANES), jnp.int32)
    for n, fact in enumerate([*starts, *shifts, live[0]]):
        facts = jnp.where(place_in_row == n, fact, facts)
    told[...] = facts
    tell = [send(told, heard.at[0], right), send(told, heard.at[1], left)]

    def send_columns(f, source, lo, hi):
        src = source(lo, hi)
        return [
            send(src, f.at[0, :, LANES + lo : LANES + hi, :], right),
            send(src, f.at[2, :, LANES + lo : LANES + hi, :], left),
        ]

    def forward_up(f, t, src=None):
        src = f.at[t, :, LANES : 2 * LANES, :] if src is None else src
        return send(src, f.at[t, :, LANES + BAND : EXT, :], above)

    def forward_down(f, t, src=None):
        src = f.at[t, :, BAND : LANES + BAND, :] if src is None else src
        return send(src, f.at[t, :, 0:LANES, :], below)

    def spread(f, sent_up, sent_down, sent_middle, forwards):
        arrive(sent_up)
        forwards += [forward_up(f, 0), forward_up(f, 2)]
        arrive(sent_down)
        forwards += [forward_down(f, 0), forward_down(f, 2)]
        return sent_middle + forwards

    def argument(lo, hi):
        return sample.at[:, lo:hi, :]

    sent_up = send_columns(field[0], argument, *UP)
    sent_down = send_columns(field[0], argument, *DOWN)
    forwards = [forward_up(field[0], 1, argument(*UP)), forward_down(field[0], 1, argument(*DOWN))]
    sent_middle = send_columns(field[0], argument, *MIDDLE)

    def clear(i, _):
        zero = jnp.zeros((STEP, LANES), jnp.float32)
        rr = pl.multiple_of(i * STEP, STEP)
        for p in range(SLOTS):
            for t in range(3):
                for at in (rr, FAR + N + rr):
                    for ch in range(2):
                        placed[p, t, ch, pl.ds(at, STEP), :] = zero
        return 0

    lax.fori_loop(0, FAR // STEP, clear, 0)
    for it in range(2):
        part[it][...] = jnp.zeros(part[it].shape, jnp.float32)
        vpart[it][...] = jnp.zeros(vpart[it].shape, jnp.float32)

    def placing(p):
        s = jnp.clip(cols_at[p] - col_anchor, 0, LANES)
        lane = lax.broadcasted_iota(jnp.int32, (STEP, LANES), 1)
        return s % LANES, lane >= s

    def total(sources, dst, first, lo, hi):
        def body(i, _):
            rr = pl.multiple_of(lo + i * 2 * STEP, 2 * STEP)
            for src, index in sources:
                values = [
                    placed[(p, *src, pl.ds(FAR + first + rr - starts[p], 2 * STEP), slice(None))]
                    for p in range(SLOTS)
                ]
                dst[(*index, pl.ds(rr, 2 * STEP), slice(None))] = (values[0] + values[1]) + (
                    values[2] + values[3]
                )
            return 0

        lax.fori_loop(0, (hi - lo) // (2 * STEP), body, 0)

    grads = [((t, ch), (t, ch)) for t in range(3) for ch in range(2)]

    def illuminate(it):
        for j in range(2):
            cols = slice(j * LANES, (j + 1) * LANES)
            value = prb[it][0, :, cols] ** 2 + prb[it][1, :, cols] ** 2
            light[j] = value + (prb[it][2, :, cols] ** 2 + prb[it][3, :, cols] ** 2)

        zero = jnp.zeros((STEP, LANES), jnp.float32)
        lane = lax.broadcasted_iota(jnp.int32, (STEP, LANES), 1)

        def place(p, _):
            for t in range(3):
                shift = known[t, 0, SLOTS + p]
                late = lane >= shift
                used = alive(p, known[t, 0, 2 * SLOTS])
                for rr in range(0, N, STEP):
                    a, b = (
                        pltpu.roll(jnp.where(used, light[j, rr : rr + STEP, :], 0.0), shift % LANES, 1)
                        for j in range(2)
                    )
                    value = (jnp.where(late, zero, b), jnp.where(late, b, a), jnp.where(late, a, zero))[t]
                    placed[p, t, 0, FAR + rr : FAR + rr + STEP, :] = value
            return 0

        lax.fori_loop(0, SLOTS, place, 0)

        def body(i, _):
            rr = pl.multiple_of(i * 2 * STEP, 2 * STEP)
            values = [
                placed[p, t, 0, pl.ds(FAR + rr - known[t, 0, p], 2 * STEP), :]
                for t in range(3)
                for p in range(SLOTS)
            ]
            w_own[it][pl.ds(rr, 2 * STEP), :] = sum(values[1:], values[0])
            return 0

        lax.fori_loop(0, EXT // (2 * STEP), body, 0)
        return [
            send(w_own[it].at[0:LANES, :], w_from_dn[it], above),
            send(w_own[it].at[LANES + BAND : EXT, :], w_from_up[it], below),
        ]

    def gather(it):
        f = field[it]

        def body(p, _):
            r0 = jnp.clip(rows_at[p] - row_anchor, 0, FAR)
            s = jnp.clip(cols_at[p] - col_anchor, 0, LANES)
            behind = (LANES - s) % LANES
            early = lax.broadcasted_iota(jnp.int32, (STEP, LANES), 1) < LANES - s
            used = alive(p, live[0])
            for rr in range(0, N, STEP):
                rows = slice(rr, rr + STEP)
                halves = []
                for ch in range(2):
                    a, b, c = (pltpu.roll(f[t, ch, pl.ds(r0 + rr, STEP), :], behind, 1) for t in range(3))
                    halves.append((jnp.where(early, a, b), jnp.where(early, b, c)))
                for j in range(2):
                    o_re, o_im = halves[0][j], halves[1][j]
                    patch[p, 0, j, rows, :] = o_re
                    patch[p, 1, j, rows, :] = o_im
                    v = jnp.where(used, o_re * o_re + o_im * o_im, 0.0).reshape(2, 8, LANES)
                    vpart[it][rr // 8 : rr // 8 + 2, j] += v
            return 0

        lax.fori_loop(0, SLOTS, body, 0)

    def order_amplitudes(p, _):
        rest = amp[p]
        total_of = None
        for _ in range(3):
            bits = rest.astype(jnp.bfloat16)
            rest = rest - bits.astype(jnp.float32)
            rows = jnp.dot(tab[4], bits, preferred_element_type=jnp.float32).astype(jnp.bfloat16)
            moved = jnp.dot(rows, tab[5], preferred_element_type=jnp.float32)
            total_of = moved if total_of is None else total_of + moved
        amp[p] = total_of
        return 0

    def position(it, p):
        pr = prb[it]
        ahead, late = placing(p)
        used = alive(p, live[0])
        f32, bf16 = jnp.float32, jnp.bfloat16
        halves = range(2)

        def lanes(first, j):
            return slice(first + j * LANES, first + (j + 1) * LANES)

        for rr in range(0, HALF, STEP):
            for j in halves:
                for m in halves:
                    both = []
                    for e in halves:
                        rows = slice(e * HALF + rr, e * HALF + rr + STEP)
                        o_re, o_im = patch[p, 0, j, rows, :], patch[p, 1, j, rows, :]
                        p_re, p_im = pr[2 * m, rows, lanes(0, j)], pr[2 * m + 1, rows, lanes(0, j)]
                        both.append((p_re * o_re - p_im * o_im, p_re * o_im + p_im * o_re))
                    for c in halves:
                        rows = slice(c * HALF + rr, c * HALF + rr + STEP)
                        wave[0, rows, lanes(m * N, j)] = (both[0][c] + both[1][c]).astype(bf16)
                        wave[1, rows, lanes(m * N, j)] = (both[0][c] - both[1][c]).astype(bf16)
        for e in halves:
            done[e] = jnp.dot(tab[e], wave[e], preferred_element_type=f32)
        for e in halves:
            for rr in range(0, HALF, STEP):
                for m in halves:
                    for c in halves:
                        rows = slice(c * HALF + rr, c * HALF + rr + STEP)
                        a, b = done[e, rows, lanes(m * N, 0)], done[e, rows, lanes(m * N, 1)]
                        rows = slice(m * HALF + rr, m * HALF + rr + STEP)
                        mid[e, 0, rows, lanes(0, c)] = (a + b).astype(bf16)
                        mid[e, 1, rows, lanes(0, c)] = (a - b).astype(bf16)
            for o in halves:
                spec[e, o] = jnp.dot(mid[e, o], tab[2 + o], preferred_element_type=f32)
            for o in halves:
                for rr in range(0, HALF, STEP):
                    rows = [slice(m * HALF + rr, m * HALF + rr + STEP) for m in halves]
                    values = [[spec[e, o, rows[m], lanes(0, c)] for c in halves] for m in halves]
                    intensity = (values[0][0] ** 2 + values[0][1] ** 2) + (
                        values[1][0] ** 2 + values[1][1] ** 2
                    )
                    measured = amp[p, e * HALF + rr : e * HALF + rr + STEP, lanes(0, o)]
                    factor = measured * lax.rsqrt(jnp.maximum(intensity, INTENSITY_FLOOR)) - 1.0
                    factor = jnp.where(used, factor, 0.0)
                    for m in halves:
                        for c in halves:
                            corr[e, o, rows[m], lanes(0, c)] = (values[m][c] * factor).astype(bf16)
            for o in halves:
                undone[e, o] = jnp.dot(corr[e, o], tab[o], preferred_element_type=f32)
            for rr in range(0, HALF, STEP):
                for m in halves:
                    for c in halves:
                        rows = slice(m * HALF + rr, m * HALF + rr + STEP)
                        a, b = undone[e, 0, rows, lanes(0, c)], undone[e, 1, rows, lanes(0, c)]
                        rows = slice(c * HALF + rr, c * HALF + rr + STEP)
                        back[e, rows, lanes(m * N, 0)] = (a + b).astype(bf16)
                        back[e, rows, lanes(m * N, 1)] = (a - b).astype(bf16)
        for e in halves:
            chi[e] = jnp.dot(tab[2 + e], back[e], preferred_element_type=f32)
        for rr in range(0, HALF, STEP):
            terms = [[None, None], [None, None]]
            for j in halves:
                waves = []
                for m in halves:
                    parts = [
                        [chi[e, c * HALF + rr : c * HALF + rr + STEP, lanes(m * N, j)] for e in halves]
                        for c in halves
                    ]
                    waves.append([(a + b, a - b) for a, b in parts])
                for e in halves:
                    at = e * HALF + rr
                    rows = slice(at, at + STEP)
                    o_re, o_im = patch[p, 0, j, rows, :], patch[p, 1, j, rows, :]
                    g_re = g_im = 0.0
                    for m in halves:
                        p_re, p_im = pr[2 * m, rows, lanes(0, j)], pr[2 * m + 1, rows, lanes(0, j)]
                        b_re, b_im = waves[m][0][e], waves[m][1][e]
                        g_re += p_re * b_re + p_im * b_im
                        g_im += p_re * b_im - p_im * b_re
                        h_re = o_re * b_re + o_im * b_im
                        h_im = o_re * b_im - o_im * b_re
                        b = at // 8
                        pair = (b // (nx * ny), b // ny % nx, slice(b % ny, b % ny + 2))
                        part[it][(*pair, 4 * m + j)] += h_re.reshape(2, 8, LANES)
                        part[it][(*pair, 4 * m + 2 + j)] += h_im.reshape(2, 8, LANES)
                    terms[e][j] = g_re, g_im
            for e in halves:
                put = slice(FAR + e * HALF + rr, FAR + e * HALF + rr + STEP)
                for ch in range(2):
                    a = pltpu.roll(terms[e][0][ch], ahead, 1)
                    b = pltpu.roll(terms[e][1][ch], ahead, 1)
                    placed[p, 0, ch, put, :] = jnp.where(late, a, 0.0)
                    placed[p, 1, ch, put, :] = jnp.where(late, b, a)
                    placed[p, 2, ch, put, :] = jnp.where(late, 0.0, b)

    def update(it, lo, hi):
        for rr in range(lo, hi, 2 * STEP):
            rows = slice(rr, rr + 2 * STEP)
            scale = w_own[it][LANES + rr : LANES + rr + 2 * STEP, :]
            for ch in range(2):
                grad = own[it][1, ch, rows, :] + (from_left[it][ch, rows, :] + from_right[it][ch, rows, :])
                value = field[it][1, ch, LANES + rr : LANES + rr + 2 * STEP, :] + grad * scale
                if it == 0:
                    field[1][1, ch, LANES + rr : LANES + rr + 2 * STEP, :] = value
                else:
                    own[1][1, ch, rows, :] = value
        if it == 1:
            return [write(own[1].at[1, :, lo:hi, :], out_sample.at[:, lo:hi, :])]
        return []

    def finish_probe():
        for i in range(N // 8):
            c, xy = i // (nx * ny), i % (nx * ny)
            for j in range(2):
                for q in range(4):
                    value = full[0][c, xy // ny, xy % ny, 2 * q + j]
                    prb[1][q, i * 8 : i * 8 + 8, j * LANES : (j + 1) * LANES] = value

    written = []

    def write(src, dst):
        copy = pltpu.make_async_copy(src, dst, load_sem.at[len(moves) + len(written)])
        copy.start()
        written.append(copy)
        return copy

    flushed = [0]

    def flush():
        for copy in copies[flushed[0] :]:
            copy.wait_send()
        flushed[0] = len(copies)

    for load in loads:
        load.wait()
    arrive(tell)
    facts_in = [
        pltpu.make_async_copy(src, known.at[t], load_sem.at[len(moves) + 6 + t])
        for t, src in enumerate((heard.at[0], told, heard.at[1]))
    ]
    for copy in facts_in:
        copy.start()
    for copy in facts_in:
        copy.wait()
    rows_w = illuminate(0)
    arrive(sent_up)
    forwards += [forward_up(field[0], 0), forward_up(field[0], 2)]
    lax.fori_loop(0, SLOTS // 2, order_amplitudes, 0)
    arrive(sent_down)
    forwards += [forward_down(field[0], 0), forward_down(field[0], 2)]
    lax.fori_loop(SLOTS // 2, SLOTS, order_amplitudes, 0)
    arrive(sent_middle + forwards)

    half = nx * ny
    for it in range(2):
        if it == 0:
            gather(0)
        else:
            write(prb[1], out_probe)
            rows_w = illuminate(1)

        mine = vfull[it].at[(core * nx + x) * ny + y]
        v_core = remote(vpart[it].at[pl.ds((1 - core) * half, half)], vrc[it], partner)
        v_x = [remote(vhs[it].at[pl.ds(xs[k] * ny, ny)], vrx[it].at[k - 1], on_x[k]) for k in range(1, nx)]
        v_y = [remote(vhx[it].at[ys[k]], vry[it].at[k - 1], on_y[k]) for k in range(1, ny)]
        v_z = [remote(vz[it].at[z], vz[it].at[z], on_z[k]) for k in range(1, nz)]
        if it == 1:
            v_back_y = [remote(mine, mine, on_y[k]) for k in range(1, ny)]
            row = vfull[it].at[pl.ds((core * nx + x) * ny, ny)]
            v_back_x = [remote(row, row, on_x[k]) for k in range(1, nx)]
            whole = vfull[it].at[pl.ds(core * half, half)]
            v_back_core = remote(whole, whole, partner)
        v_core.start()

        def weight_core(it=it, v_core=v_core, v_x=v_x):
            v_core.wait_recv()
            vhs[it][...] = vpart[it][pl.ds(core * half, half)] + vrc[it][...]
            start(v_x)

        def weight_x(it=it, v_x=v_x, v_y=v_y):
            arrive(v_x)
            value = vhs[it][pl.ds(x * ny, ny)]
            for k in range(nx - 1):
                value += vrx[it][k]
            vhx[it][...] = value
            start(v_y)

        def weight_y(it=it, v_y=v_y, v_z=v_z):
            arrive(v_y)
            value = vhx[it][y]
            for k in range(ny - 1):
                value += vry[it][k]
            vz[it][z] = value
            start(v_z)

        def visit(p, _, it=it, hooks=(weight_core, weight_x, weight_y)):
            for n, hook in zip((1, 2, 3), hooks, strict=True):
                pl.when(p == n)(hook)
            position(it, p)
            return 0

        lax.fori_loop(0, SLOTS, visit, 0)

        sums, mates = part[it], rc[it]
        order = (2, 1, 3, 0)
        swap = [send(sums.at[1 - core, :, ys[k]], mates.at[:, ys[k]], partner) for k in order]
        planes = [slice(4 * h, 4 * h + 4) for h in range(2)]

        total(grads, halo_up[it], 0, 0, LANES)
        rows_up = send(halo_up[it], from_dn[it], above)
        total(grads, halo_dn[it], LANES + BAND, 0, LANES)
        rows_down = send(halo_dn[it], from_up[it], below)

        def sum_core(n, it=it, swap=swap):
            swap[n].wait_recv()
            at = ys[order[n]]
            hs[it][:, at] = part[it][core, :, at] + rc[it][:, at]

        def send_sides(lo, hi, it=it):
            return [
                send(own[it].at[0, :, lo:hi, :], from_right[it].at[:, lo:hi, :], left),
                send(own[it].at[2, :, lo:hi, :], from_left[it].at[:, lo:hi, :], right),
            ]

        total(grads, own[it], LANES, *MIDDLE)
        side_middle = send_sides(*MIDDLE)

        sum_core(0)
        far = [
            [
                send(hs[it].at[0:2, ys[2], p], r1[it].at[0, h], on_y[1]),
                send(hs[it].at[2:4, ys[2], p], r1[it].at[1, h], on_y[3]),
            ]
            for h, p in enumerate(planes)
        ]

        sum_core(1)
        sum_core(2)
        near = []
        for h, p in enumerate(planes):
            arrive(far[h])
            hs[it][0:2, ys[1], p] += r1[it][0, h]
            hs[it][2:4, ys[3], p] += r1[it][1, h]
            near.append(
                [
                    send(hs[it].at[:, ys[1], p], r2[it].at[0, h], on_y[1]),
                    send(hs[it].at[:, ys[3], p], r2[it].at[1, h], on_y[3]),
                ]
            )
        sum_core(3)

        def add_rows(src, lo, it=it):
            for t in range(3):
                for ch in range(2):
                    own[it][t, ch, lo : lo + LANES, :] += src[t, ch]

        def edges(it=it, rows_down=rows_down, rows_up=rows_up, send_sides=send_sides, add_rows=add_rows):
            total(grads, own[it], LANES, *UP)
            total(grads, own[it], LANES, *DOWN)
            rows_down.wait_recv()
            add_rows(from_up[it], UP[0])
            upper = send_sides(*UP)
            rows_up.wait_recv()
            add_rows(from_dn[it], DOWN[0])
            return upper, send_sides(*DOWN)

        if it == 0:
            side_up, side_down = edges()
        to_x = []
        for h, p in enumerate(planes):
            arrive(near[h])
            hy[it][h] = hs[it][:, y, p] + (r2[it][0, h] + r2[it][1, h])
            to_x.append([send(hy[it].at[h, xs[k]], rx[it].at[h, k - 1], on_x[k]) for k in range(1, nx)])

        if it == 1:
            side_up, side_down = edges()

        arrive(v_z)
        value = vz[it][0]
        for k in range(1, nz):
            value += vz[it][k]
        vfull[it][(core * nx + x) * ny + y] = value
        if it == 1:
            start(v_back_y)

        arrive(rows_w)
        w_own[it][LANES : 2 * LANES, :] += w_from_up[it][...]
        w_own[it][BAND : LANES + BAND, :] += w_from_dn[it][...]
        w_own[it][LANES : LANES + BAND, :] = 1.0 / (w_own[it][LANES : LANES + BAND, :] + SAMPLE_DAMPING)

        for h, p in enumerate(planes):
            arrive(to_x[h])
            value = hy[it][h, x]
            for k in range(nx - 1):
                value += rx[it][h, k]
            zb[it][p] = value
        to_z = [send(zb[it].at[zs[k]], rz[it].at[k - 1], on_z[k]) for k in range(1, nz)]

        if it == 1:
            arrive(v_back_y)
            start(v_back_x)

        if it == 0:
            arrive(side_middle)
            update(it, *MIDDLE)

        arrive(to_z)
        value = zb[it][z]
        for k in range(nz - 1):
            value += rz[it][k]
        if it == 0:
            at = (core * nx + x) * ny + y
            rows = pl.ds(pl.multiple_of(at * 8, 8), 8)
            even = lax.broadcasted_iota(jnp.int32, (8, LANES), 0) * 0 + z % 2 == 0
            base = jnp.where(even, prb[0][z // 2, rows, 0:LANES], prb[0][z // 2, rows, LANES:N])
            value = base + value / (vfull[0][at, z % 2] + PROBE_DAMPING)
        zg[it][z] = value
        back_z = [send(zg[it].at[z], zg[it].at[z], on_z[k]) for k in range(1, nz)]

        if it == 0:
            arrive(side_up)
            update(it, *UP)

            def updated(lo, hi):
                return field[1].at[1, :, LANES + lo : LANES + hi, :]

            sent_up = send_columns(field[1], updated, *UP)
            forwards = [forward_up(field[1], 1)]

        arrive(back_z)
        result = full[it]
        result[core, x, y] = zg[it][...]
        mine = [result.at[core, x, y, p] for p in planes]
        back_x = [[send(m, m, on_x[k]) for k in range(1, nx)] for m in mine]
        if it == 1:
            arrive(v_back_x)
            v_back_core.start()
            flush()

        if it == 0:
            arrive(side_down)
            update(it, *DOWN)
            sent_down = send_columns(field[1], updated, *DOWN)
            forwards.append(forward_down(field[1], 1))
            sent_middle = send_columns(field[1], updated, *MIDDLE)

        def to_core(k, result=result):
            piece = result.at[core, :, ys[k]]
            return send(piece, piece, partner)

        back_near = []
        for h, p in enumerate(planes):
            arrive(back_x[h])
            mine = result.at[core, :, y, p]
            back_near.append([send(mine, mine, on_y[k]) for k in (1, 3)])
        back_core = [to_core(0)]
        back_far = []
        for h, p in enumerate(planes):
            arrive(back_near[h])
            low, high = result.at[core, 0:2, ys[3], p], result.at[core, 2:4, ys[1], p]
            back_far.append([send(low, low, on_y[1]), send(high, high, on_y[3])])
        back_core += [to_core(1), to_core(3)]
        if it == 0:
            waiting = spread(field[1], sent_up, sent_down, sent_middle, forwards)
        for h in range(2):
            arrive(back_far[h])
        back_core.append(to_core(2))
        if it == 0:
            arrive(waiting)
            gather(1)
            arrive(back_core)
            finish_probe()
        else:
            for side, rows in ((side_middle, MIDDLE), (side_up, UP), (side_down, DOWN)):
                arrive(side)
                update(it, *rows)
            v_back_core.wait_recv()
            write(vfull[1], out_weight)
            flush()
            arrive(back_core)
            write(full[1], out_sums)

    for copy in written:
        copy.wait()


def finish(scale, sample, probe, sums, weight, new_sample, new_probe, probe_gradient):
    new_sample[...] = sample[...]
    for b in range(sums.shape[0]):
        rows = slice(8 * b, 8 * b + 8)
        for j in range(2):
            cols = slice(j * LANES, (j + 1) * LANES)
            damped = 1.0 / (weight[b, j] + PROBE_DAMPING)
            for q in range(4):
                grad = sums[b, 2 * q + j]
                new_probe[q // 2, q % 2, rows, cols] = probe[q, rows, cols] + grad * damped
                probe_gradient[q // 2, q % 2, rows, cols] = grad * scale


def solution(mesh):
    ng, nd = mesh.shape["grp"], mesh.shape["dev"]
    ny = ng // 2
    nz = nd // 4
    nx = nd // nz
    blocks = 2 * nx * ny
    table = tables()

    def vmem(*shape, dtype=jnp.float32):
        return pltpu.VMEM(shape, dtype)

    def two(*shape):
        return [vmem(*shape)] * 2

    def local(sample, probe, amps, rows_at, cols_at, live):
        hbm = pl.BlockSpec(memory_space=pl.ANY)
        smem = pl.BlockSpec(memory_space=pltpu.SMEM)
        f32 = jnp.float32
        raw_sample, raw_probe, sums, weight = pl.pallas_call(
            functools.partial(kernel, (nx, ny, nz)),
            out_shape=[
                jax.ShapeDtypeStruct((2, BAND, LANES), f32),
                jax.ShapeDtypeStruct((4, N, N), f32),
                jax.ShapeDtypeStruct((2, nx, ny, 8, 8, LANES), f32),
                jax.ShapeDtypeStruct((blocks, 2, 8, LANES), f32),
            ],
            in_specs=[hbm] * 4 + [smem] * 3,
            out_specs=[hbm] * 4,
            scratch_shapes=[
                *two(3, 2, EXT, LANES),
                *two(4, N, N),
                vmem(SLOTS, N, N),
                vmem(6, N, N, dtype=jnp.bfloat16),
                vmem(SLOTS, 2, 2, N, LANES),
                *[vmem(2, N, 2 * N, dtype=jnp.bfloat16)] * 2,
                *[vmem(2, 2, N, N, dtype=jnp.bfloat16)] * 2,
                vmem(2, N, 2 * N),
                *[vmem(2, 2, N, N)] * 2,
                vmem(2, N, 2 * N),
                vmem(2, N, LANES),
                vmem(SLOTS, 3, 2, 2 * FAR + N, LANES),
                *two(3, 2, LANES, LANES),
                *two(3, 2, LANES, LANES),
                *two(3, 2, BAND, LANES),
                *two(3, 2, LANES, LANES),
                *two(3, 2, LANES, LANES),
                *two(2, BAND, LANES),
                *two(2, BAND, LANES),
                vmem(8, LANES, dtype=jnp.int32),
                vmem(2, 8, LANES, dtype=jnp.int32),
                pltpu.SMEM((3, 8, LANES), jnp.int32),
                *two(EXT, LANES),
                *two(LANES, LANES),
                *two(LANES, LANES),
                *two(2, nx, ny, 8, 8, LANES),
                *two(nx, ny, 8, 8, LANES),
                *two(nx, ny, 8, 8, LANES),
                *two(2, 2, nx // 2, 4, 8, LANES),
                *two(2, 2, nx, 4, 8, LANES),
                *two(2, nx, 4, 8, LANES),
                *two(2, nx - 1, 4, 8, LANES),
                *two(8, 8, LANES),
                *two(nz - 1, 8, LANES),
                *two(8, 8, LANES),
                *two(2, nx, ny, 8, 8, LANES),
                *two(blocks, 2, 8, LANES),
                *two(blocks // 2, 2, 8, LANES),
                *two(blocks // 2, 2, 8, LANES),
                *two(nx - 1, ny, 2, 8, LANES),
                *two(ny, 2, 8, LANES),
                *two(ny - 1, 2, 8, LANES),
                *two(nz, 2, 8, LANES),
                *two(blocks, 2, 8, LANES),
                pltpu.SemaphoreType.DMA((13,)),
                pltpu.SemaphoreType.DMA((COPIES,)),
                pltpu.SemaphoreType.DMA((COPIES,)),
            ],
            compiler_params=pltpu.CompilerParams(
                collective_id=0, has_side_effects=True, vmem_limit_bytes=60 * 1024 * 1024
            ),
            cost_estimate=pl.CostEstimate(
                flops=2 * 4 * 4 * 2 * 512**3, bytes_accessed=6 << 20, transcendentals=8 * N * N
            ),
        )(sample, probe.reshape(4, N, N), amps, table, rows_at, cols_at, live)
        steps = 4
        some, rows = blocks // steps, N // steps
        tile = pl.BlockSpec((2, BAND // steps, LANES), lambda i: (0, i, 0))
        modes = pl.BlockSpec((2, 2, rows, N), lambda i: (0, 0, i, 0))
        return pl.pallas_call(
            functools.partial(finish, 1.0 / math.sqrt(SLOTS * ng * nd)),
            grid=(steps,),
            out_shape=[
                jax.ShapeDtypeStruct((2, BAND, LANES), f32),
                jax.ShapeDtypeStruct((2, 2, N, N), f32),
                jax.ShapeDtypeStruct((2, 2, N, N), f32),
            ],
            in_specs=[
                tile,
                pl.BlockSpec((4, rows, N), lambda i: (0, i, 0)),
                pl.BlockSpec((some, 8, 8, LANES), lambda i: (i, 0, 0, 0)),
                pl.BlockSpec((some, 2, 8, LANES), lambda i: (i, 0, 0, 0)),
            ],
            out_specs=[tile, modes, modes],
            compiler_params=pltpu.CompilerParams(vmem_limit_bytes=60 * 1024 * 1024),
            cost_estimate=pl.CostEstimate(flops=16 * N * N, bytes_accessed=6 << 20, transcendentals=0),
        )(raw_sample, raw_probe, sums.reshape(blocks, 8, 8, LANES), weight)

    return jax.shard_map(
        local,
        mesh=mesh,
        in_specs=(
            P(None, "grp", "dev"),
            P(),
            P(("grp", "dev"), None, None),
            P(("grp", "dev")),
            P(("grp", "dev")),
            P(("grp", "dev")),
        ),
        out_specs=(P(None, "grp", "dev"), P(), P()),
        check_vma=False,
    )
```

```python
import functools
import math

import jax
import jax.numpy as jnp
import ml_dtypes
import numpy as np
from jax import lax
from jax.experimental import pallas as pl
from jax.experimental.pallas import tpu as pltpu
from jax.sharding import PartitionSpec as P

INTENSITY_FLOOR = 0.25
SAMPLE_DAMPING = 0.5
PROBE_DAMPING = 1.0
MESH = pl.DeviceIdType.MESH
LANES = 128
N = 256
HALF = 128
BAND = 512
EXT = BAND + 2 * LANES
FAR = 512
STEP = 16
SLOTS = 4
COPIES = 192
UP, MIDDLE, DOWN = (0, 128), (128, 384), (384, 512)


def tables():
    k = np.arange(N)
    angles = (np.outer(k, k) % N).astype(np.float32) * np.float32(2.0 * math.pi / N)
    c = (np.cos(angles) / np.float32(16.0)).astype(ml_dtypes.bfloat16)
    s = (np.sin(angles) / np.float32(16.0)).astype(ml_dtypes.bfloat16)
    split = [np.block([[c[e::2, :HALF], s[e::2, :HALF]], [-s[e::2, :HALF], c[e::2, :HALF]]]) for e in range(2)]
    order = np.eye(N)[np.concatenate([k[0::2], k[1::2]])].astype(ml_dtypes.bfloat16)
    return np.stack([*split, split[0].T, split[1].T, order, order.T])


def kernel(shape, *refs):
    sample, probe, amps, table, rows_at, cols_at, live = refs[:7]
    out_sample, out_probe, out_sums, out_weight = refs[7:11]
    scratch = iter(refs[11:])

    def two():
        return next(scratch), next(scratch)

    nx, ny, nz = shape
    field, prb = two(), two()
    amp, tab, patch, wave, back, mid, corr, done, spec, undone, chi, light, placed = (
        next(scratch) for _ in range(13)
    )
    halo_up, halo_dn, own, from_up, from_dn, from_left, from_right = (two() for _ in range(7))
    told, heard, known = (next(scratch) for _ in range(3))
    w_own, w_from_up, w_from_dn = (two() for _ in range(3))
    part, rc, hs, r1, r2, hy, rx, zb, rz, zg, full = (two() for _ in range(11))
    vpart, vrc, vhs, vrx, vhx, vry, vz, vfull = (two() for _ in range(8))
    load_sem, send_sem, recv_sem = scratch

    g, d = lax.axis_index("grp"), lax.axis_index("dev")
    ng, nd = 2 * ny, nx * nz
    y, core = g // 2, g % 2
    x, z = d // nz, d % nz
    above = {"grp": (g + ng - 1) % ng, "dev": d}
    below = {"grp": (g + 1) % ng, "dev": d}
    left = {"grp": g, "dev": (d + nd - 1) % nd}
    right = {"grp": g, "dev": (d + 1) % nd}
    partner = {"grp": y * 2 + 1 - core, "dev": d}
    xs = [(x + k) % nx for k in range(nx)]
    ys = [(y + k) % ny for k in range(ny)]
    zs = [(z + k) % nz for k in range(nz)]
    on_x = [{"grp": g, "dev": v * nz + z} for v in xs]
    on_y = [{"grp": v * 2 + core, "dev": d} for v in ys]
    on_z = [{"grp": g, "dev": x * nz + v} for v in zs]

    copies = []

    def remote(src, dst, to):
        n = len(copies)
        copy = pltpu.make_async_remote_copy(
            src_ref=src, dst_ref=dst, send_sem=send_sem.at[n], recv_sem=recv_sem.at[n],
            device_id=to, device_id_type=MESH,
        )
        copies.append(copy)
        return copy

    def start(group):
        for copy in group:
            copy.start()
        return group

    def send(src, dst, to):
        return start([remote(src, dst, to)])[0]

    def arrive(group):
        for copy in group:
            copy.wait_recv()

    moves = [(sample, field[0].at[1, :, LANES : LANES + BAND, :]), (probe, prb[0]), (table, tab), (amps, amp)]
    loads = [pltpu.make_async_copy(src, dst, load_sem.at[n]) for n, (src, dst) in enumerate(moves)]
    for load in loads:
        load.start()

    barrier = pltpu.get_barrier_semaphore()
    peers = [above, below, left, right, partner] + on_x[1:] + on_y[1:] + on_z[1:]
    for peer in peers:
        pl.semaphore_signal(barrier, inc=1, device_id=peer, device_id_type=MESH)
    pl.semaphore_wait(barrier, len(peers))

    row_anchor = g * BAND - LANES
    col_anchor = d * LANES - LANES
    starts = [jnp.clip(rows_at[p] - row_anchor, 0, FAR) for p in range(SLOTS)]

    shifts = [jnp.clip(cols_at[p] - col_anchor, 0, LANES) for p in range(SLOTS)]

    def alive(p, count):
        return jnp.full((STEP, LANES), p, jnp.int32) < jnp.full((STEP, LANES), count, jnp.int32)

    place_in_row = lax.broadcasted_iota(jnp.int32, (8, LANES), 1)
    facts = jnp.zeros((8, LANES), jnp.int32)
    for n, fact in enumerate([*starts, *shifts, live[0]]):
        facts = jnp.where(place_in_row == n, fact, facts)
    told[...] = facts
    tell = [send(told, heard.at[0], right), send(told, heard.at[1], left)]

    def send_columns(f, source, lo, hi):
        src = source(lo, hi)
        return [
            send(src, f.at[0, :, LANES + lo : LANES + hi, :], right),
            send(src, f.at[2, :, LANES + lo : LANES + hi, :], left),
        ]

    def forward_up(f, t, src=None):
        src = f.at[t, :, LANES : 2 * LANES, :] if src is None else src
        return send(src, f.at[t, :, LANES + BAND : EXT, :], above)

    def forward_down(f, t, src=None):
        src = f.at[t, :, BAND : LANES + BAND, :] if src is None else src
        return send(src, f.at[t, :, 0:LANES, :], below)

    def spread(f, sent_up, sent_down, sent_middle, forwards):
        arrive(sent_up)
        forwards += [forward_up(f, 0), forward_up(f, 2)]
        arrive(sent_down)
        forwards += [forward_down(f, 0), forward_down(f, 2)]
        return sent_middle + forwards

    def argument(lo, hi):
        return sample.at[:, lo:hi, :]

    sent_up = send_columns(field[0], argument, *UP)
    sent_down = send_columns(field[0], argument, *DOWN)
    forwards = [forward_up(field[0], 1, argument(*UP)), forward_down(field[0], 1, argument(*DOWN))]
    sent_middle = send_columns(field[0], argument, *MIDDLE)

    def clear(i, _):
        zero = jnp.zeros((STEP, LANES), jnp.float32)
        rr = pl.multiple_of(i * STEP, STEP)
        for p in range(SLOTS):
            for t in range(3):
                for at in (rr, FAR + N + rr):
                    for ch in range(2):
                        placed[p, t, ch, pl.ds(at, STEP), :] = zero
        return 0

    lax.fori_loop(0, FAR // STEP, clear, 0)
    for it in range(2):
        part[it][...] = jnp.zeros(part[it].shape, jnp.float32)
        vpart[it][...] = jnp.zeros(vpart[it].shape, jnp.float32)

    def placing(p):
        s = jnp.clip(cols_at[p] - col_anchor, 0, LANES)
        lane = lax.broadcasted_iota(jnp.int32, (STEP, LANES), 1)
        return s % LANES, lane >= s

    def total(sources, dst, first, lo, hi):
        def body(i, _):
            rr = pl.multiple_of(lo + i * 2 * STEP, 2 * STEP)
            for src, index in sources:
                values = [
                    placed[(p, *src, pl.ds(FAR + first + rr - starts[p], 2 * STEP), slice(None))]
                    for p in range(SLOTS)
                ]
                dst[(*index, pl.ds(rr, 2 * STEP), slice(None))] = (values[0] + values[1]) + (
                    values[2] + values[3]
                )
            return 0

        lax.fori_loop(0, (hi - lo) // (2 * STEP), body, 0)

    grads = [((t, ch), (t, ch)) for t in range(3) for ch in range(2)]

    def illuminate(it):
        for j in range(2):
            cols = slice(j * LANES, (j + 1) * LANES)
            value = prb[it][0, :, cols] ** 2 + prb[it][1, :, cols] ** 2
            light[j] = value + (prb[it][2, :, cols] ** 2 + prb[it][3, :, cols] ** 2)

        zero = jnp.zeros((STEP, LANES), jnp.float32)
        lane = lax.broadcasted_iota(jnp.int32, (STEP, LANES), 1)

        def place(p, _):
            for t in range(3):
                shift = known[t, 0, SLOTS + p]
                late = lane >= shift
                used = alive(p, known[t, 0, 2 * SLOTS])
                for rr in range(0, N, STEP):
                    a, b = (
                        pltpu.roll(jnp.where(used, light[j, rr : rr + STEP, :], 0.0), shift % LANES, 1)
                        for j in range(2)
                    )
                    value = (jnp.where(late, zero, b), jnp.where(late, b, a), jnp.where(late, a, zero))[t]
                    placed[p, t, 0, FAR + rr : FAR + rr + STEP, :] = value
            return 0

        lax.fori_loop(0, SLOTS, place, 0)

        def body(i, _):
            rr = pl.multiple_of(i * 2 * STEP, 2 * STEP)
            values = [
                placed[p, t, 0, pl.ds(FAR + rr - known[t, 0, p], 2 * STEP), :]
                for t in range(3)
                for p in range(SLOTS)
            ]
            w_own[it][pl.ds(rr, 2 * STEP), :] = sum(values[1:], values[0])
            return 0

        lax.fori_loop(0, EXT // (2 * STEP), body, 0)
        return [
            send(w_own[it].at[0:LANES, :], w_from_dn[it], above),
            send(w_own[it].at[LANES + BAND : EXT, :], w_from_up[it], below),
        ]

    def gather(it):
        f = field[it]

        def body(p, _):
            r0 = jnp.clip(rows_at[p] - row_anchor, 0, FAR)
            s = jnp.clip(cols_at[p] - col_anchor, 0, LANES)
            behind = (LANES - s) % LANES
            early = lax.broadcasted_iota(jnp.int32, (STEP, LANES), 1) < LANES - s
            used = alive(p, live[0])
            for rr in range(0, N, STEP):
                rows = slice(rr, rr + STEP)
                halves = []
                for ch in range(2):
                    a, b, c = (pltpu.roll(f[t, ch, pl.ds(r0 + rr, STEP), :], behind, 1) for t in range(3))
                    halves.append((jnp.where(early, a, b), jnp.where(early, b, c)))
                for j in range(2):
                    o_re, o_im = halves[0][j], halves[1][j]
                    patch[p, 0, j, rows, :] = o_re
                    patch[p, 1, j, rows, :] = o_im
                    v = jnp.where(used, o_re * o_re + o_im * o_im, 0.0).reshape(2, 8, LANES)
                    vpart[it][rr // 8 : rr // 8 + 2, j] += v
            return 0

        lax.fori_loop(0, SLOTS, body, 0)

    def order_amplitudes(p, _):
        rest = amp[p]
        total_of = None
        for _ in range(3):
            bits = rest.astype(jnp.bfloat16)
            rest = rest - bits.astype(jnp.float32)
            rows = jnp.dot(tab[4], bits, preferred_element_type=jnp.float32).astype(jnp.bfloat16)
            moved = jnp.dot(rows, tab[5], preferred_element_type=jnp.float32)
            total_of = moved if total_of is None else total_of + moved
        amp[p] = total_of
        return 0

    def position(it, p):
        pr = prb[it]
        ahead, late = placing(p)
        used = alive(p, live[0])
        f32, bf16 = jnp.float32, jnp.bfloat16
        halves = range(2)

        def lanes(first, j):
            return slice(first + j * LANES, first + (j + 1) * LANES)

        for rr in range(0, HALF, STEP):
            for j in halves:
                for m in halves:
                    both = []
                    for e in halves:
                        rows = slice(e * HALF + rr, e * HALF + rr + STEP)
                        o_re, o_im = patch[p, 0, j, rows, :], patch[p, 1, j, rows, :]
                        p_re, p_im = pr[2 * m, rows, lanes(0, j)], pr[2 * m + 1, rows, lanes(0, j)]
                        both.append((p_re * o_re - p_im * o_im, p_re * o_im + p_im * o_re))
                    for c in halves:
                        rows = slice(c * HALF + rr, c * HALF + rr + STEP)
                        wave[0, rows, lanes(m * N, j)] = (both[0][c] + both[1][c]).astype(bf16)
                        wave[1, rows, lanes(m * N, j)] = (both[0][c] - both[1][c]).astype(bf16)
        for e in halves:
            done[e] = jnp.dot(tab[e], wave[e], preferred_element_type=f32)
        for e in halves:
            for rr in range(0, HALF, STEP):
                for m in halves:
                    for c in halves:
                        rows = slice(c * HALF + rr, c * HALF + rr + STEP)
                        a, b = done[e, rows, lanes(m * N, 0)], done[e, rows, lanes(m * N, 1)]
                        rows = slice(m * HALF + rr, m * HALF + rr + STEP)
                        mid[e, 0, rows, lanes(0, c)] = (a + b).astype(bf16)
                        mid[e, 1, rows, lanes(0, c)] = (a - b).astype(bf16)
            for o in halves:
                spec[e, o] = jnp.dot(mid[e, o], tab[2 + o], preferred_element_type=f32)
            for o in halves:
                for rr in range(0, HALF, STEP):
                    rows = [slice(m * HALF + rr, m * HALF + rr + STEP) for m in halves]
                    values = [[spec[e, o, rows[m], lanes(0, c)] for c in halves] for m in halves]
                    intensity = (values[0][0] ** 2 + values[0][1] ** 2) + (
                        values[1][0] ** 2 + values[1][1] ** 2
                    )
                    measured = amp[p, e * HALF + rr : e * HALF + rr + STEP, lanes(0, o)]
                    factor = measured * lax.rsqrt(jnp.maximum(intensity, INTENSITY_FLOOR)) - 1.0
                    factor = jnp.where(used, factor, 0.0)
                    for m in halves:
                        for c in halves:
                            corr[e, o, rows[m], lanes(0, c)] = (values[m][c] * factor).astype(bf16)
            for o in halves:
                undone[e, o] = jnp.dot(corr[e, o], tab[o], preferred_element_type=f32)
            for rr in range(0, HALF, STEP):
                for m in halves:
                    for c in halves:
                        rows = slice(m * HALF + rr, m * HALF + rr + STEP)
                        a, b = undone[e, 0, rows, lanes(0, c)], undone[e, 1, rows, lanes(0, c)]
                        rows = slice(c * HALF + rr, c * HALF + rr + STEP)
                        back[e, rows, lanes(m * N, 0)] = (a + b).astype(bf16)
                        back[e, rows, lanes(m * N, 1)] = (a - b).astype(bf16)
        for e in halves:
            chi[e] = jnp.dot(tab[2 + e], back[e], preferred_element_type=f32)
        for rr in range(0, HALF, STEP):
            terms = [[None, None], [None, None]]
            for j in halves:
                waves = []
                for m in halves:
                    parts = [
                        [chi[e, c * HALF + rr : c * HALF + rr + STEP, lanes(m * N, j)] for e in halves]
                        for c in halves
                    ]
                    waves.append([(a + b, a - b) for a, b in parts])
                for e in halves:
                    at = e * HALF + rr
                    rows = slice(at, at + STEP)
                    o_re, o_im = patch[p, 0, j, rows, :], patch[p, 1, j, rows, :]
                    g_re = g_im = 0.0
                    for m in halves:
                        p_re, p_im = pr[2 * m, rows, lanes(0, j)], pr[2 * m + 1, rows, lanes(0, j)]
                        b_re, b_im = waves[m][0][e], waves[m][1][e]
                        g_re += p_re * b_re + p_im * b_im
                        g_im += p_re * b_im - p_im * b_re
                        h_re = o_re * b_re + o_im * b_im
                        h_im = o_re * b_im - o_im * b_re
                        b = at // 8
                        pair = (b // (nx * ny), b // ny % nx, slice(b % ny, b % ny + 2))
                        part[it][(*pair, 4 * m + j)] += h_re.reshape(2, 8, LANES)
                        part[it][(*pair, 4 * m + 2 + j)] += h_im.reshape(2, 8, LANES)
                    terms[e][j] = g_re, g_im
            for e in halves:
                put = slice(FAR + e * HALF + rr, FAR + e * HALF + rr + STEP)
                for ch in range(2):
                    a = pltpu.roll(terms[e][0][ch], ahead, 1)
                    b = pltpu.roll(terms[e][1][ch], ahead, 1)
                    placed[p, 0, ch, put, :] = jnp.where(late, a, 0.0)
                    placed[p, 1, ch, put, :] = jnp.where(late, b, a)
                    placed[p, 2, ch, put, :] = jnp.where(late, 0.0, b)

    def update(it, lo, hi):
        for rr in range(lo, hi, 2 * STEP):
            rows = slice(rr, rr + 2 * STEP)
            scale = w_own[it][LANES + rr : LANES + rr + 2 * STEP, :]
            for ch in range(2):
                grad = own[it][1, ch, rows, :] + (from_left[it][ch, rows, :] + from_right[it][ch, rows, :])
                value = field[it][1, ch, LANES + rr : LANES + rr + 2 * STEP, :] + grad * scale
                if it == 0:
                    field[1][1, ch, LANES + rr : LANES + rr + 2 * STEP, :] = value
                else:
                    own[1][1, ch, rows, :] = value
        if it == 1:
            return [write(own[1].at[1, :, lo:hi, :], out_sample.at[:, lo:hi, :])]
        return []

    def finish_probe():
        for i in range(N // 8):
            c, xy = i // (nx * ny), i % (nx * ny)
            for j in range(2):
                for q in range(4):
                    value = full[0][c, xy // ny, xy % ny, 2 * q + j]
                    prb[1][q, i * 8 : i * 8 + 8, j * LANES : (j + 1) * LANES] = value

    written = []

    def write(src, dst):
        copy = pltpu.make_async_copy(src, dst, load_sem.at[len(moves) + len(written)])
        copy.start()
        written.append(copy)
        return copy

    flushed = [0]

    def flush():
        for copy in copies[flushed[0] :]:
            copy.wait_send()
        flushed[0] = len(copies)

    for load in loads:
        load.wait()
    lax.fori_loop(0, SLOTS, order_amplitudes, 0)
    arrive(tell)
    facts_in = [
        pltpu.make_async_copy(src, known.at[t], load_sem.at[len(moves) + 6 + t])
        for t, src in enumerate((heard.at[0], told, heard.at[1]))
    ]
    for copy in facts_in:
        copy.start()
    for copy in facts_in:
        copy.wait()
    rows_w = illuminate(0)
    waiting = spread(field[0], sent_up, sent_down, sent_middle, forwards)
    arrive(waiting)

    half = nx * ny
    for it in range(2):
        if it == 0:
            gather(0)
        else:
            write(prb[1], out_probe)
            rows_w = illuminate(1)

        mine = vfull[it].at[(core * nx + x) * ny + y]
        v_core = remote(vpart[it].at[pl.ds((1 - core) * half, half)], vrc[it], partner)
        v_x = [remote(vhs[it].at[pl.ds(xs[k] * ny, ny)], vrx[it].at[k - 1], on_x[k]) for k in range(1, nx)]
        v_y = [remote(vhx[it].at[ys[k]], vry[it].at[k - 1], on_y[k]) for k in range(1, ny)]
        v_z = [remote(vz[it].at[z], vz[it].at[z], on_z[k]) for k in range(1, nz)]
        if it == 1:
            v_back_y = [remote(mine, mine, on_y[k]) for k in range(1, ny)]
            row = vfull[it].at[pl.ds((core * nx + x) * ny, ny)]
            v_back_x = [remote(row, row, on_x[k]) for k in range(1, nx)]
            whole = vfull[it].at[pl.ds(core * half, half)]
            v_back_core = remote(whole, whole, partner)
        v_core.start()

        def weight_core(it=it, v_core=v_core, v_x=v_x):
            v_core.wait_recv()
            vhs[it][...] = vpart[it][pl.ds(core * half, half)] + vrc[it][...]
            start(v_x)

        def weight_x(it=it, v_x=v_x, v_y=v_y):
            arrive(v_x)
            value = vhs[it][pl.ds(x * ny, ny)]
            for k in range(nx - 1):
                value += vrx[it][k]
            vhx[it][...] = value
            start(v_y)

        def weight_y(it=it, v_y=v_y, v_z=v_z):
            arrive(v_y)
            value = vhx[it][y]
            for k in range(ny - 1):
                value += vry[it][k]
            vz[it][z] = value
            start(v_z)

        def visit(p, _, it=it, hooks=(weight_core, weight_x, weight_y)):
            for n, hook in zip((1, 2, 3), hooks, strict=True):
                pl.when(p == n)(hook)
            position(it, p)
            return 0

        lax.fori_loop(0, SLOTS, visit, 0)

        sums, mates = part[it], rc[it]
        order = (2, 1, 3, 0)
        planes = [slice(4 * h, 4 * h + 4) for h in range(2)]

        total(grads, halo_up[it], 0, 0, LANES)
        rows_up = send(halo_up[it], from_dn[it], above)
        total(grads, halo_dn[it], LANES + BAND, 0, LANES)
        rows_down = send(halo_dn[it], from_up[it], below)

        def send_sides(lo, hi, it=it):
            return [
                send(own[it].at[0, :, lo:hi, :], from_right[it].at[:, lo:hi, :], left),
                send(own[it].at[2, :, lo:hi, :], from_left[it].at[:, lo:hi, :], right),
            ]

        total(grads, own[it], LANES, *MIDDLE)
        side_middle = send_sides(*MIDDLE)
        swap = [send(sums.at[1 - core, :, ys[k]], mates.at[:, ys[k]], partner) for k in order]
        total(grads, own[it], LANES, *UP)
        total(grads, own[it], LANES, *DOWN)

        def sum_core(n, it=it, swap=swap):
            swap[n].wait_recv()
            at = ys[order[n]]
            hs[it][:, at] = part[it][core, :, at] + rc[it][:, at]

        sum_core(0)
        far = [
            [
                send(hs[it].at[0:2, ys[2], p], r1[it].at[0, h], on_y[1]),
                send(hs[it].at[2:4, ys[2], p], r1[it].at[1, h], on_y[3]),
            ]
            for h, p in enumerate(planes)
        ]

        sum_core(1)
        sum_core(2)
        def add_rows(src, lo, it=it):
            for t in range(3):
                for ch in range(2):
                    own[it][t, ch, lo : lo + LANES, :] += src[t, ch]

        rows_down.wait_recv()
        add_rows(from_up[it], UP[0])
        side_up = send_sides(*UP)
        rows_up.wait_recv()
        add_rows(from_dn[it], DOWN[0])
        side_down = send_sides(*DOWN)

        near = []
        for h, p in enumerate(planes):
            arrive(far[h])
            hs[it][0:2, ys[1], p] += r1[it][0, h]
            hs[it][2:4, ys[3], p] += r1[it][1, h]
            near.append(
                [
                    send(hs[it].at[:, ys[1], p], r2[it].at[0, h], on_y[1]),
                    send(hs[it].at[:, ys[3], p], r2[it].at[1, h], on_y[3]),
                ]
            )
        sum_core(3)

        to_x = []
        for h, p in enumerate(planes):
            arrive(near[h])
            hy[it][h] = hs[it][:, y, p] + (r2[it][0, h] + r2[it][1, h])
            to_x.append([send(hy[it].at[h, xs[k]], rx[it].at[h, k - 1], on_x[k]) for k in range(1, nx)])

        arrive(v_z)
        value = vz[it][0]
        for k in range(1, nz):
            value += vz[it][k]
        vfull[it][(core * nx + x) * ny + y] = value
        if it == 1:
            start(v_back_y)

        arrive(rows_w)
        w_own[it][LANES : 2 * LANES, :] += w_from_up[it][...]
        w_own[it][BAND : LANES + BAND, :] += w_from_dn[it][...]
        w_own[it][LANES : LANES + BAND, :] = 1.0 / (w_own[it][LANES : LANES + BAND, :] + SAMPLE_DAMPING)

        for h, p in enumerate(planes):
            arrive(to_x[h])
            value = hy[it][h, x]
            for k in range(nx - 1):
                value += rx[it][h, k]
            zb[it][p] = value
        to_z = [send(zb[it].at[zs[k]], rz[it].at[k - 1], on_z[k]) for k in range(1, nz)]

        if it == 1:
            arrive(v_back_y)
            start(v_back_x)

        arrive(side_middle)
        update(it, *MIDDLE)

        arrive(to_z)
        value = zb[it][z]
        for k in range(nz - 1):
            value += rz[it][k]
        if it == 0:
            at = (core * nx + x) * ny + y
            rows = pl.ds(pl.multiple_of(at * 8, 8), 8)
            even = lax.broadcasted_iota(jnp.int32, (8, LANES), 0) * 0 + z % 2 == 0
            base = jnp.where(even, prb[0][z // 2, rows, 0:LANES], prb[0][z // 2, rows, LANES:N])
            value = base + value / (vfull[0][at, z % 2] + PROBE_DAMPING)
        zg[it][z] = value
        back_z = [send(zg[it].at[z], zg[it].at[z], on_z[k]) for k in range(1, nz)]

        arrive(side_up)
        update(it, *UP)
        if it == 0:

            def updated(lo, hi):
                return field[1].at[1, :, LANES + lo : LANES + hi, :]

            sent_up = send_columns(field[1], updated, *UP)
            forwards = [forward_up(field[1], 1)]

        arrive(back_z)
        result = full[it]
        result[core, x, y] = zg[it][...]
        mine = [result.at[core, x, y, p] for p in planes]
        back_x = [[send(m, m, on_x[k]) for k in range(1, nx)] for m in mine]
        if it == 1:
            arrive(v_back_x)
            v_back_core.start()
            flush()

        arrive(side_down)
        update(it, *DOWN)
        if it == 0:
            sent_down = send_columns(field[1], updated, *DOWN)
            forwards.append(forward_down(field[1], 1))
            sent_middle = send_columns(field[1], updated, *MIDDLE)

        def to_core(k, result=result):
            piece = result.at[core, :, ys[k]]
            return send(piece, piece, partner)

        back_near = []
        for h, p in enumerate(planes):
            arrive(back_x[h])
            mine = result.at[core, :, y, p]
            back_near.append([send(mine, mine, on_y[k]) for k in (1, 3)])
        back_core = [to_core(0)]
        back_far = []
        for h, p in enumerate(planes):
            arrive(back_near[h])
            low, high = result.at[core, 0:2, ys[3], p], result.at[core, 2:4, ys[1], p]
            back_far.append([send(low, low, on_y[1]), send(high, high, on_y[3])])
        back_core += [to_core(1), to_core(3)]
        if it == 0:
            waiting = spread(field[1], sent_up, sent_down, sent_middle, forwards)
        for h in range(2):
            arrive(back_far[h])
        back_core.append(to_core(2))
        if it == 0:
            arrive(waiting)
            gather(1)
            arrive(back_core)
            finish_probe()
        else:
            v_back_core.wait_recv()
            write(vfull[1], out_weight)
            flush()
            arrive(back_core)
            write(full[1], out_sums)

    for copy in written:
        copy.wait()


def finish(scale, sample, probe, sums, weight, new_sample, new_probe, probe_gradient):
    new_sample[...] = sample[...]
    for b in range(sums.shape[0]):
        rows = slice(8 * b, 8 * b + 8)
        for j in range(2):
            cols = slice(j * LANES, (j + 1) * LANES)
            damped = 1.0 / (weight[b, j] + PROBE_DAMPING)
            for q in range(4):
                grad = sums[b, 2 * q + j]
                new_probe[q // 2, q % 2, rows, cols] = probe[q, rows, cols] + grad * damped
                probe_gradient[q // 2, q % 2, rows, cols] = grad * scale


def solution(mesh):
    ng, nd = mesh.shape["grp"], mesh.shape["dev"]
    ny = ng // 2
    nz = nd // 4
    nx = nd // nz
    blocks = 2 * nx * ny
    table = tables()

    def vmem(*shape, dtype=jnp.float32):
        return pltpu.VMEM(shape, dtype)

    def two(*shape):
        return [vmem(*shape)] * 2

    def local(sample, probe, amps, rows_at, cols_at, live):
        hbm = pl.BlockSpec(memory_space=pl.ANY)
        smem = pl.BlockSpec(memory_space=pltpu.SMEM)
        f32 = jnp.float32
        raw_sample, raw_probe, sums, weight = pl.pallas_call(
            functools.partial(kernel, (nx, ny, nz)),
            out_shape=[
                jax.ShapeDtypeStruct((2, BAND, LANES), f32),
                jax.ShapeDtypeStruct((4, N, N), f32),
                jax.ShapeDtypeStruct((2, nx, ny, 8, 8, LANES), f32),
                jax.ShapeDtypeStruct((blocks, 2, 8, LANES), f32),
            ],
            in_specs=[hbm] * 4 + [smem] * 3,
            out_specs=[hbm] * 4,
            scratch_shapes=[
                *two(3, 2, EXT, LANES),
                *two(4, N, N),
                vmem(SLOTS, N, N),
                vmem(6, N, N, dtype=jnp.bfloat16),
                vmem(SLOTS, 2, 2, N, LANES),
                *[vmem(2, N, 2 * N, dtype=jnp.bfloat16)] * 2,
                *[vmem(2, 2, N, N, dtype=jnp.bfloat16)] * 2,
                vmem(2, N, 2 * N),
                *[vmem(2, 2, N, N)] * 2,
                vmem(2, N, 2 * N),
                vmem(2, N, LANES),
                vmem(SLOTS, 3, 2, 2 * FAR + N, LANES),
                *two(3, 2, LANES, LANES),
                *two(3, 2, LANES, LANES),
                *two(3, 2, BAND, LANES),
                *two(3, 2, LANES, LANES),
                *two(3, 2, LANES, LANES),
                *two(2, BAND, LANES),
                *two(2, BAND, LANES),
                vmem(8, LANES, dtype=jnp.int32),
                vmem(2, 8, LANES, dtype=jnp.int32),
                pltpu.SMEM((3, 8, LANES), jnp.int32),
                *two(EXT, LANES),
                *two(LANES, LANES),
                *two(LANES, LANES),
                *two(2, nx, ny, 8, 8, LANES),
                *two(nx, ny, 8, 8, LANES),
                *two(nx, ny, 8, 8, LANES),
                *two(2, 2, nx // 2, 4, 8, LANES),
                *two(2, 2, nx, 4, 8, LANES),
                *two(2, nx, 4, 8, LANES),
                *two(2, nx - 1, 4, 8, LANES),
                *two(8, 8, LANES),
                *two(nz - 1, 8, LANES),
                *two(8, 8, LANES),
                *two(2, nx, ny, 8, 8, LANES),
                *two(blocks, 2, 8, LANES),
                *two(blocks // 2, 2, 8, LANES),
                *two(blocks // 2, 2, 8, LANES),
                *two(nx - 1, ny, 2, 8, LANES),
                *two(ny, 2, 8, LANES),
                *two(ny - 1, 2, 8, LANES),
                *two(nz, 2, 8, LANES),
                *two(blocks, 2, 8, LANES),
                pltpu.SemaphoreType.DMA((13,)),
                pltpu.SemaphoreType.DMA((COPIES,)),
                pltpu.SemaphoreType.DMA((COPIES,)),
            ],
            compiler_params=pltpu.CompilerParams(
                collective_id=0, has_side_effects=True, vmem_limit_bytes=60 * 1024 * 1024
            ),
            cost_estimate=pl.CostEstimate(
                flops=2 * 4 * 4 * 2 * 512**3, bytes_accessed=6 << 20, transcendentals=8 * N * N
            ),
        )(sample, probe.reshape(4, N, N), amps, table, rows_at, cols_at, live)
        steps = 4
        some, rows = blocks // steps, N // steps
        tile = pl.BlockSpec((2, BAND // steps, LANES), lambda i: (0, i, 0))
        modes = pl.BlockSpec((2, 2, rows, N), lambda i: (0, 0, i, 0))
        return pl.pallas_call(
            functools.partial(finish, 1.0 / math.sqrt(SLOTS * ng * nd)),
            grid=(steps,),
            out_shape=[
                jax.ShapeDtypeStruct((2, BAND, LANES), f32),
                jax.ShapeDtypeStruct((2, 2, N, N), f32),
                jax.ShapeDtypeStruct((2, 2, N, N), f32),
            ],
            in_specs=[
                tile,
                pl.BlockSpec((4, rows, N), lambda i: (0, i, 0)),
                pl.BlockSpec((some, 8, 8, LANES), lambda i: (i, 0, 0, 0)),
                pl.BlockSpec((some, 2, 8, LANES), lambda i: (i, 0, 0, 0)),
            ],
            out_specs=[tile, modes, modes],
            compiler_params=pltpu.CompilerParams(vmem_limit_bytes=60 * 1024 * 1024),
            cost_estimate=pl.CostEstimate(flops=16 * N * N, bytes_accessed=6 << 20, transcendentals=0),
        )(raw_sample, raw_probe, sums.reshape(blocks, 8, 8, LANES), weight)

    return jax.shard_map(
        local,
        mesh=mesh,
        in_specs=(
            P(None, "grp", "dev"),
            P(),
            P(("grp", "dev"), None, None),
            P(("grp", "dev")),
            P(("grp", "dev")),
            P(("grp", "dev")),
        ),
        out_specs=(P(None, "grp", "dev"), P(), P()),
        check_vma=False,
    )
```
